32 devices in a mesh: dp: 2 (over x), seq: 16 (over z, y, core).
Axes of the slice: x: 2, y: 2, z: 4, core: 2. Of those that a mesh axis runs over, the one named last changes fastest.
Arguments:
- states: bfloat16 [4, 1024, 1152], P('dp', 'seq'), may hold values from -6 to 6
- counts: int32 [4, 4], P('dp'), may hold values from 0 to 1024, as said below
- cotangent: bfloat16 [4, 1024, 1152], P('dp', 'seq'), may hold values from -6 to 6
- w_qkv: bfloat16 [3, 1152, 1152], replicated, may hold values from -0.1875 to 0.1875
- w_out: bfloat16 [1152, 1152], replicated, may hold values from -1.5 to 1.5
- attn_bias: float32 [3, 1152], replicated, may hold values from -3 to 3
- norm_gain: float32 [2, 1152], replicated, may hold values from 0.25 to 1.75
- norm_bias: float32 [2, 1152], replicated, may hold values from -2 to 2
- w_up: bfloat16 [1152, 4304], replicated, may hold values from -0.1875 to 0.1875
- up_bias: float32 [4304], replicated, may hold values from -3 to 3
- w_down: bfloat16 [4304, 1152], replicated, may hold values from -0.09375 to 0.09375
- down_bias: float32 [1152], replicated, may hold values from -3 to 3
Outputs:
- layer_out: bfloat16 [4, 1024, 1152], P('dp', 'seq')
- state_grad: bfloat16 [4, 1024, 1152], P('dp', 'seq')
- grad_qkv: float32 [3, 1152, 1152], P(None, 'seq', 'dp')
- grad_out: float32 [1152, 1152], P('seq', 'dp')
- grad_attn_bias: float32 [3, 1152], P(None, 'seq')
- grad_gain: float32 [2, 1152], P(None, 'seq')
- grad_shift: float32 [2, 1152], P(None, 'seq')
- grad_up: float32 [1152, 4304], P('seq', 'dp')
- grad_up_bias: float32 [4304], P('seq')
- grad_down: float32 [4304, 1152], P('seq', 'dp')
- grad_down_bias: float32 [1152], P('seq')
The draws below stay inside these ranges and needn't reach their ends.
Inputs may be any that keep to these rules, and one draw needn't show every extreme that they name: A group's 4 slots give patch counts packed from position 0 in slot order: used slots come first and hold 256 or more patches each, unused slots hold 0; their sum is at most 1024 and the rest of the group is padding. In some group a single image fills all 1024 positions.
All inputs are finite; a program needn't handle non-finite values.
Results may differ from the reference program's by a relative error of at most 0.02.
Values may be sent and summed in bfloat16 or wider, within the bound.
A program may use at most 256 MiB of HBM per device.

```python
import math
import jax
import jax.numpy as jnp
from jax import lax

D = 1152
HEADS = 16
FF = 4304
TOK_DEV = 64
IMAGES = 4
MIN_IMG = 256
HEAD_DIM = 72
SEQ_LEN = 1024
GROUPS = 4


def draw_counts(key, part):
    key = jax.random.fold_in(key, 7)
    key_pick, key_groups = jax.random.split(key)
    chosen = jax.random.randint(key_pick, (), 0, GROUPS)
    keys = jax.random.split(key_groups, GROUPS)
    indices = jnp.arange(GROUPS, dtype=jnp.int32)
    slots = jnp.arange(IMAGES, dtype=jnp.int32)

    def one_group(group_key, index):
        key_used, key_sizes = jax.random.split(group_key)
        used = jax.random.randint(key_used, (), 1, IMAGES + 1)
        span = (SEQ_LEN - used * MIN_IMG) // used
        extra = jax.random.randint(key_sizes, (IMAGES,), 0, span + 1)
        sizes = jnp.where(slots < used, MIN_IMG + extra, 0)
        whole = jnp.where(slots == 0, SEQ_LEN, 0)
        return jnp.where(index == chosen, whole, sizes).astype(jnp.int32)
    return jax.vmap(one_group)(keys, indices)


def block_scale(rng, dims, pieces, smallest, largest):
    level, own = 1.0, jax.random.fold_in(rng, 6)
    for position, shards_of in pieces:
        steps = jnp.exp(jax.random.uniform(jax.random.fold_in(own, position), (shards_of,), jnp.float32, smallest / len(pieces), largest / len(pieces)))
        level = level * jnp.repeat(steps, dims[position] // shards_of).reshape([-1 if axis == position else 1 for axis in range(len(dims))])
    return level


def normal_values(own_key, shape, deviation, bound, cuts=(), held_as=jnp.bfloat16):
    entries = jax.random.normal(own_key, shape, jnp.float32) * deviation
    if len(cuts) > 0:
        entries = block_scale(own_key, shape, cuts, -0.22, 0.18) * entries
    return jnp.clip(entries, min=-bound, max=bound).astype(held_as)


def setup_inputs(seed: int = 0) -> dict:
    arg_keys = jax.random.split(jax.random.key(seed), 13)
    return {
        "states": normal_values(arg_keys[0], (GROUPS, SEQ_LEN, D), 1.0, 6.0, ((0, 2), (1, 16))),
        "counts": draw_counts(jax.random.fold_in(arg_keys[12], 71), 0),
        "cotangent": normal_values(arg_keys[2], (GROUPS, SEQ_LEN, D), 1.0, 6.0, ((0, 2), (1, 16))),
        "w_qkv": normal_values(arg_keys[3], (3, D, D), D ** -0.5, 0.1875),
        "w_out": normal_values(arg_keys[4], (D, D), (max(D * 16 // SEQ_LEN, 1)) ** -0.5, 1.5),
        "attn_bias": normal_values(arg_keys[5], (3, D), 0.5, 3.0, (), jnp.float32),
        "norm_gain": jnp.clip(1.0 + 0.15 * jax.random.normal(arg_keys[6], (2, D), jnp.float32), 0.25, 1.75),
        "norm_bias": normal_values(arg_keys[7], (2, D), 0.3, 2.0, (), jnp.float32),
        "w_up": normal_values(arg_keys[8], (D, FF), D ** -0.5, 0.1875),
        "up_bias": normal_values(arg_keys[9], (FF,), 0.5, 3.0, (), jnp.float32),
        "w_down": normal_values(arg_keys[10], (FF, D), FF ** -0.5, 0.09375),
        "down_bias": normal_values(arg_keys[11], (D,), 0.5, 3.0, (), jnp.float32),
    }


@jax.custom_vjp
def low(v):
    return lax.optimization_barrier(v.astype(jnp.bfloat16)).astype(jnp.float32)

@jax.custom_vjp
def low_back(v):
    return v

def low_keep(v):
    return (low(v), None)

def low_pass(kept, grad):
    return (grad,)

def back_keep(v):
    return (v, None)

def back_low(kept, grad):
    return (low(grad),)
low.defvjp(low_keep, low_pass)
low_back.defvjp(back_keep, back_low)
EPS = 1e-06
NEG = -1e+30

def matmul(left, right):
    return jnp.matmul(left, right, precision=lax.Precision.HIGHEST)

def layer_norm(values, gain, shift):
    mean = lax.optimization_barrier(jnp.mean(values, axis=-1, keepdims=True))
    centred = values - mean
    spread = lax.optimization_barrier(jnp.mean(centred * centred, axis=-1, keepdims=True))
    return centred * lax.rsqrt(spread + EPS) * gain + shift

def image_ids(counts, length):
    ends = jnp.cumsum(counts)
    positions = jnp.arange(length, dtype=jnp.int32)
    return lax.optimization_barrier(jnp.sum((positions[:, None] >= ends[None, :]).astype(jnp.int32), axis=1))

def attend(query, keys, values, ids):
    length = query.shape[0]
    key_heads = keys.reshape(length, HEADS, HEAD_DIM)
    value_heads = values.reshape(length, HEADS, HEAD_DIM)
    blocks = length // TOK_DEV
    query_blocks = query.reshape(blocks, TOK_DEV, HEADS, HEAD_DIM)
    id_blocks = ids.reshape(blocks, TOK_DEV)

    def block(args):
        query_block, id_block = args
        scores = jnp.einsum('qhd,khd->hqk', query_block, key_heads, precision=lax.Precision.HIGHEST)
        scores = low_back(scores)
        same = id_block[None, :, None] == ids[None, None, :]
        masked = jnp.where(same, scores, NEG)
        highest = lax.optimization_barrier(jnp.max(masked, axis=-1, keepdims=True))
        weights = jnp.where(same, jnp.exp(masked - highest), 0.0)
        probs = weights / lax.optimization_barrier(jnp.sum(weights, axis=-1, keepdims=True))
        mixed = jnp.einsum('hqk,khd->qhd', low(probs), value_heads, precision=lax.Precision.HIGHEST)
        return mixed.reshape(TOK_DEV, HEADS * HEAD_DIM)
    return lax.map(jax.checkpoint(block), (query_blocks, id_blocks)).reshape(length, HEADS * HEAD_DIM)

def reference(states, counts, cotangent, w_qkv, w_out, attn_bias, norm_gain, norm_bias, w_up, up_bias, w_down, down_bias):
    factor = 1.0 / math.sqrt(HEAD_DIM)
    floats = (states.astype(jnp.float32), w_qkv.astype(jnp.float32), w_out.astype(jnp.float32), attn_bias, norm_gain, norm_bias, w_up.astype(jnp.float32), up_bias, w_down.astype(jnp.float32), down_bias)

    def forward(inputs, qkv_w, out_w, a_bias, n_gain, n_bias, up_w, u_bias, down_w, d_bias):

        def one_group(args):
            values_in, group_counts = args
            ids = image_ids(group_counts, SEQ_LEN)
            hidden_one = low(layer_norm(values_in, n_gain[0], n_bias[0]))
            query = low(low_back(matmul(hidden_one, qkv_w[0]) + a_bias[0]) * factor)
            keys = low(low_back(matmul(hidden_one, qkv_w[1])))
            values = low(low_back(matmul(hidden_one, qkv_w[2]) + a_bias[1]))
            attended = low(low_back(attend(query, keys, values, ids)))
            middle = values_in + low_back(matmul(attended, out_w)) + a_bias[2]
            hidden_two = low(layer_norm(middle, n_gain[1], n_bias[1]))
            hidden = low_back(matmul(hidden_two, up_w) + u_bias)
            activated = low(jax.nn.gelu(hidden, approximate=True))
            result = middle + matmul(activated, down_w) + d_bias
            valid = (ids < IMAGES).astype(jnp.float32)
            return result * valid[:, None]
        return lax.map(jax.checkpoint(one_group), (inputs, counts))
    result, pullback = jax.vjp(forward, *floats)
    grads = pullback(cotangent.astype(jnp.float32))
    return (result.astype(jnp.bfloat16), grads[0].astype(jnp.bfloat16), grads[1], grads[2], grads[3], grads[4], grads[5], grads[6], grads[7], grads[8], grads[9])
```

```python
import functools
import math

import jax
import jax.numpy as jnp
from jax import lax
from jax.sharding import PartitionSpec as P

HEADS = 16
EPS = 1e-06
NEG = -1e30
F32 = jnp.float32
BF16 = jnp.bfloat16


def mm(spec, a, b):
    return jnp.einsum(spec, a, b, preferred_element_type=F32)


def normalize(values):
    mean = jnp.mean(values, axis=-1, keepdims=True)
    centred = values - mean
    scale = lax.rsqrt(jnp.mean(centred * centred, axis=-1, keepdims=True) + EPS)
    return (centred * scale, scale)


def norm_back(grad_norm, normed, scale, gain):
    scaled = grad_norm * gain
    return scale * (
        scaled
        - jnp.mean(scaled, axis=-1, keepdims=True)
        - normed * jnp.mean(scaled * normed, axis=-1, keepdims=True)
    )


def body(
    states, counts, cotangent, w_qkv, w_out, attn_bias, norm_gain, norm_bias,
    w_up, up_bias, w_down, down_bias,
):
    groups, rows, width = states.shape
    shards = lax.axis_size("seq")
    me = lax.axis_index("seq")
    size = width // HEADS
    ff = w_up.shape[1] // shards
    total = rows * shards
    factor = 1.0 / math.sqrt(size)
    ends = jnp.cumsum(counts, axis=1)
    ids = jnp.sum(
        (jnp.arange(total, dtype=jnp.int32)[None, :, None] >= ends[:, None, :]).astype(jnp.int32), axis=2
    )
    valid_all = (ids < counts.shape[1]).astype(F32)[..., None]
    valid = lax.dynamic_slice_in_dim(valid_all, me * rows, rows, 1)
    same = ids[:, :, None] == ids[:, None, :]

    def gather(x):
        return lax.all_gather(x, "seq", axis=1, tiled=True)

    wq = lax.dynamic_slice_in_dim(w_qkv, me * size, size, 2)
    wo = lax.dynamic_slice_in_dim(w_out, me * size, size, 0)
    wu = lax.dynamic_slice_in_dim(w_up, me * ff, ff, 1)
    wd = lax.dynamic_slice_in_dim(w_down, me * ff, ff, 0)
    bq = lax.dynamic_slice_in_dim(attn_bias, me * size, size, 1)
    bu = lax.dynamic_slice_in_dim(up_bias, me * ff, ff, 0)

    inputs = states.astype(F32)
    normed_one, scale_one = normalize(inputs)
    h1 = gather((normed_one * norm_gain[0] + norm_bias[0]).astype(BF16))
    grad_y = cotangent.astype(F32) * valid
    gy = gather(grad_y.astype(BF16))

    proj = mm("gtd,cde->cgte", h1, wq)
    query = ((proj[0] + bq[0]) * factor).astype(BF16)
    key = proj[1].astype(BF16)
    value = (proj[2] + bq[1]).astype(BF16)
    scores = jnp.where(same, mm("gqd,gkd->gqk", query, key), NEG)
    highest = jnp.max(scores, axis=-1, keepdims=True)
    weights = jnp.exp(scores - highest)
    totals = jnp.sum(weights, axis=-1, keepdims=True)
    attended = mm("gqk,gkd->gqd", weights.astype(BF16), value) / totals
    lse = highest + jnp.log(totals)
    att_b = attended.astype(BF16)
    att_mine = lax.all_to_all(att_b, "seq", split_axis=1, concat_axis=2, tiled=True)

    middle = inputs + mm("gtd,de->gte", att_mine, w_out) + attn_bias[2]
    normed_two, scale_two = normalize(middle)
    h2 = gather((normed_two * norm_gain[1] + norm_bias[1]).astype(BF16))
    hidden = mm("gtd,df->gtf", h2, wu) + bu
    act, gelu_back = jax.vjp(functools.partial(jax.nn.gelu, approximate=True), hidden)
    act_b = act.astype(BF16)
    down = lax.psum_scatter(
        mm("gtf,fd->gtd", act_b, wd).astype(BF16), "seq", scatter_dimension=1, tiled=True
    ).astype(F32)
    layer_out = ((middle + down + down_bias) * valid).astype(BF16)

    grad_down = mm("gtf,gtd->fd", act_b, gy)
    grad_down_bias = jnp.sum(gy.astype(F32), axis=(0, 1))
    grad_hidden = gelu_back(mm("gtd,fd->gtf", gy, wd))[0].astype(BF16)
    grad_up_bias = jnp.sum(grad_hidden.astype(F32), axis=(0, 1))
    grad_up = mm("gtd,gtf->df", h2, grad_hidden)
    grad_h2 = lax.psum_scatter(
        mm("gtf,df->gtd", grad_hidden, wu).astype(BF16), "seq", scatter_dimension=1, tiled=True
    ).astype(F32)
    gain_two = jnp.sum(grad_h2 * normed_two, axis=(0, 1))
    shift_two = jnp.sum(grad_h2, axis=(0, 1))
    grad_mid = grad_y + norm_back(grad_h2, normed_two, scale_two, norm_gain[1])
    out_bias = jnp.sum(grad_mid, axis=(0, 1))
    gm = gather(grad_mid.astype(BF16))
    grad_out = mm("gtd,gte->de", att_b, gm)
    grad_att = mm("gte,de->gtd", gm, wo).astype(BF16)

    delta = jnp.sum(grad_att.astype(F32) * attended, axis=-1, keepdims=True)
    scores2 = jnp.where(same, mm("gqd,gkd->gqk", query, key), NEG)
    probs = jnp.exp(scores2 - lse)
    grad_scores = (probs * (mm("gqd,gkd->gqk", grad_att, value) - delta)).astype(BF16)
    pre = jnp.stack(
        [
            (mm("gqk,gkd->gqd", grad_scores, key) * factor).astype(BF16),
            mm("gqk,gqd->gkd", grad_scores, query).astype(BF16),
            mm("gqk,gqd->gkd", probs.astype(BF16), grad_att).astype(BF16),
        ]
    )
    bias_sums = jnp.sum(pre.astype(F32), axis=(1, 2))
    grad_qkv = mm("gtd,cgte->cde", h1, pre)
    pre_mine = lax.all_to_all(pre, "seq", split_axis=2, concat_axis=3, tiled=True)
    grad_h1 = mm("cgte,cde->gtd", pre_mine, w_qkv)
    gain_one = jnp.sum(grad_h1 * normed_one, axis=(0, 1))
    shift_one = jnp.sum(grad_h1, axis=(0, 1))
    state_grad = (grad_mid + norm_back(grad_h1, normed_one, scale_one, norm_gain[0])).astype(BF16)

    qkv_rows = lax.all_to_all(grad_qkv.astype(BF16), "seq", split_axis=1, concat_axis=2, tiled=True)
    up_rows = lax.all_to_all(grad_up.astype(BF16), "seq", split_axis=0, concat_axis=1, tiled=True)
    wide = jnp.concatenate(
        [qkv_rows.reshape(-1, width), grad_out.astype(BF16), grad_down.astype(BF16)], axis=0
    )
    wide = lax.psum_scatter(wide, "dp", scatter_dimension=1, tiled=True).astype(F32)
    up_part = lax.psum_scatter(up_rows, "dp", scatter_dimension=1, tiled=True).astype(F32)
    vectors = lax.psum(jnp.stack([gain_one, gain_two, shift_one, shift_two, out_bias]), ("dp", "seq"))
    vectors = lax.dynamic_slice_in_dim(vectors, me * size, size, 1)
    pairs = lax.psum(
        (
            jnp.stack(
                [bias_sums[0], bias_sums[2], lax.dynamic_slice_in_dim(grad_down_bias, me * size, size, 0)]
            ),
            grad_up_bias,
        ),
        "dp",
    )
    narrow = wide.shape[1]
    return (
        layer_out,
        state_grad,
        wide[: 3 * size].reshape(3, size, narrow),
        wide[3 * size : 4 * size],
        jnp.stack([pairs[0][0], pairs[0][1], vectors[4]]),
        vectors[0:2],
        vectors[2:4],
        up_part,
        pairs[1],
        wide[4 * size :],
        pairs[0][2],
    )


def solution(mesh):
    placed = (P("dp", "seq", None), P("dp", None), P("dp", "seq", None)) + (P(),) * 9
    return jax.shard_map(
        body,
        mesh=mesh,
        in_specs=placed,
        out_specs=(
            P("dp", "seq", None), P("dp", "seq", None), P(None, "seq", "dp"), P("seq", "dp"),
            P(None, "seq"), P(None, "seq"), P(None, "seq"), P("seq", "dp"), P("seq"),
            P("seq", "dp"), P("seq"),
        ),
        check_vma=False,
    )
```

```python
import functools
import math

import jax
import jax.numpy as jnp
from jax import lax
from jax.experimental import pallas as pl
from jax.experimental.pallas import tpu as pltpu
from jax.sharding import PartitionSpec as P

HEADS = 16
EPS = 1e-06
NEG = -1e30
F32 = jnp.float32
BF16 = jnp.bfloat16
MESH = pl.DeviceIdType.MESH
VMEM = pltpu.VMEM
DMA = pltpu.SemaphoreType.DMA


def mm(spec, a, b):
    return jnp.einsum(spec, a, b, preferred_element_type=F32)


def dot(a, b, ca=1, cb=0):
    return lax.dot_general(a, b, (((ca,), (cb,)), ((), ())), preferred_element_type=F32)


def pad_to(x, axis, size):
    pads = [(0, 0)] * x.ndim
    pads[axis] = (0, size - x.shape[axis])
    return jnp.pad(x, pads)


def up128(n):
    return -(-n // 128) * 128


def normalize(values):
    mean = jnp.mean(values, axis=-1, keepdims=True)
    centred = values - mean
    scale = lax.rsqrt(jnp.mean(centred * centred, axis=-1, keepdims=True) + EPS)
    return (centred * scale, scale)


def norm_back(grad_norm, normed, scale, gain):
    scaled = grad_norm * gain
    return scale * (
        scaled
        - jnp.mean(scaled, axis=-1, keepdims=True)
        - normed * jnp.mean(scaled * normed, axis=-1, keepdims=True)
    )


def gelu_both(v):
    c, a = 0.7978845608028654, 0.044715
    sq = v * v
    t = jnp.tanh(c * (v + a * v * sq))
    half = 0.5 * (1.0 + t)
    return v * half, half + 0.5 * v * (1.0 - t * t) * (c * (1.0 + 3.0 * a * sq))


class Ring:
    def __init__(self, shards):
        self.n = shards // 2
        self.half = self.n // 2
        self.me = lax.axis_index("seq")
        self.chip = self.me // 2
        self.core = self.me % 2
        odd = self.chip % 2
        self.pos = (1 - odd) * (self.chip // 2) + odd * (self.n - 1 - self.chip // 2)
        self.to = (self.at(1, 1) * 2 + self.core, self.at(1, 0) * 2 + self.core)
        self.sib = self.chip * 2 + 1 - self.core

    def at(self, k, d):
        p = (self.pos + (self.n - k if d == 0 else k)) % self.n
        hi = p // self.half
        return (1 - hi) * 2 * p + hi * (2 * (self.n - 1 - p) + 1)

    def greet(self):
        bar = pltpu.get_barrier_semaphore()
        for d in self.to + (self.sib,):
            pl.semaphore_signal(bar, inc=1, device_id={"seq": d}, device_id_type=MESH)

    def met(self):
        pl.semaphore_wait(pltpu.get_barrier_semaphore(), 3)


def gather_sems(shards):
    return [DMA((2, shards // 4 + 1, 2))] * 4


class Gather:
    def __init__(self, ring, buf, sems):
        self.ring, self.buf = ring, buf
        self.ring_s, self.ring_r, self.sib_s, self.sib_r = sems
        self.sent = []

    def copy(self, k, d, g, to_sib):
        block = self.buf.at[self.ring.at(k, d) * 2 + self.ring.core, g]
        s, r = (self.sib_s, self.sib_r) if to_sib else (self.ring_s, self.ring_r)
        return pltpu.make_async_remote_copy(
            src_ref=block, dst_ref=block, send_sem=s.at[d, k, g], recv_sem=r.at[d, k, g],
            device_id={"seq": self.ring.sib if to_sib else self.ring.to[d]}, device_id_type=MESH,
        )

    def units(self, k):
        if k == self.ring.half:
            return [(0, 0), (1, 1)]
        return [(0, 0), (1, 1), (0, 1), (1, 0)]

    def hop(self, k):
        half = self.ring.half
        for d, g in self.units(k):
            if k > 0:
                self.copy(k - 1, d, g, False).wait_recv()
            if k < half - 1 or (k == half - 1 and g == d):
                c = self.copy(k, d, g, False)
                c.start()
                self.sent.append(c)
        for d, g in self.units(k):
            if k > 0 or d == g:
                c = self.copy(k, d, g, True)
                c.start()
                self.sent.append(c)

    def ready(self, k):
        for d, g in self.units(k):
            if k > 0 or d == g:
                self.copy(k, d, g, True).wait_recv()

    def blocks(self, k):
        if k == 0 or k == self.ring.half:
            return [self.ring.at(k, 0)]
        return [self.ring.at(k, 0), self.ring.at(k, 1)]

    def finish(self):
        for c in self.sent:
            c.wait_send()


def scatter_scratch(shards, rows, width):
    n = shards // 2
    return [
        VMEM((n, 2, rows, width), BF16), VMEM((2, n // 2, 2, rows, width), BF16),
        DMA((n,)), DMA((n,)), DMA((2, n // 2, 2)), DMA((2, n // 2, 2)),
    ]


class Scatter:
    def __init__(self, ring, part, scratch):
        self.ring, self.part = ring, part
        self.sib_land, self.land, self.sib_s, self.sib_r, self.ring_s, self.ring_r = scratch
        self.sent = []

    def slot(self, k, d):
        if k == 0:
            return 0
        return self.ring.n - 1 if k == self.ring.half else 2 * k - 1 + d

    def sib_copy(self, k, d):
        r, i = self.ring, self.slot(k, d)
        return pltpu.make_async_remote_copy(
            src_ref=self.part.at[r.at(k, d) * 2 + 1 - r.core], dst_ref=self.sib_land.at[i],
            send_sem=self.sib_s.at[i], recv_sem=self.sib_r.at[i],
            device_id={"seq": r.sib}, device_id_type=MESH,
        )

    def give(self, k, d):
        c = self.sib_copy(k, d)
        c.start()
        self.sent.append(c)

    def ring_copy(self, h, d, g):
        r = self.ring
        return pltpu.make_async_remote_copy(
            src_ref=self.part.at[r.at(r.half - h, 1 - d) * 2 + r.core, g], dst_ref=self.land.at[d, h, g],
            send_sem=self.ring_s.at[d, h, g], recv_sem=self.ring_r.at[d, h, g],
            device_id={"seq": r.to[d]}, device_id_type=MESH,
        )

    def hop(self, h):
        r = self.ring
        j = r.half - h
        order = [(0, 0), (1, 1)] if h == 0 else [(0, 0), (1, 1), (0, 1), (1, 0)]
        if h == 0:
            self.sib_copy(j, 0).wait_recv()
        else:
            self.sib_copy(j, 0).wait_recv()
            self.sib_copy(j, 1).wait_recv()
        for d, g in order:
            own = r.at(j, 1 - d) * 2 + r.core
            val = self.part[own, g].astype(F32) + self.sib_land[self.slot(j, 1 - d), g].astype(F32)
            if h >= 2 or (h == 1 and g == d):
                self.ring_copy(h - 1, d, g).wait_recv()
                val = val + self.land[d, h - 1, g].astype(F32)
            self.part[own, g] = val.astype(BF16)
            c = self.ring_copy(h, d, g)
            c.start()
            self.sent.append(c)

    def result(self):
        r = self.ring
        self.sib_copy(0, 0).wait_recv()
        out = []
        for g in range(2):
            val = self.part[r.me, g].astype(F32) + self.sib_land[0, g].astype(F32)
            for d in range(2):
                self.ring_copy(r.half - 1, d, g).wait_recv()
                val = val + self.land[d, r.half - 1, g].astype(F32)
            out.append(val)
        return jnp.concatenate(out, axis=0)

    def finish(self):
        for c in self.sent:
            c.wait_send()


def first_kernel(shards, x_ref, vec_ref, w_ref, b_ref, h_ref, qkv_ref, *sems):
    ring = Ring(shards)
    ring.greet()
    groups, rows, width = x_ref.shape
    normed, _ = normalize(x_ref[...].reshape(groups * rows, width).astype(F32))
    h = (normed * vec_ref[0:1] + vec_ref[1:2]).astype(BF16)
    h_ref[ring.me] = h.reshape(groups, rows, width)
    ring.met()
    gat = Gather(ring, h_ref, sems)

    def work(chip):
        block = h_ref[pl.ds(2 * chip, 2)].reshape(4 * rows, width)
        out = ((dot(block, w_ref[...]) + b_ref[0:1]) * b_ref[1:2]).astype(BF16)
        qkv_ref[pl.ds(2 * chip, 2)] = out.reshape(2, groups, rows, out.shape[1])

    gat.hop(0)
    for k in range(1, ring.half + 1):
        gat.ready(k - 1)
        for chip in gat.blocks(k - 1):
            work(chip)
        gat.hop(k)
    gat.ready(ring.half)
    for chip in gat.blocks(ring.half):
        work(chip)
    gat.finish()


def first(shards, states, vecs, weights, consts):
    groups, rows, width = states.shape
    wide = weights.shape[1]
    return pl.pallas_call(
        functools.partial(first_kernel, shards),
        out_shape=[
            jax.ShapeDtypeStruct((shards, groups, rows, width), BF16),
            jax.ShapeDtypeStruct((shards, groups, rows, wide), BF16),
        ],
        in_specs=[pl.BlockSpec(memory_space=VMEM)] * 4,
        out_specs=[pl.BlockSpec(memory_space=VMEM)] * 2,
        scratch_shapes=gather_sems(shards),
        name="first",
        compiler_params=pltpu.CompilerParams(
            collective_id=0, has_side_effects=True, vmem_limit_bytes=40 << 20
        ),
    )(states, vecs, weights, consts)


def middle_kernel(
    shards, att_ref, x_ref, gy_ref, atts_ref, vec_ref, bu_ref, wout_ref, wo_ref, wu_ref, wd_ref,
    mid_ref, gmid_ref, gatt_ref, gout_ref, gup_ref, gdown_ref, down_ref, sums_ref, bup_ref,
    h_buf, m_buf, part, act_buf, ghid_buf, gact_buf, *rest,
):
    ring = Ring(shards)
    ring.greet()
    groups, rows, width = x_ref.shape
    own = groups * rows
    gat = Gather(ring, h_buf, rest[0:4])
    gat2 = Gather(ring, m_buf, rest[4:8])
    sca = Scatter(ring, part, rest[8:14])
    half = ring.half
    mid = (
        x_ref[...].reshape(own, width).astype(F32)
        + dot(att_ref[...].reshape(own, width), wout_ref[...])
        + vec_ref[2:3]
    )
    mid_ref[...] = mid.reshape(groups, rows, width)
    normed, scale = normalize(mid)
    h_buf[ring.me] = (normed * vec_ref[0:1] + vec_ref[1:2]).astype(BF16).reshape(groups, rows, width)
    ring.met()

    def rows_of(ref, chip):
        return ref[pl.ds(2 * chip, 2)].reshape(4 * rows, ref.shape[-1])

    def put(ref, chip, val):
        ref[pl.ds(2 * chip, 2)] = val.astype(ref.dtype).reshape((2, groups, rows, ref.shape[-1]))

    def grad_act(chip):
        put(gact_buf, chip, dot(rows_of(gy_ref, chip), wd_ref[...], 1, 1))

    def forward(chip):
        hidden = dot(rows_of(h_buf, chip), wu_ref[...]) + bu_ref[...]
        act, slope = gelu_both(hidden)
        put(act_buf, chip, act)
        ghid = (rows_of(gact_buf, chip) * slope).astype(BF16)
        put(ghid_buf, chip, ghid)
        put(part, chip, dot(ghid, wu_ref[...], 1, 1))

    gat.hop(0)
    grad_act(ring.at(0, 0))
    for k in range(half):
        gat.ready(k)
        for d, chip in enumerate(gat.blocks(k)):
            forward(chip)
            sca.give(k, d)
        for chip in gat.blocks(k + 1):
            grad_act(chip)
        gat.hop(k + 1)
    gat.ready(half)
    forward(ring.at(half, 0))
    sca.give(half, 0)
    for h in range(half):
        sca.hop(h)
    grad_h2 = sca.result()
    mean_h = mid_ref[...].reshape(own, width)
    normed, scale = normalize(mean_h)
    gy_own = gy_ref[ring.me].reshape(own, width).astype(F32)
    gmid = gy_own + norm_back(grad_h2, normed, scale, vec_ref[0:1])
    gmid_ref[...] = gmid.reshape(groups, rows, width)
    m_buf[ring.me] = gmid.astype(BF16).reshape(groups, rows, width)
    gat2.hop(0)
    sums_ref[0:1] = jnp.sum(grad_h2 * normed, axis=0, keepdims=True)
    sums_ref[1:2] = jnp.sum(grad_h2, axis=0, keepdims=True)
    sums_ref[2:3] = jnp.sum(gmid, axis=0, keepdims=True)

    def back(chip, first_one):
        block = rows_of(m_buf, chip)
        put(gatt_ref, chip, dot(block, wo_ref[...], 1, 1))
        part_out = dot(rows_of(atts_ref, chip), block, 0, 0)
        gout_ref[...] = part_out if first_one else gout_ref[...] + part_out

    tokens = shards * own
    flat = lambda ref: ref[...].reshape(tokens, ref.shape[-1])

    def down_part(chip):
        put(down_ref, chip, dot(rows_of(act_buf, chip), wd_ref[...]))

    for k in range(half):
        if k == 0:
            sums_ref[3:4] = jnp.sum(flat(gy_ref).astype(F32), axis=0, keepdims=True)
            bup_ref[...] = jnp.sum(flat(ghid_buf).astype(F32), axis=0, keepdims=True)
            gdown_ref[...] = dot(flat(act_buf), flat(gy_ref), 0, 0)
        if k == 1:
            gup_ref[...] = dot(flat(ghid_buf), flat(h_buf), 0, 0)
        for chip in gat.blocks(k):
            down_part(chip)
        gat2.hop(k + 1)
        gat2.ready(k)
        for chip in gat2.blocks(k):
            back(chip, k == 0)
    down_part(ring.at(half, 0))
    gat2.ready(half)
    back(ring.at(half, 0), False)
    gat.finish()
    gat2.finish()
    sca.finish()


def middle(shards, att, states, gy, att_head, vecs, bu, w_out, wo, wu, wd):
    groups, rows, width = states.shape
    ffp, hp = wu.shape[1], wo.shape[0]
    blocks = (shards, groups, rows)
    sds = jax.ShapeDtypeStruct
    return pl.pallas_call(
        functools.partial(middle_kernel, shards),
        out_shape=[
            sds((groups, rows, width), F32), sds((groups, rows, width), F32), sds(blocks + (hp,), BF16),
            sds((hp, width), F32), sds((ffp, width), F32), sds((ffp, width), F32), sds(blocks + (width,), BF16),
            sds((8, width), F32), sds((1, ffp), F32),
        ],
        in_specs=[pl.BlockSpec(memory_space=VMEM)] * 10,
        out_specs=[pl.BlockSpec(memory_space=VMEM)] * 9,
        scratch_shapes=[
            VMEM(blocks + (width,), BF16), VMEM(blocks + (width,), BF16), VMEM(blocks + (width,), BF16),
            VMEM(blocks + (ffp,), BF16), VMEM(blocks + (ffp,), BF16), VMEM(blocks + (ffp,), F32),
        ]
        + gather_sems(shards) * 2
        + scatter_scratch(shards, rows, width),
        name="middle",
        compiler_params=pltpu.CompilerParams(
            collective_id=1, has_side_effects=True, vmem_limit_bytes=60 << 20
        ),
    )(att, states, gy, att_head, vecs, bu, w_out, wo, wu, wd)


def body(
    states, counts, cotangent, w_qkv, w_out, attn_bias, norm_gain, norm_bias,
    w_up, up_bias, w_down, down_bias,
):
    groups, rows, width = states.shape
    shards = lax.axis_size("seq")
    me = lax.axis_index("seq")
    size = width // HEADS
    sp = up128(size)
    ff = w_up.shape[1] // shards
    ffp = up128(ff)
    total = rows * shards
    factor = 1.0 / math.sqrt(size)
    ends = jnp.cumsum(counts, axis=1)
    ids = jnp.sum(
        (jnp.arange(total, dtype=jnp.int32)[None, :, None] >= ends[:, None, :]).astype(jnp.int32), axis=2
    )
    valid_all = (ids < counts.shape[1]).astype(F32)[..., None]
    valid = lax.dynamic_slice_in_dim(valid_all, me * rows, rows, 1)
    same = ids[:, :, None] == ids[:, None, :]

    def by_block(x):
        return jnp.transpose(x.reshape(groups, shards, rows, -1), (1, 0, 2, 3))

    def by_group(x):
        return jnp.transpose(x, (1, 0, 2, 3)).reshape(groups, total, -1)

    def mine(x, axis, count):
        return lax.dynamic_slice_in_dim(x, me * count, count, axis)

    wq = pad_to(mine(w_qkv, 2, size), 2, sp)
    wq = jnp.transpose(wq, (1, 0, 2)).reshape(width, 3 * sp)
    wo = pad_to(mine(w_out, 0, size), 0, sp)
    wu = pad_to(mine(w_up, 1, ff), 1, ffp)
    wd = pad_to(mine(w_down, 0, ff), 0, ffp)
    bq = pad_to(mine(attn_bias, 1, size), 1, sp)
    bu = pad_to(mine(up_bias, 0, ff), 0, ffp)[None]
    consts = jnp.stack(
        [
            jnp.concatenate([bq[0], jnp.zeros_like(bq[0]), bq[1]]),
            jnp.concatenate([jnp.full((sp,), factor, F32), jnp.ones((2 * sp,), F32)]),
        ]
    )

    h1, qkv = first(shards, states, jnp.stack([norm_gain[0], norm_bias[0]]), wq, consts)
    grad_y = (cotangent.astype(F32) * valid).astype(BF16)
    gy = lax.all_gather(grad_y, "seq", axis=0)

    qkv = by_group(qkv)
    query, key, value = qkv[..., :sp], qkv[..., sp : 2 * sp], qkv[..., 2 * sp :]
    scores = jnp.where(same, mm("gqd,gkd->gqk", query, key), NEG)
    highest = jnp.max(scores, axis=-1, keepdims=True)
    weights = jnp.exp(scores - highest)
    totals = jnp.sum(weights, axis=-1, keepdims=True)
    attended = mm("gqk,gkd->gqd", weights.astype(BF16), value) / totals
    lse = highest + jnp.log(totals)
    att_b = attended.astype(BF16)
    att_mine = lax.all_to_all(att_b[..., :size], "seq", split_axis=1, concat_axis=2, tiled=True)

    mid, grad_mid, grad_att, grad_out, grad_up, grad_down, down_part, sums, up_sums = middle(
        shards, att_mine, states, gy, by_block(att_b),
        jnp.stack([norm_gain[1], norm_bias[1], attn_bias[2]]), bu, w_out, wo, wu, wd,
    )
    down = lax.psum_scatter(down_part, "seq", scatter_dimension=0, tiled=False).astype(F32)
    layer_out = ((mid + down + down_bias) * valid).astype(BF16)
    grad_att = by_group(grad_att)
    grad_out, grad_up, grad_down = grad_out[:size], grad_up[:ff], grad_down[:ff]

    delta = jnp.sum(grad_att.astype(F32) * attended, axis=-1, keepdims=True)
    scores2 = jnp.where(same, mm("gqd,gkd->gqk", query, key), NEG)
    probs = jnp.exp(scores2 - lse)
    grad_scores = (probs * (mm("gqd,gkd->gqk", grad_att, value) - delta)).astype(BF16)
    pre = jnp.stack(
        [
            (mm("gqk,gkd->gqd", grad_scores, key) * factor).astype(BF16),
            mm("gqk,gqd->gkd", grad_scores, query).astype(BF16),
            mm("gqk,gqd->gkd", probs.astype(BF16), grad_att).astype(BF16),
        ]
    )[..., :size]
    bias_sums = jnp.sum(pre.astype(F32), axis=(1, 2))
    grad_qkv = mm("gtd,cgte->cde", by_group(h1), pre)
    pre_mine = lax.all_to_all(pre, "seq", split_axis=2, concat_axis=3, tiled=True)
    grad_h1 = mm("cgte,cde->gtd", pre_mine, w_qkv)
    normed_one, scale_one = normalize(states.astype(F32))
    gain_one = jnp.sum(grad_h1 * normed_one, axis=(0, 1))
    shift_one = jnp.sum(grad_h1, axis=(0, 1))
    state_grad = (grad_mid + norm_back(grad_h1, normed_one, scale_one, norm_gain[0])).astype(BF16)

    qkv_rows = lax.all_to_all(grad_qkv.astype(BF16), "seq", split_axis=1, concat_axis=2, tiled=True)
    up_rows = lax.all_to_all(grad_up.T.astype(BF16), "seq", split_axis=0, concat_axis=1, tiled=True)
    wide = jnp.concatenate(
        [qkv_rows.reshape(-1, width), grad_out.astype(BF16), grad_down.astype(BF16)], axis=0
    )
    wide = lax.psum_scatter(wide, "dp", scatter_dimension=1, tiled=True).astype(F32)
    up_part = lax.psum_scatter(up_rows, "dp", scatter_dimension=1, tiled=True).astype(F32)
    vectors = lax.psum(jnp.stack([gain_one, sums[0], shift_one, sums[1], sums[2]]), ("dp", "seq"))
    vectors = mine(vectors, 1, size)
    pairs = lax.psum(
        (jnp.stack([bias_sums[0], bias_sums[2], mine(sums[3], 0, size)]), up_sums[0, :ff]), "dp"
    )
    narrow = wide.shape[1]
    return (
        layer_out,
        state_grad,
        wide[: 3 * size].reshape(3, size, narrow),
        wide[3 * size : 4 * size],
        jnp.stack([pairs[0][0], pairs[0][1], vectors[4]]),
        vectors[0:2],
        vectors[2:4],
        up_part,
        pairs[1],
        wide[4 * size :],
        pairs[0][2],
    )


def solution(mesh):
    placed = (P("dp", "seq", None), P("dp", None), P("dp", "seq", None)) + (P(),) * 9
    return jax.shard_map(
        body,
        mesh=mesh,
        in_specs=placed,
        out_specs=(
            P("dp", "seq", None), P("dp", "seq", None), P(None, "seq", "dp"), P("seq", "dp"),
            P(None, "seq"), P(None, "seq"), P(None, "seq"), P("seq", "dp"), P("seq"),
            P("seq", "dp"), P("seq"),
        ),
        check_vma=False,
    )
```

```python
import functools
import math

import jax
import jax.numpy as jnp
from jax import lax
from jax.experimental import pallas as pl
from jax.experimental.pallas import tpu as pltpu
from jax.sharding import PartitionSpec as P

HEADS = 16
EPS = 1e-06
NEG = -1e30
F32 = jnp.float32
BF16 = jnp.bfloat16
MESH = pl.DeviceIdType.MESH
VMEM = pltpu.VMEM
DMA = pltpu.SemaphoreType.DMA


def mm(spec, a, b):
    return jnp.einsum(spec, a, b, preferred_element_type=F32)


def dot(a, b, ca=1, cb=0):
    return lax.dot_general(a, b, (((ca,), (cb,)), ((), ())), preferred_element_type=F32)


def pad_to(x, axis, size):
    pads = [(0, 0)] * x.ndim
    pads[axis] = (0, size - x.shape[axis])
    return jnp.pad(x, pads)


def up128(n):
    return -(-n // 128) * 128


def normalize(values):
    mean = jnp.mean(values, axis=-1, keepdims=True)
    centred = values - mean
    scale = lax.rsqrt(jnp.mean(centred * centred, axis=-1, keepdims=True) + EPS)
    return (centred * scale, scale)


def norm_back(grad_norm, normed, scale, gain):
    scaled = grad_norm * gain
    return scale * (
        scaled
        - jnp.mean(scaled, axis=-1, keepdims=True)
        - normed * jnp.mean(scaled * normed, axis=-1, keepdims=True)
    )


def gelu_both(v):
    c, a = 0.7978845608028654, 0.044715
    sq = v * v
    t = jnp.tanh(c * (v + a * v * sq))
    half = 0.5 * (1.0 + t)
    return v * half, half + 0.5 * v * (1.0 - t * t) * (c * (1.0 + 3.0 * a * sq))


class Ring:
    def __init__(self, shards):
        self.n = shards // 2
        self.half = self.n // 2
        self.me = lax.axis_index("seq")
        self.chip = self.me // 2
        self.core = self.me % 2
        odd = self.chip % 2
        self.pos = (1 - odd) * (self.chip // 2) + odd * (self.n - 1 - self.chip // 2)
        self.to = (self.at(1, 1) * 2 + self.core, self.at(1, 0) * 2 + self.core)
        self.sib = self.chip * 2 + 1 - self.core

    def at(self, k, d):
        p = (self.pos + (self.n - k if d == 0 else k)) % self.n
        hi = p // self.half
        return (1 - hi) * 2 * p + hi * (2 * (self.n - 1 - p) + 1)

    def greet(self, everyone=False):
        bar = pltpu.get_barrier_semaphore()
        others = self.to + (self.sib,)
        if everyone:
            others = [(self.me + j) % (2 * self.n) for j in range(1, 2 * self.n)]
        for d in others:
            pl.semaphore_signal(bar, inc=1, device_id={"seq": d}, device_id_type=MESH)
        self.greeted = len(others)

    def met(self):
        pl.semaphore_wait(pltpu.get_barrier_semaphore(), self.greeted)


def gather_sems(shards):
    return [DMA((2, shards // 4 + 1, 2))] * 4


class Gather:
    def __init__(self, ring, buf, sems):
        self.ring, self.buf = ring, buf
        self.ring_s, self.ring_r, self.sib_s, self.sib_r = sems
        self.sent = []

    def copy(self, k, d, g, to_sib):
        block = self.buf.at[self.ring.at(k, d) * 2 + self.ring.core, g]
        s, r = (self.sib_s, self.sib_r) if to_sib else (self.ring_s, self.ring_r)
        return pltpu.make_async_remote_copy(
            src_ref=block, dst_ref=block, send_sem=s.at[d, k, g], recv_sem=r.at[d, k, g],
            device_id={"seq": self.ring.sib if to_sib else self.ring.to[d]}, device_id_type=MESH,
        )

    def units(self, k):
        if k == self.ring.half:
            return [(0, 0), (1, 1)]
        return [(0, 0), (1, 1), (0, 1), (1, 0)]

    def hop(self, k):
        half = self.ring.half
        for d, g in self.units(k):
            if k > 0:
                self.copy(k - 1, d, g, False).wait_recv()
            if k < half - 1 or (k == half - 1 and g == d):
                c = self.copy(k, d, g, False)
                c.start()
                self.sent.append(c)
        for d, g in self.units(k):
            if k > 0 or d == g:
                c = self.copy(k, d, g, True)
                c.start()
                self.sent.append(c)

    def ready(self, k):
        for d, g in self.units(k):
            if k > 0 or d == g:
                self.copy(k, d, g, True).wait_recv()

    def blocks(self, k):
        if k == 0 or k == self.ring.half:
            return [self.ring.at(k, 0)]
        return [self.ring.at(k, 0), self.ring.at(k, 1)]

    def finish(self):
        for c in self.sent:
            c.wait_send()


def scatter_scratch(shards, rows, width):
    n = shards // 2
    return [
        VMEM((n, 2, rows, width), BF16), VMEM((2, n // 2, 2, rows, width), BF16),
        DMA((n,)), DMA((n,)), DMA((2, n // 2, 2)), DMA((2, n // 2, 2)),
    ]


class Scatter:
    def __init__(self, ring, part, scratch):
        self.ring, self.part = ring, part
        self.sib_land, self.land, self.sib_s, self.sib_r, self.ring_s, self.ring_r = scratch
        self.sent = []

    def slot(self, k, d):
        if k == 0:
            return 0
        return self.ring.n - 1 if k == self.ring.half else 2 * k - 1 + d

    def sib_copy(self, k, d):
        r, i = self.ring, self.slot(k, d)
        return pltpu.make_async_remote_copy(
            src_ref=self.part.at[r.at(k, d) * 2 + 1 - r.core], dst_ref=self.sib_land.at[i],
            send_sem=self.sib_s.at[i], recv_sem=self.sib_r.at[i],
            device_id={"seq": r.sib}, device_id_type=MESH,
        )

    def give(self, k, d):
        c = self.sib_copy(k, d)
        c.start()
        self.sent.append(c)

    def ring_copy(self, h, d, g):
        r = self.ring
        return pltpu.make_async_remote_copy(
            src_ref=self.part.at[r.at(r.half - h, 1 - d) * 2 + r.core, g], dst_ref=self.land.at[d, h, g],
            send_sem=self.ring_s.at[d, h, g], recv_sem=self.ring_r.at[d, h, g],
            device_id={"seq": r.to[d]}, device_id_type=MESH,
        )

    def hop(self, h):
        r = self.ring
        j = r.half - h
        order = [(0, 0), (1, 1)] if h == 0 else [(0, 0), (1, 1), (0, 1), (1, 0)]
        if h == 0:
            self.sib_copy(j, 0).wait_recv()
        else:
            self.sib_copy(j, 0).wait_recv()
            self.sib_copy(j, 1).wait_recv()
        for d, g in order:
            own = r.at(j, 1 - d) * 2 + r.core
            val = self.part[own, g].astype(F32) + self.sib_land[self.slot(j, 1 - d), g].astype(F32)
            if h >= 2 or (h == 1 and g == d):
                self.ring_copy(h - 1, d, g).wait_recv()
                val = val + self.land[d, h - 1, g].astype(F32)
            self.part[own, g] = val.astype(BF16)
            c = self.ring_copy(h, d, g)
            c.start()
            self.sent.append(c)

    def result(self):
        r = self.ring
        self.sib_copy(0, 0).wait_recv()
        out = []
        for g in range(2):
            val = self.part[r.me, g].astype(F32) + self.sib_land[0, g].astype(F32)
            for d in range(2):
                self.ring_copy(r.half - 1, d, g).wait_recv()
                val = val + self.land[d, r.half - 1, g].astype(F32)
            out.append(val)
        return jnp.concatenate(out, axis=0)

    def finish(self):
        for c in self.sent:
            c.wait_send()


def chip_rows(ref, chip):
    val = ref[pl.ds(2 * chip, 2)]
    return val.reshape(-1, val.shape[-1])


def chip_put(ref, chip, val):
    ref[pl.ds(2 * chip, 2)] = val.astype(ref.dtype).reshape((2,) + ref.shape[1:])


def chip_put_grouped(ref, chip, val):
    rows = ref.shape[2]
    val = val.astype(ref.dtype)
    for i in range(2):
        for g in range(2):
            at = (2 * i + g) * rows
            ref[g, 2 * chip + i] = val[at : at + rows]


def chip_rows_grouped(ref, chip):
    return jnp.concatenate([ref[g, 2 * chip + i] for i in range(2) for g in range(2)], axis=0)


def first_kernel(shards, x_ref, vec_ref, w_ref, b_ref, h_ref, q_ref, k_ref, v_ref, *sems):
    ring = Ring(shards)
    ring.greet()
    groups, rows, width = x_ref.shape
    normed, _ = normalize(x_ref[...].reshape(groups * rows, width).astype(F32))
    h = (normed * vec_ref[0:1] + vec_ref[1:2]).astype(BF16)
    h_ref[ring.me] = h.reshape(groups, rows, width)
    ring.met()
    gat = Gather(ring, h_ref, sems)

    def work(chip):
        out = (dot(chip_rows(h_ref, chip), w_ref[...]) + b_ref[0:1]) * b_ref[1:2]
        part = out.shape[1] // 3
        for i, ref in enumerate((q_ref, k_ref, v_ref)):
            chip_put_grouped(ref, chip, out[:, i * part : (i + 1) * part])

    gat.hop(0)
    for k in range(1, ring.half + 1):
        gat.ready(k - 1)
        for chip in gat.blocks(k - 1):
            work(chip)
        gat.hop(k)
    gat.ready(ring.half)
    for chip in gat.blocks(ring.half):
        work(chip)
    gat.finish()


def first(shards, states, vecs, weights, consts):
    groups, rows, width = states.shape
    wide = weights.shape[1]
    return pl.pallas_call(
        functools.partial(first_kernel, shards),
        out_shape=[
            jax.ShapeDtypeStruct((shards, groups, rows, width), BF16),
        ]
        + [jax.ShapeDtypeStruct((groups, shards, rows, wide // 3), BF16)] * 3,
        in_specs=[pl.BlockSpec(memory_space=VMEM)] * 4,
        out_specs=[pl.BlockSpec(memory_space=VMEM)] * 4,
        scratch_shapes=gather_sems(shards),
        name="first",
        compiler_params=pltpu.CompilerParams(
            collective_id=0, has_side_effects=True, vmem_limit_bytes=40 << 20
        ),
    )(states, vecs, weights, consts)


def middle_kernel(
    shards, size, ff, parts,
    att_ref, x_ref, gy_ref, vec_ref, bu_ref, wout_ref, wo_ref, wu_ref, wd_ref,
    mid_ref, gmid_ref, gatt_ref, gup_ref, gdo_ref, down_ref, sums_ref, bup_ref,
    h_buf, m_buf, part, act_buf, ghid_buf, gact_buf, att_land, att_buf, att_s, att_r, att_l, *rest,
):
    ring = Ring(shards)
    ring.greet(True)
    groups, rows, width = x_ref.shape
    own = groups * rows
    gat = Gather(ring, h_buf, rest[0:4])
    gat2 = Gather(ring, m_buf, rest[4:8])
    sca = Scatter(ring, part, rest[8:14])
    half = ring.half

    def grad_act(chip):
        chip_put(gact_buf, chip, dot(chip_rows(gy_ref, chip), wd_ref[...], 1, 1))

    def forward(chip):
        hidden = dot(chip_rows(h_buf, chip), wu_ref[...]) + bu_ref[...]
        act, slope = gelu_both(hidden)
        chip_put(act_buf, chip, act)
        ghid = (chip_rows(gact_buf, chip) * slope).astype(BF16)
        chip_put(ghid_buf, chip, ghid)
        chip_put(part, chip, dot(ghid, wu_ref[...], 1, 1))

    def att_copy(j):
        to = (ring.me + j) % shards
        return pltpu.make_async_remote_copy(
            src_ref=att_ref.at[:, to], dst_ref=att_land.at[ring.me], send_sem=att_s.at[j], recv_sem=att_r.at[j],
            device_id={"seq": to}, device_id_type=MESH,
        )

    def att_wait(j):
        frm = (ring.me + shards - j) % shards
        return pltpu.make_async_remote_copy(
            src_ref=att_ref.at[:, frm], dst_ref=att_land.at[frm], send_sem=att_s.at[j], recv_sem=att_r.at[j],
            device_id={"seq": frm}, device_id_type=MESH,
        )

    local = pltpu.make_async_copy(att_ref.at[:, ring.me], att_land.at[ring.me], att_l)
    local.start()
    ring.met()
    for j in range(1, shards):
        att_copy(j).start()
    grad_act(ring.at(0, 0))
    for d in range(2):
        grad_act(ring.at(1, d))
    local.wait()
    for j in range(1, shards):
        att_wait(j).wait_recv()
    for h in range(shards):
        att_buf[:, h * size : (h + 1) * size] = att_land[h].reshape(own, -1)[:, :size]
    mid = x_ref[...].reshape(own, width).astype(F32) + dot(att_buf[...], wout_ref[...]) + vec_ref[2:3]
    mid_ref[...] = mid.reshape(groups, rows, width)
    normed, scale = normalize(mid)
    h_buf[ring.me] = (normed * vec_ref[0:1] + vec_ref[1:2]).astype(BF16).reshape(groups, rows, width)

    gat.hop(0)
    for k in range(half):
        gat.ready(k)
        for d, chip in enumerate(gat.blocks(k)):
            forward(chip)
            sca.give(k, d)
        if k > 0:
            for chip in gat.blocks(k + 1):
                grad_act(chip)
        gat.hop(k + 1)
    gat.ready(half)
    forward(ring.at(half, 0))
    sca.give(half, 0)
    for h in range(half):
        sca.hop(h)
    grad_h2 = sca.result()
    normed, scale = normalize(mid_ref[...].reshape(own, width))
    gy_own = gy_ref[ring.me].reshape(own, width).astype(F32)
    gmid = gy_own + norm_back(grad_h2, normed, scale, vec_ref[0:1])
    gmid_ref[...] = gmid.reshape(groups, rows, width)
    m_buf[ring.me] = gmid.astype(BF16).reshape(groups, rows, width)
    gat2.hop(0)
    sums_ref[0:1] = jnp.sum(grad_h2 * normed, axis=0, keepdims=True)
    sums_ref[1:2] = jnp.sum(grad_h2, axis=0, keepdims=True)
    sums_ref[2:3] = jnp.sum(gmid, axis=0, keepdims=True)

    def back(chip):
        block = chip_rows(m_buf, chip)
        chip_put_grouped(gatt_ref, chip, dot(block, wo_ref[...], 1, 1))
        return dot(chip_rows_grouped(att_ref, chip), block, 0, 0)

    def flat(ref):
        return ref[...].reshape(shards * own, ref.shape[-1])

    def down_part(chip):
        chip_put(down_ref, chip, dot(chip_rows(act_buf, chip), wd_ref[...]))

    cols = width // parts

    def put_columns(val, at):
        val = val.astype(BF16)
        for i in range(parts):
            gdo_ref[i, at : at + val.shape[0], :cols] = val[:, i * cols : (i + 1) * cols]

    gout = None
    ffr = gdo_ref.shape[1] - (size + 15) // 16 * 16
    for k in range(half):
        if k == 0:
            sums_ref[3:4] = jnp.sum(flat(gy_ref).astype(F32), axis=0, keepdims=True)
            bup_ref[...] = jnp.sum(flat(ghid_buf).astype(F32), axis=0, keepdims=True)
            put_columns(dot(flat(act_buf), flat(gy_ref), 0, 0)[:ffr], 0)
        if k == 1:
            gup = jnp.transpose(dot(flat(ghid_buf), flat(h_buf), 0, 0)).astype(BF16)
            for i in range(shards):
                gup_ref[i, :size] = gup[i * size : (i + 1) * size]
        for chip in gat.blocks(k):
            down_part(chip)
        gat2.hop(k + 1)
        gat2.ready(k)
        for chip in gat2.blocks(k):
            more = back(chip)
            gout = more if gout is None else gout + more
    down_part(ring.at(half, 0))
    gat2.ready(half)
    gout = gout + back(ring.at(half, 0))
    put_columns(gout[: gdo_ref.shape[1] - ffr], ffr)
    for j in range(1, shards):
        att_copy(j).wait_send()
    gat.finish()
    gat2.finish()
    sca.finish()


def middle(shards, size, ff, parts, att, states, gy, vecs, bu, w_out, wo, wu, wd):
    groups, rows, width = states.shape
    ffp, hp = wu.shape[1], wo.shape[0]
    blocks = (shards, groups, rows)
    sds = jax.ShapeDtypeStruct
    r16 = lambda n: -(-n // 16) * 16
    return pl.pallas_call(
        functools.partial(middle_kernel, shards, size, ff, parts),
        out_shape=[
            sds((groups, rows, width), F32), sds((groups, rows, width), F32),
            sds((groups, shards, rows, hp), BF16), sds((shards, r16(size), ffp), BF16),
            sds((parts, r16(ff) + r16(size), up128(width // parts)), BF16), sds(blocks + (width,), BF16),
            sds((8, width), F32), sds((1, ffp), F32),
        ],
        in_specs=[pl.BlockSpec(memory_space=VMEM)] * 9,
        out_specs=[pl.BlockSpec(memory_space=VMEM)] * 8,
        scratch_shapes=[
            VMEM(blocks + (width,), BF16), VMEM(blocks + (width,), BF16), VMEM(blocks + (width,), BF16),
            VMEM(blocks + (ffp,), BF16), VMEM(blocks + (ffp,), BF16), VMEM(blocks + (ffp,), F32),
            VMEM(blocks + (hp,), BF16), VMEM((groups * rows, width), BF16),
            DMA((shards,)), DMA((shards,)), DMA,
        ]
        + gather_sems(shards) * 2
        + scatter_scratch(shards, rows, width),
        name="middle",
        compiler_params=pltpu.CompilerParams(
            collective_id=1, has_side_effects=True, vmem_limit_bytes=60 << 20
        ),
    )(att, states, gy, vecs, bu, w_out, wo, wu, wd)


def last_kernel(
    shards, size, ff, parts,
    dq_ref, dk_ref, dv_ref, x_ref, h_ref, gmid_ref, gup_ref, gdo_ref, sums_ref, bup_ref, vec_ref, w_ref,
    sg_ref, qkv_ref, up_ref, do_ref, small_ref,
    pre_buf, pre_land, mine_buf, qkv_buf, qkv_land, up_land, do_land, vec_buf, vec_land, tiny_land,
    pre_s, pre_r, qkv_s, qkv_r, up_s, up_r, do_s, do_r, vec_s, vec_r, tiny_s, tiny_r, loc,
):
    me = lax.axis_index("seq")
    dp = lax.axis_index("dp")
    groups, rows, width = x_ref.shape
    own = groups * rows
    per = shards // parts
    keeper = me // per
    everyone = [
        ((dp + i) % parts, (me + j) % shards) for i in range(parts) for j in range(shards) if i + j > 0
    ]
    bar = pltpu.get_barrier_semaphore()
    for dev in everyone:
        pl.semaphore_signal(bar, inc=1, device_id=dev, device_id_type=MESH)

    for i, ref in enumerate((dq_ref, dk_ref, dv_ref)):
        for g in range(groups):
            pre_buf[:, g, :, i * size : (i + 1) * size] = ref[g][:, :, :size]
        small = jnp.sum(ref[...].reshape(shards * own, -1).astype(F32), axis=0, keepdims=True)
        if i == 0:
            bias_q = small
        if i == 2:
            bias_v = small
    spare = pre_buf.shape[3] - 3 * size
    pre_buf[:, :, :, 3 * size :] = jnp.zeros((shards, groups, rows, spare), BF16)
    pl.semaphore_wait(bar, len(everyone))

    def send(src, dst, s, r, dev):
        return pltpu.make_async_remote_copy(
            src_ref=src, dst_ref=dst, send_sem=s, recv_sem=r, device_id=dev, device_id_type=MESH
        )

    def pre_copy(j):
        to = (me + j) % shards
        return send(pre_buf.at[to], pre_land.at[me], pre_s.at[j], pre_r.at[me], (dp, to))

    def to_keeper(buf, land, s, r, j, go):
        to = (me + j) % shards
        slot = (me % per) * parts + dp
        copy = lambda: send(buf.at[to], land.at[slot], s.at[j], r.at[slot], (keeper, to))
        if j > 0:
            go(copy())
            return

        @pl.when(keeper != dp)
        def _():
            go(copy())

    def from_keepers(buf, land, r, s):
        for i in range(per):
            for x in range(parts):
                slot = i * parts + x
                frm = dp * per + i
                wait = lambda: send(buf.at[0], land.at[slot], s.at[0], r.at[slot], (x, frm)).wait_recv()
                away = (frm != me).astype(jnp.int32) + (dp != x).astype(jnp.int32)
                pl.when(away > 0)(wait)

    def keep_own(buf, land, sem):
        @pl.when(keeper == dp)
        def _():
            c = pltpu.make_async_copy(buf.at[me], land.at[(me % per) * parts + dp], sem)
            c.start()
            c.wait()

    def do_copy(i):
        to = (dp + i) % parts
        return send(gdo_ref.at[to], do_land.at[dp], do_s.at[i], do_r.at[dp], (to, me))

    def do_wait(i):
        frm = (dp + i) % parts
        send(gdo_ref.at[frm], do_land.at[frm], do_s.at[i], do_r.at[frm], (frm, me)).wait_recv()

    start = lambda c: c.start()
    done = lambda c: c.wait_send()
    for j in range(1, shards):
        pre_copy(j).start()
    pre_land[me] = pre_buf[me]
    for i in range(1, parts):
        do_copy(i).start()
    for j in range(shards):
        to_keeper(gup_ref, up_land, up_s, up_r, j, start)
    tokens = shards * own
    gqkv = dot(pre_buf[...].reshape(tokens, -1), h_ref[...].reshape(tokens, width), 0, 0)
    gqkv = jnp.transpose(gqkv).astype(BF16)
    for i in range(shards):
        qkv_buf[i, :size] = gqkv[i * size : (i + 1) * size]
    for j in range(shards):
        to_keeper(qkv_buf, qkv_land, qkv_s, qkv_r, j, start)
    for j in range(1, shards):
        frm = (me + shards - j) % shards
        send(pre_buf.at[frm], pre_land.at[frm], pre_s.at[j], pre_r.at[frm], (dp, frm)).wait_recv()
    for h in range(shards):
        block = pre_land[h].reshape(own, -1)
        for c in range(3):
            at = c * width + h * size
            mine_buf[:, at : at + size] = block[:, c * size : (c + 1) * size]
    grad_h1 = dot(mine_buf[:, :width], w_ref[0], 1, 1)
    for c in range(1, 3):
        grad_h1 = grad_h1 + dot(mine_buf[:, c * width : (c + 1) * width], w_ref[c], 1, 1)
    normed, scale = normalize(x_ref[...].reshape(own, width).astype(F32))
    sg = gmid_ref[...].reshape(own, width) + norm_back(grad_h1, normed, scale, vec_ref[0:1])
    sg_ref[...] = sg.reshape(groups, rows, width).astype(BF16)
    gain = jnp.sum(grad_h1 * normed, axis=0, keepdims=True)
    shift = jnp.sum(grad_h1, axis=0, keepdims=True)
    vecs = jnp.concatenate(
        [gain, sums_ref[0:1], shift, sums_ref[1:2], sums_ref[2:3], sums_ref[3:4], gain, gain], axis=0
    )
    for i in range(shards):
        vec_buf[i, :, :size] = vecs[:, i * size : (i + 1) * size]
    for j in range(shards):
        to_keeper(vec_buf, vec_land, vec_s, vec_r, j, start)
    keep_own(vec_buf, vec_land, loc)

    for i in range(1, parts):
        do_wait(i)
    do_land[dp] = gdo_ref[dp]
    total = do_land[0].astype(F32)
    for i in range(1, parts):
        total = total + do_land[i].astype(F32)
    do_ref[...] = total
    keep_own(gup_ref, up_land, loc)
    keep_own(qkv_buf, qkv_land, loc)
    from_keepers(gup_ref, up_land, up_r, up_s)
    for i in range(per):
        total = up_land[i * parts].astype(F32)
        for x in range(1, parts):
            total = total + up_land[i * parts + x].astype(F32)
        up_ref[:, i * ff : (i + 1) * ff] = total[:size, :ff]
    from_keepers(vec_buf, vec_land, vec_r, vec_s)
    total = vec_land[0]
    for i in range(1, shards):
        total = total + vec_land[i]
    tiny_land[dp, 0:5] = total[0:5]
    tiny_land[dp, 5:6] = bias_q
    tiny_land[dp, 6:7] = bias_v
    tiny_land[dp, 7:8] = vec_buf[me][5:6]
    for i in range(bup_ref.shape[1] // 128):
        tiny_land[dp, 8 + i : 9 + i] = bup_ref[:, i * 128 : (i + 1) * 128]

    def tiny(i):
        to = (dp + i) % parts
        return send(tiny_land.at[dp], tiny_land.at[dp], tiny_s.at[i], tiny_r.at[dp], (to, me))

    for i in range(1, parts):
        tiny(i).start()
    from_keepers(qkv_buf, qkv_land, qkv_r, qkv_s)
    for i in range(per):
        total = qkv_land[i * parts].astype(F32)
        for x in range(1, parts):
            total = total + qkv_land[i * parts + x].astype(F32)
        for c in range(3):
            qkv_ref[c, :, i * size : (i + 1) * size] = total[:size, c * size : (c + 1) * size]
    for i in range(1, parts):
        frm = (dp + i) % parts
        send(tiny_land.at[frm], tiny_land.at[frm], tiny_s.at[i], tiny_r.at[frm], (frm, me)).wait_recv()
    total = tiny_land[0]
    for i in range(1, parts):
        total = total + tiny_land[i]
    small_ref[...] = total
    for j in range(1, shards):
        pre_copy(j).wait_send()
    for i in range(1, parts):
        do_copy(i).wait_send()
        tiny(i).wait_send()
    for j in range(shards):
        to_keeper(gup_ref, up_land, up_s, up_r, j, done)
        to_keeper(qkv_buf, qkv_land, qkv_s, qkv_r, j, done)
        to_keeper(vec_buf, vec_land, vec_s, vec_r, j, done)


def last(shards, size, ff, parts, dq, dk, dv, states, h1, gmid, gup, gdo, sums, bup, vecs, w_qkv):
    groups, rows, width = states.shape
    per = shards // parts
    wp = up128(3 * size)
    sds = jax.ShapeDtypeStruct
    tiny = 8 + bup.shape[1] // 128
    return pl.pallas_call(
        functools.partial(last_kernel, shards, size, ff, parts),
        out_shape=[
            sds((groups, rows, width), BF16), sds((3, size, per * size), F32), sds((size, per * ff), F32),
            sds(gdo.shape[1:], F32), sds((tiny, 128), F32),
        ],
        in_specs=[pl.BlockSpec(memory_space=VMEM)] * 12,
        out_specs=[pl.BlockSpec(memory_space=VMEM)] * 5,
        scratch_shapes=[
            VMEM((shards, groups, rows, wp), BF16), VMEM((shards, groups, rows, wp), BF16),
            VMEM((groups * rows, 3 * width), BF16),
            VMEM((shards,) + gup.shape[1:2] + (wp,), BF16), VMEM((shards,) + gup.shape[1:2] + (wp,), BF16),
            VMEM(gup.shape, BF16), VMEM(gdo.shape, BF16),
            VMEM((shards, 8, 128), F32), VMEM((shards, 8, 128), F32), VMEM((parts, tiny, 128), F32),
        ]
        + [DMA((shards,))] * 6 + [DMA((parts,))] * 2 + [DMA((shards,))] * 2 + [DMA((parts,))] * 2 + [DMA],
        name="last",
        compiler_params=pltpu.CompilerParams(
            collective_id=2, has_side_effects=True, vmem_limit_bytes=48 << 20
        ),
    )(dq, dk, dv, states, h1, gmid, gup, gdo, sums, bup, vecs, w_qkv)


def body(
    states, counts, cotangent, w_qkv, w_out, attn_bias, norm_gain, norm_bias,
    w_up, up_bias, w_down, down_bias,
):
    groups, rows, width = states.shape
    shards = lax.axis_size("seq")
    parts = lax.axis_size("dp")
    me = lax.axis_index("seq")
    size = width // HEADS
    sp = up128(size)
    ff = w_up.shape[1] // shards
    ffp = up128(ff)
    total = rows * shards
    factor = 1.0 / math.sqrt(size)
    ends = jnp.cumsum(counts, axis=1)
    ids = jnp.sum(
        (jnp.arange(total, dtype=jnp.int32)[None, :, None] >= ends[:, None, :]).astype(jnp.int32), axis=2
    )
    valid_all = (ids < counts.shape[1]).astype(F32)[..., None]
    valid = lax.dynamic_slice_in_dim(valid_all, me * rows, rows, 1)
    same = ids[:, :, None] == ids[:, None, :]

    def mine(x, axis, count):
        return lax.dynamic_slice_in_dim(x, me * count, count, axis)

    wq = pad_to(mine(w_qkv, 2, size), 2, sp)
    wq = jnp.transpose(wq, (1, 0, 2)).reshape(width, 3 * sp)
    wo = pad_to(mine(w_out, 0, size), 0, sp)
    wu = pad_to(mine(w_up, 1, ff), 1, ffp)
    wd = pad_to(mine(w_down, 0, ff), 0, ffp)
    bq = pad_to(mine(attn_bias, 1, size), 1, sp)
    bu = pad_to(mine(up_bias, 0, ff), 0, ffp)[None]
    consts = jnp.stack(
        [
            jnp.concatenate([bq[0], jnp.zeros_like(bq[0]), bq[1]]),
            jnp.concatenate([jnp.full((sp,), factor, F32), jnp.ones((2 * sp,), F32)]),
        ]
    )

    h1, query, key, value = first(shards, states, jnp.stack([norm_gain[0], norm_bias[0]]), wq, consts)
    grad_y = (cotangent.astype(F32) * valid).astype(BF16)
    gy = lax.all_gather(grad_y, "seq", axis=0)

    query, key, value = (x.reshape(groups, total, sp) for x in (query, key, value))
    scores = jnp.where(same, mm("gqd,gkd->gqk", query, key), NEG)
    highest = jnp.max(scores, axis=-1, keepdims=True)
    weights = jnp.exp(scores - highest)
    totals = jnp.sum(weights, axis=-1, keepdims=True)
    attended = mm("gqk,gkd->gqd", weights.astype(BF16), value) / totals
    lse = highest + jnp.log(totals)
    att_b = attended.astype(BF16).reshape(groups, shards, rows, sp)

    mid, grad_mid, grad_att, grad_up, gdo, down_part, sums, up_sums = middle(
        shards, size, ff, parts, att_b, states, gy,
        jnp.stack([norm_gain[1], norm_bias[1], attn_bias[2]]), bu, w_out, wo, wu, wd,
    )
    down = lax.psum_scatter(down_part, "seq", scatter_dimension=0, tiled=False).astype(F32)
    grad_att = grad_att.reshape(groups, total, sp)

    delta = jnp.sum(grad_att.astype(F32) * attended, axis=-1, keepdims=True)
    scores2 = jnp.where(same, mm("gqd,gkd->gqk", query, key), NEG)
    probs = jnp.exp(scores2 - lse)
    grad_scores = (probs * (mm("gqd,gkd->gqk", grad_att, value) - delta)).astype(BF16)
    pre = (
        (mm("gqk,gkd->gqd", grad_scores, key) * factor).astype(BF16),
        mm("gqk,gqd->gkd", grad_scores, query).astype(BF16),
        mm("gqk,gqd->gkd", probs.astype(BF16), grad_att).astype(BF16),
    )
    state_grad, g_qkv, g_up, g_do, small = last(
        shards, size, ff, parts, *(x.reshape(groups, shards, rows, sp) for x in pre),
        states, h1, grad_mid, grad_up, gdo, sums, up_sums, norm_gain, w_qkv,
    )
    layer_out = ((mid + down + down_bias) * valid).astype(BF16)
    cols = width // parts
    ffr = -(-ff // 16) * 16
    return (
        layer_out,
        state_grad,
        g_qkv,
        g_do[ffr : ffr + size, :cols],
        jnp.stack([small[5], small[6], small[4]])[:, :size],
        small[0:2, :size],
        small[2:4, :size],
        g_up,
        small[8:].reshape(-1)[:ff],
        g_do[:ff, :cols],
        small[7, :size],
    )


def solution(mesh):
    placed = (P("dp", "seq", None), P("dp", None), P("dp", "seq", None)) + (P(),) * 9
    return jax.shard_map(
        body,
        mesh=mesh,
        in_specs=placed,
        out_specs=(
            P("dp", "seq", None), P("dp", "seq", None), P(None, "seq", "dp"), P("seq", "dp"),
            P(None, "seq"), P(None, "seq"), P(None, "seq"), P("seq", "dp"), P("seq"),
            P("seq", "dp"), P("seq"),
        ),
        check_vma=False,
    )
```

```python
import functools
import math

import jax
import jax.numpy as jnp
from jax import lax
from jax.experimental import pallas as pl
from jax.experimental.pallas import tpu as pltpu
from jax.sharding import PartitionSpec as P

HEADS = 16
EPS = 1e-06
NEG = -1e30
F32 = jnp.float32
BF16 = jnp.bfloat16
MESH = pl.DeviceIdType.MESH
VMEM = pltpu.VMEM
DMA = pltpu.SemaphoreType.DMA


def mm(spec, a, b):
    return jnp.einsum(spec, a, b, preferred_element_type=F32)


def dot(a, b, ca=1, cb=0):
    return lax.dot_general(a, b, (((ca,), (cb,)), ((), ())), preferred_element_type=F32)


def pad_to(x, axis, size):
    pads = [(0, 0)] * x.ndim
    pads[axis] = (0, size - x.shape[axis])
    return jnp.pad(x, pads)


def up128(n):
    return -(-n // 128) * 128


def normalize(values):
    mean = jnp.mean(values, axis=-1, keepdims=True)
    centred = values - mean
    scale = lax.rsqrt(jnp.mean(centred * centred, axis=-1, keepdims=True) + EPS)
    return (centred * scale, scale)


def norm_back(grad_norm, normed, scale, gain):
    scaled = grad_norm * gain
    return scale * (
        scaled
        - jnp.mean(scaled, axis=-1, keepdims=True)
        - normed * jnp.mean(scaled * normed, axis=-1, keepdims=True)
    )


def gelu_both(v):
    c, a = 0.7978845608028654, 0.044715
    sq = v * v
    t = jnp.tanh(c * (v + a * v * sq))
    half = 0.5 * (1.0 + t)
    return v * half, half + 0.5 * v * (1.0 - t * t) * (c * (1.0 + 3.0 * a * sq))


class Ring:
    def __init__(self, shards):
        self.n = shards // 2
        self.half = self.n // 2
        self.me = lax.axis_index("seq")
        self.chip = self.me // 2
        self.core = self.me % 2
        odd = self.chip % 2
        self.pos = (1 - odd) * (self.chip // 2) + odd * (self.n - 1 - self.chip // 2)
        self.to = (self.at(1, 1) * 2 + self.core, self.at(1, 0) * 2 + self.core)
        self.sib = self.chip * 2 + 1 - self.core

    def at(self, k, d):
        p = (self.pos + (self.n - k if d == 0 else k)) % self.n
        hi = p // self.half
        return (1 - hi) * 2 * p + hi * (2 * (self.n - 1 - p) + 1)

    def greet(self, everyone=False):
        bar = pltpu.get_barrier_semaphore()
        others = self.to + (self.sib,)
        if everyone:
            others = [(self.me + j) % (2 * self.n) for j in range(1, 2 * self.n)]
        for d in others:
            pl.semaphore_signal(bar, inc=1, device_id={"seq": d}, device_id_type=MESH)
        self.greeted = len(others)

    def met(self):
        pl.semaphore_wait(pltpu.get_barrier_semaphore(), self.greeted)


def gather_sems(shards):
    return [DMA((2, shards // 4 + 1, 2))] * 4


class Gather:
    def __init__(self, ring, buf, sems):
        self.ring, self.buf = ring, buf
        self.ring_s, self.ring_r, self.sib_s, self.sib_r = sems
        self.sent = []

    def copy(self, k, d, g, to_sib):
        block = self.buf.at[self.ring.at(k, d) * 2 + self.ring.core, g]
        s, r = (self.sib_s, self.sib_r) if to_sib else (self.ring_s, self.ring_r)
        return pltpu.make_async_remote_copy(
            src_ref=block, dst_ref=block, send_sem=s.at[d, k, g], recv_sem=r.at[d, k, g],
            device_id={"seq": self.ring.sib if to_sib else self.ring.to[d]}, device_id_type=MESH,
        )

    def units(self, k):
        if k == self.ring.half:
            return [(0, 0), (1, 1)]
        return [(0, 0), (1, 1), (0, 1), (1, 0)]

    def hop(self, k):
        half = self.ring.half
        for d, g in self.units(k):
            if k > 0:
                self.copy(k - 1, d, g, False).wait_recv()
            if k < half - 1 or (k == half - 1 and g == d):
                c = self.copy(k, d, g, False)
                c.start()
                self.sent.append(c)
        for d, g in self.units(k):
            if k > 0 or d == g:
                c = self.copy(k, d, g, True)
                c.start()
                self.sent.append(c)

    def ready(self, k):
        for d, g in self.units(k):
            if k > 0 or d == g:
                self.copy(k, d, g, True).wait_recv()

    def blocks(self, k):
        if k == 0 or k == self.ring.half:
            return [self.ring.at(k, 0)]
        return [self.ring.at(k, 0), self.ring.at(k, 1)]

    def finish(self):
        for c in self.sent:
            c.wait_send()


def scatter_scratch(shards, rows, width):
    n = shards // 2
    return [
        VMEM((n, 2, rows, width), BF16), VMEM((2, n // 2, 2, rows, width), BF16),
        DMA((n,)), DMA((n,)), DMA((2, n // 2, 2)), DMA((2, n // 2, 2)),
    ]


class Scatter:
    def __init__(self, ring, part, scratch):
        self.ring, self.part = ring, part
        self.sib_land, self.land, self.sib_s, self.sib_r, self.ring_s, self.ring_r = scratch
        self.sent = []
        self.have = set()

    def slot(self, k, d):
        if k == 0:
            return 0
        return self.ring.n - 1 if k == self.ring.half else 2 * k - 1 + d

    def sib_copy(self, k, d):
        r, i = self.ring, self.slot(k, d)
        return pltpu.make_async_remote_copy(
            src_ref=self.part.at[r.at(k, d) * 2 + 1 - r.core], dst_ref=self.sib_land.at[i],
            send_sem=self.sib_s.at[i], recv_sem=self.sib_r.at[i],
            device_id={"seq": r.sib}, device_id_type=MESH,
        )

    def give(self, k, d):
        c = self.sib_copy(k, d)
        c.start()
        self.sent.append(c)

    def from_sib(self, k, d):
        i = self.slot(k, d)
        if i not in self.have:
            self.have.add(i)
            self.sib_copy(k, d).wait_recv()
        return self.sib_land.at[i]

    def steps(self):
        return self.ring.half

    def dist(self, h, d, g):
        return self.ring.half - h if g == d else self.ring.half - 1 - h

    def ring_copy(self, h, d, g):
        r = self.ring
        return pltpu.make_async_remote_copy(
            src_ref=self.part.at[r.at(self.dist(h, d, g), 1 - d) * 2 + r.core, g], dst_ref=self.land.at[d, h, g],
            send_sem=self.ring_s.at[d, h, g], recv_sem=self.ring_r.at[d, h, g],
            device_id={"seq": r.to[d]}, device_id_type=MESH,
        )

    def hop(self, h):
        r = self.ring
        for d, g in [(0, 0), (1, 1), (0, 1), (1, 0)]:
            j = self.dist(h, d, g)
            if j == 0:
                continue
            own = r.at(j, 1 - d) * 2 + r.core
            val = self.part[own, g].astype(F32) + self.from_sib(j, 1 - d)[g].astype(F32)
            if h > 0:
                self.ring_copy(h - 1, d, g).wait_recv()
                val = val + self.land[d, h - 1, g].astype(F32)
            self.part[own, g] = val.astype(BF16)
            c = self.ring_copy(h, d, g)
            c.start()
            self.sent.append(c)

    def result(self):
        r = self.ring
        out = []
        for g in range(2):
            val = self.part[r.me, g].astype(F32) + self.from_sib(0, 0)[g].astype(F32)
            for d in range(2):
                h = r.half - 1 if g == d else r.half - 2
                self.ring_copy(h, d, g).wait_recv()
                val = val + self.land[d, h, g].astype(F32)
            out.append(val)
        return jnp.concatenate(out, axis=0)

    def finish(self):
        for c in self.sent:
            c.wait_send()


def chip_rows(ref, chip):
    val = ref[pl.ds(2 * chip, 2)]
    return val.reshape(-1, val.shape[-1])


def chip_put(ref, chip, val):
    ref[pl.ds(2 * chip, 2)] = val.astype(ref.dtype).reshape((2,) + ref.shape[1:])


def chip_put_grouped(ref, chip, val):
    rows = ref.shape[2]
    val = val.astype(ref.dtype)
    for i in range(2):
        for g in range(2):
            at = (2 * i + g) * rows
            ref[g, 2 * chip + i] = val[at : at + rows]


def chip_rows_grouped(ref, chip):
    return jnp.concatenate([ref[g, 2 * chip + i] for i in range(2) for g in range(2)], axis=0)


def send(src, dst, s, r, dev):
    return pltpu.make_async_remote_copy(
        src_ref=src, dst_ref=dst, send_sem=s, recv_sem=r, device_id=dev, device_id_type=MESH
    )


def ends_of(counts_ref, g):
    out = [counts_ref[g, 0]]
    for i in range(1, counts_ref.shape[1]):
        out.append(out[-1] + counts_ref[g, i])
    return out


def ids_at(positions, ends):
    total = (positions >= ends[0]).astype(jnp.int32)
    for end in ends[1:]:
        total = total + (positions >= end).astype(jnp.int32)
    return total


def valid_rows(counts_ref, me, groups, rows):
    at = lax.broadcasted_iota(jnp.int32, (rows, 1), 0) + me * rows
    return jnp.concatenate(
        [(at < ends_of(counts_ref, g)[-1]).astype(F32) for g in range(groups)], axis=0
    )


QB = 256


def front_kernel(
    shards, size, ff, parts,
    counts_ref, x_ref, ct_ref, gain_ref, nbias_ref, abias_ref, wq_ref, bq_ref, wout_ref, wo_ref, wu_ref, wd_ref, bu_ref,
    h_ref, q_ref, k_ref, v_ref, att_ref, lse_ref,
    mid_ref, gmid_ref, gatt_ref, gup_ref, gdo_ref, down_ref, sums_ref, bup_ref,
    gy_buf, h_buf, m_buf, part, act_buf, ghid_buf, att_b, att_land, att_buf,
    wq_buf, wu_buf, wd_buf, wo_buf, att_s, att_r, *rest,
):
    ring = Ring(shards)
    ring.greet(True)
    me = ring.me
    groups, rows, width = x_ref.shape
    own = groups * rows
    sp = q_ref.shape[3]
    total = shards * rows
    factor = 1.0 / math.sqrt(size)
    gat1 = Gather(ring, h_ref, rest[0:4])
    gaty = Gather(ring, gy_buf, rest[4:8])
    gat = Gather(ring, h_buf, rest[8:12])
    gat2 = Gather(ring, m_buf, rest[12:16])
    sca = Scatter(ring, part, rest[16:22])
    half = ring.half

    inputs = x_ref[...].reshape(own, width).astype(F32)
    normed, _ = normalize(inputs)
    h_ref[me] = (normed * gain_ref[0:1] + nbias_ref[0:1]).astype(BF16).reshape(groups, rows, width)
    ring.met()
    gat1.hop(0)
    grad_y = ct_ref[...].reshape(own, width).astype(F32) * valid_rows(counts_ref, me, groups, rows)
    gy_buf[me] = grad_y.astype(BF16).reshape(groups, rows, width)
    wq_buf[...] = jnp.zeros(wq_buf.shape, BF16)
    for c in range(3):
        wq_buf[:, c * sp : c * sp + size] = wq_ref[c]

    def project(chip):
        out = dot(chip_rows(h_ref, chip), wq_buf[...])
        for i, ref in enumerate((q_ref, k_ref, v_ref)):
            val = out[:, i * sp : (i + 1) * sp]
            if i != 1:
                val = val + bq_ref[i // 2 : i // 2 + 1]
            if i == 0:
                val = val * factor
            chip_put_grouped(ref, chip, val)

    for k in range(1, half + 1):
        gat1.ready(k - 1)
        for chip in gat1.blocks(k - 1):
            project(chip)
        gat1.hop(k)
        if k == half - 1:
            gaty.hop(0)
        if k == 1:
            wu_buf[...] = jnp.zeros(wu_buf.shape, BF16)
            wu_buf[:, :ff] = wu_ref[...]
            wd_buf[...] = jnp.zeros(wd_buf.shape, BF16)
            wd_buf[:ff] = wd_ref[...]
            wo_buf[...] = jnp.zeros(wo_buf.shape, BF16)
            wo_buf[:size] = wo_ref[...]
    gat1.ready(half)
    project(ring.at(half, 0))

    per = QB // rows

    def att_copy(g, to):
        return send(att_b.at[g, to], att_land.at[me, g], att_s.at[g, to], att_r.at[g, me], {"seq": to})

    for g in range(groups):
        ends = ends_of(counts_ref, g)
        key_ids = ids_at(lax.broadcasted_iota(jnp.int32, (1, total), 1), ends)

        @pl.loop(0, total // QB)
        def _(i):
            query = q_ref[g, pl.ds(i * per, per)].reshape(QB, sp)
            query_ids = ids_at(lax.broadcasted_iota(jnp.int32, (QB, 1), 0) + i * QB, ends)
            scores = dot(query, k_ref[g].reshape(total, sp), 1, 1)
            scores = jnp.where(query_ids == key_ids, scores, NEG)
            high = jnp.max(scores, axis=-1, keepdims=True)
            weights = jnp.exp(scores - high)
            sums = jnp.sum(weights, axis=-1, keepdims=True)
            out = dot(weights.astype(BF16), v_ref[g].reshape(total, sp)) / sums
            att_ref[g, pl.ds(i * per, per)] = out.reshape(per, rows, sp)
            att_b[g, pl.ds(i * per, per)] = out.astype(BF16).reshape(per, rows, sp)
            lse = jnp.broadcast_to(high + jnp.log(sums), (QB, 128))
            lse_ref[g, i] = jnp.transpose(lse)[0:8]
            for t in range(per):
                to = i * per + t

                @pl.when(to != me)
                def _():
                    att_copy(g, to).start()

        gaty.hop(1 + g)
    att_land[me] = att_b[:, me]
    gaty.hop(3)
    for j in range(1, shards):
        frm = (me + shards - j) % shards
        for g in range(groups):
            send(att_b.at[g, frm], att_land.at[frm, g], att_s.at[g, frm], att_r.at[g, frm], {"seq": frm}).wait_recv()
    for h in range(shards):
        att_buf[:, h * size : (h + 1) * size] = att_land[h].reshape(own, -1)[:, :size]
    mid = inputs + dot(att_buf[...], wout_ref[...]) + abias_ref[2:3]
    mid_ref[...] = mid.reshape(groups, rows, width)
    normed, scale = normalize(mid)
    h_buf[me] = (normed * gain_ref[1:2] + nbias_ref[1:2]).astype(BF16).reshape(groups, rows, width)
    gat.hop(0)
    gaty.hop(half)

    def forward(chip):
        hidden = dot(chip_rows(h_buf, chip), wu_buf[...]) + bu_ref[...]
        act, slope = gelu_both(hidden)
        chip_put(act_buf, chip, act)
        ghid = (dot(chip_rows(gy_buf, chip), wd_buf[...], 1, 1) * slope).astype(BF16)
        chip_put(ghid_buf, chip, ghid)
        chip_put(part, chip, dot(ghid, wu_buf[...], 1, 1))

    for k in range(half):
        gaty.ready(k)
        gat.ready(k)
        for d, chip in enumerate(gat.blocks(k)):
            forward(chip)
            sca.give(k, d)
        gat.hop(k + 1)
    gaty.ready(half)
    gat.ready(half)
    forward(ring.at(half, 0))
    sca.give(half, 0)
    for h in range(half):
        sca.hop(h)
    grad_h2 = sca.result()
    normed, scale = normalize(mid_ref[...].reshape(own, width))
    gmid = gy_buf[me].reshape(own, width).astype(F32) + norm_back(grad_h2, normed, scale, gain_ref[1:2])
    gmid_ref[...] = gmid.reshape(groups, rows, width)
    m_buf[me] = gmid.astype(BF16).reshape(groups, rows, width)
    gat2.hop(0)
    sums_ref[0:1] = jnp.sum(grad_h2 * normed, axis=0, keepdims=True)
    sums_ref[1:2] = jnp.sum(grad_h2, axis=0, keepdims=True)
    sums_ref[2:3] = jnp.sum(gmid, axis=0, keepdims=True)

    def back(chip):
        block = chip_rows(m_buf, chip)
        chip_put_grouped(gatt_ref, chip, dot(block, wo_buf[...], 1, 1))
        return dot(chip_rows_grouped(att_b, chip), block, 0, 0)

    def flat(ref):
        return ref[...].reshape(shards * own, ref.shape[-1])

    def down_part(chip):
        chip_put(down_ref, chip, dot(chip_rows(act_buf, chip), wd_buf[...]))

    cols = width // parts

    def put_columns(val, at):
        val = val.astype(BF16)
        for i in range(parts):
            gdo_ref[i, at : at + val.shape[0], :cols] = val[:, i * cols : (i + 1) * cols]

    gout = None
    ffr = gdo_ref.shape[1] - (size + 15) // 16 * 16
    for k in range(half):
        if k == 0:
            sums_ref[3:4] = jnp.sum(flat(gy_buf).astype(F32), axis=0, keepdims=True)
            bup_ref[...] = jnp.sum(flat(ghid_buf).astype(F32), axis=0, keepdims=True)
            put_columns(dot(flat(act_buf), flat(gy_buf), 0, 0)[:ffr], 0)
        if k == 1:
            gup = jnp.transpose(dot(flat(ghid_buf), flat(h_buf), 0, 0)).astype(BF16)
            for i in range(shards):
                gup_ref[i, :size] = gup[i * size : (i + 1) * size]
        for chip in gat.blocks(k):
            down_part(chip)
        gat2.hop(k + 1)
        gat2.ready(k)
        for chip in gat2.blocks(k):
            more = back(chip)
            gout = more if gout is None else gout + more
    down_part(ring.at(half, 0))
    gat2.ready(half)
    gout = gout + back(ring.at(half, 0))
    put_columns(gout[: gdo_ref.shape[1] - ffr], ffr)
    for j in range(1, shards):
        for g in range(groups):
            att_copy(g, (me + j) % shards).wait_send()
    for x in (gat1, gaty, gat, gat2, sca):
        x.finish()


def front(shards, size, ff, parts, counts, states, cotangent, gains, nbias, abias, wq, bq, w_out, wo, wu, wd, bu):
    groups, rows, width = states.shape
    ffp, sp = up128(ff), up128(size)
    blocks = (shards, groups, rows)
    grouped = (groups, shards, rows)
    sds = jax.ShapeDtypeStruct
    r16 = lambda n: -(-n // 16) * 16
    return pl.pallas_call(
        functools.partial(front_kernel, shards, size, ff, parts),
        out_shape=[
            sds(blocks + (width,), BF16), sds(grouped + (sp,), BF16), sds(grouped + (sp,), BF16),
            sds(grouped + (sp,), BF16), sds(grouped + (sp,), F32), sds((groups, shards * rows // QB, 8, QB), F32),
            sds((groups, rows, width), F32), sds((groups, rows, width), F32),
            sds(grouped + (sp,), BF16), sds((shards, r16(size), ffp), BF16),
            sds((parts, r16(ff) + r16(size), up128(width // parts)), BF16), sds(blocks + (width,), BF16),
            sds((8, width), F32), sds((1, ffp), F32),
        ],
        in_specs=[pl.BlockSpec(memory_space=pltpu.SMEM)] + [pl.BlockSpec(memory_space=VMEM)] * 12,
        out_specs=[pl.BlockSpec(memory_space=VMEM)] * 14,
        scratch_shapes=[VMEM(blocks + (width,), BF16)] * 4
        + [
            VMEM(blocks + (ffp,), BF16), VMEM(blocks + (ffp,), BF16),
            VMEM(grouped + (sp,), BF16), VMEM(blocks + (sp,), BF16), VMEM((groups * rows, width), BF16),
            VMEM((width, 3 * sp), BF16), VMEM((width, ffp), BF16), VMEM((ffp, width), BF16), VMEM((sp, width), BF16),
            DMA((groups, shards)), DMA((groups, shards)),
        ]
        + gather_sems(shards) * 4
        + scatter_scratch(shards, rows, width),
        name="front",
        compiler_params=pltpu.CompilerParams(
            collective_id=0, has_side_effects=True, vmem_limit_bytes=62 << 20
        ),
    )(counts, states, cotangent, gains, nbias, abias, wq, bq, w_out, wo, wu, wd, bu)


def rear_kernel(
    shards, size, ff, parts,
    counts_ref, q_ref, k_ref, v_ref, gatt_ref, att_ref, lse_ref, x_ref, mid_ref, gmid_ref, gup_ref, gdo_ref,
    sums_ref, bup_ref, gain_ref, dbias_ref, h_hbm, down_hbm, w_hbm,
    out_ref, sg_ref, qkv_ref, gout_ref, gab_ref, ggain_ref, gshift_ref, up_ref, gub_ref, gdown_ref, gdb_ref,
    h_buf, part, w_buf, dk_acc, dv_acc,
    pre_buf, pre_land, mine_buf, qkv_buf, qkv_land, up_land, do_land, vec_buf, vec_land, tiny_land,
    pre_s, pre_r, qkv_s, qkv_r, up_s, up_r, do_s, do_r, vec_s, vec_r, tiny_s, tiny_r, loc, *rest,
):
    ring = Ring(shards)
    me = ring.me
    dp = lax.axis_index("dp")
    groups, rows, width = x_ref.shape
    own = groups * rows
    sp = q_ref.shape[3]
    total = shards * rows
    tokens = shards * own
    factor = 1.0 / math.sqrt(size)
    half = ring.half
    sca = Scatter(ring, part, rest)
    load_part = pltpu.make_async_copy(down_hbm, part, loc.at[0])
    load_h = pltpu.make_async_copy(h_hbm, h_buf, loc.at[1])
    load_w = pltpu.make_async_copy(w_hbm, w_buf, loc.at[2])
    load_part.start()
    load_h.start()
    load_w.start()
    per = shards // parts
    keeper = me // per
    everyone = [
        ((dp + i) % parts, (me + j) % shards) for i in range(parts) for j in range(shards) if i + j > 0
    ]
    bar = pltpu.get_barrier_semaphore()
    for dev in everyone:
        pl.semaphore_signal(bar, inc=1, device_id=dev, device_id_type=MESH)
    spare = pre_buf.shape[3] - 3 * size
    pre_buf[:, :, :, 3 * size :] = jnp.zeros((shards, groups, rows, spare), BF16)
    load_part.wait()
    pl.semaphore_wait(bar, len(everyone))

    def to_keeper(buf, land, s, r, j, go):
        to = (me + j) % shards
        slot = (me % per) * parts + dp
        copy = lambda: send(buf.at[to], land.at[slot], s.at[j], r.at[slot], (keeper, to))
        if j > 0:
            go(copy())
            return

        @pl.when(keeper != dp)
        def _():
            go(copy())

    def from_keepers(buf, land, r, s):
        for i in range(per):
            for x in range(parts):
                slot = i * parts + x
                frm = dp * per + i
                wait = lambda: send(buf.at[0], land.at[slot], s.at[0], r.at[slot], (x, frm)).wait_recv()
                away = (frm != me).astype(jnp.int32) + (dp != x).astype(jnp.int32)
                pl.when(away > 0)(wait)

    def keep_own(buf, land):
        @pl.when(keeper == dp)
        def _():
            c = pltpu.make_async_copy(buf.at[me], land.at[(me % per) * parts + dp], loc.at[3])
            c.start()
            c.wait()

    def do_copy(i):
        to = (dp + i) % parts
        return send(gdo_ref.at[to], do_land.at[dp], do_s.at[i], do_r.at[dp], (to, me))

    def do_wait(i):
        frm = (dp + i) % parts
        send(gdo_ref.at[frm], do_land.at[frm], do_s.at[i], do_r.at[frm], (frm, me)).wait_recv()

    def pre_copy(j, g):
        to = (me + j) % shards
        return send(pre_buf.at[to, g], pre_land.at[me, g], pre_s.at[g, j], pre_r.at[g, me], (dp, to))

    start = lambda c: c.start()
    done = lambda c: c.wait_send()
    for k in range(half + 1):
        for d in range(1 if k in (0, half) else 2):
            sca.give(k, d)
    sca.hop(0)
    for i in range(1, parts):
        do_copy(i).start()

    qn = QB // rows
    hops = 1
    bias_q = bias_v = None
    for g in range(groups):
        ends = ends_of(counts_ref, g)
        key_ids = ids_at(lax.broadcasted_iota(jnp.int32, (total, 1), 0), ends)
        dk_acc[...] = jnp.zeros(dk_acc.shape, F32)
        dv_acc[...] = jnp.zeros(dv_acc.shape, F32)

        def attend(i):
            query = q_ref[g, pl.ds(i * qn, qn)].reshape(QB, sp)
            grad = gatt_ref[g, pl.ds(i * qn, qn)].reshape(QB, sp)
            keys = k_ref[g].reshape(total, sp)
            att = att_ref[g, pl.ds(i * qn, qn)].reshape(QB, sp)
            delta = jnp.sum(grad.astype(F32) * att, axis=-1, keepdims=True)
            delta = jnp.transpose(jnp.broadcast_to(delta, (QB, 128)))[0:1]
            query_ids = ids_at(lax.broadcasted_iota(jnp.int32, (1, QB), 1) + i * QB, ends)
            scores = dot(keys, query, 1, 1)
            probs = jnp.exp(jnp.where(key_ids == query_ids, scores, NEG) - lse_ref[g, i][0:1])
            grad_probs = dot(v_ref[g].reshape(total, sp), grad, 1, 1)
            grad_scores = (probs * (grad_probs - delta)).astype(BF16)
            dv_acc[...] += dot(probs.astype(BF16), grad)
            dk_acc[...] += dot(grad_scores, query)
            dq = (dot(grad_scores, keys, 0, 0) * factor).astype(BF16)
            pre_buf[pl.ds(i * qn, qn), g, :, :size] = dq[:, :size].reshape(qn, rows, size)
            return jnp.sum(dq.astype(F32), axis=0, keepdims=True)

        for i in range(total // QB):
            more = attend(i)
            bias_q = more if bias_q is None else bias_q + more
            if i % 2 == 1 and hops < half:
                sca.hop(hops)
                hops += 1
        dk = dk_acc[...].astype(BF16)
        dv = dv_acc[...].astype(BF16)
        more = jnp.sum(dv.astype(F32), axis=0, keepdims=True)
        bias_v = more if bias_v is None else bias_v + more
        pre_buf[:, g, :, size : 2 * size] = dk[:, :size].reshape(shards, rows, size)
        pre_buf[:, g, :, 2 * size : 3 * size] = dv[:, :size].reshape(shards, rows, size)
        for j in range(1, shards):
            pre_copy(j, g).start()
    for j in range(shards):
        to_keeper(gup_ref, up_land, up_s, up_r, j, start)
    pre_land[me] = pre_buf[me]
    load_h.wait()
    gqkv = dot(pre_buf[...].reshape(tokens, -1), h_buf[...].reshape(tokens, width), 0, 0)
    gqkv = jnp.transpose(gqkv).astype(BF16)
    for i in range(shards):
        qkv_buf[i, :size] = gqkv[i * size : (i + 1) * size]
    for j in range(shards):
        to_keeper(qkv_buf, qkv_land, qkv_s, qkv_r, j, start)
    down = sca.result()
    out = mid_ref[...].reshape(own, width) + down + dbias_ref[...]
    out = out * valid_rows(counts_ref, me, groups, rows)
    out_ref[...] = out.astype(BF16).reshape(groups, rows, width)
    load_w.wait()
    for j in range(1, shards):
        frm = (me + shards - j) % shards
        for g in range(groups):
            send(pre_buf.at[frm, g], pre_land.at[frm, g], pre_s.at[g, j], pre_r.at[g, frm], (dp, frm)).wait_recv()
    for h in range(shards):
        block = pre_land[h].reshape(own, -1)
        for c in range(3):
            at = c * width + h * size
            mine_buf[:, at : at + size] = block[:, c * size : (c + 1) * size]
    grad_h1 = dot(mine_buf[:, :width], w_buf[0], 1, 1)
    for c in range(1, 3):
        grad_h1 = grad_h1 + dot(mine_buf[:, c * width : (c + 1) * width], w_buf[c], 1, 1)
    normed, scale = normalize(x_ref[...].reshape(own, width).astype(F32))
    sg = gmid_ref[...].reshape(own, width) + norm_back(grad_h1, normed, scale, gain_ref[0:1])
    sg_ref[...] = sg.reshape(groups, rows, width).astype(BF16)
    gain = jnp.sum(grad_h1 * normed, axis=0, keepdims=True)
    shift = jnp.sum(grad_h1, axis=0, keepdims=True)
    vecs = jnp.concatenate(
        [gain, sums_ref[0:1], shift, sums_ref[1:2], sums_ref[2:3], sums_ref[3:4], gain, gain], axis=0
    )
    for i in range(shards):
        vec_buf[i, :, :size] = vecs[:, i * size : (i + 1) * size]
    for j in range(shards):
        to_keeper(vec_buf, vec_land, vec_s, vec_r, j, start)
    keep_own(vec_buf, vec_land)

    for i in range(1, parts):
        do_wait(i)
    do_land[dp] = gdo_ref[dp]
    acc = do_land[0].astype(F32)
    for i in range(1, parts):
        acc = acc + do_land[i].astype(F32)
    cols = width // parts
    ffr = gdo_ref.shape[1] - (size + 15) // 16 * 16
    gdown_ref[...] = acc[:ff, :cols]
    gout_ref[...] = acc[ffr : ffr + size, :cols]
    keep_own(gup_ref, up_land)
    keep_own(qkv_buf, qkv_land)
    from_keepers(gup_ref, up_land, up_r, up_s)
    for i in range(per):
        acc = up_land[i * parts].astype(F32)
        for x in range(1, parts):
            acc = acc + up_land[i * parts + x].astype(F32)
        up_ref[:, i * ff : (i + 1) * ff] = acc[:size, :ff]
    from_keepers(vec_buf, vec_land, vec_r, vec_s)
    acc = vec_land[0]
    for i in range(1, shards):
        acc = acc + vec_land[i]
    tiny_land[dp, 0:5] = acc[0:5]
    tiny_land[dp, 5:6] = bias_q
    tiny_land[dp, 6:7] = bias_v
    tiny_land[dp, 7:8] = vec_buf[me][5:6]
    for i in range(bup_ref.shape[1] // 128):
        tiny_land[dp, 8 + i : 9 + i] = bup_ref[:, i * 128 : (i + 1) * 128]

    def tiny(i):
        to = (dp + i) % parts
        return send(tiny_land.at[dp], tiny_land.at[dp], tiny_s.at[i], tiny_r.at[dp], (to, me))

    for i in range(1, parts):
        tiny(i).start()
    from_keepers(qkv_buf, qkv_land, qkv_r, qkv_s)
    for i in range(per):
        acc = qkv_land[i * parts].astype(F32)
        for x in range(1, parts):
            acc = acc + qkv_land[i * parts + x].astype(F32)
        for c in range(3):
            qkv_ref[c, :, i * size : (i + 1) * size] = acc[:size, c * size : (c + 1) * size]
    for i in range(1, parts):
        frm = (dp + i) % parts
        send(tiny_land.at[frm], tiny_land.at[frm], tiny_s.at[i], tiny_r.at[frm], (frm, me)).wait_recv()
    acc = tiny_land[0]
    for i in range(1, parts):
        acc = acc + tiny_land[i]
    ggain_ref[...] = acc[0:2, :size]
    gshift_ref[...] = acc[2:4, :size]
    gab_ref[0:2] = acc[5:7, :size]
    gab_ref[2:3] = acc[4:5, :size]
    gdb_ref[...] = acc[7:8, :size]
    for i in range(bup_ref.shape[1] // 128):
        n = min(128, ff - i * 128)
        if n > 0:
            gub_ref[:, i * 128 : i * 128 + n] = acc[8 + i : 9 + i, :n]
    for j in range(1, shards):
        for g in range(groups):
            pre_copy(j, g).wait_send()
    for i in range(1, parts):
        do_copy(i).wait_send()
        tiny(i).wait_send()
    for j in range(shards):
        to_keeper(gup_ref, up_land, up_s, up_r, j, done)
        to_keeper(qkv_buf, qkv_land, qkv_s, qkv_r, j, done)
        to_keeper(vec_buf, vec_land, vec_s, vec_r, j, done)
    sca.finish()


def rear(
    shards, size, ff, parts, counts, q, k, v, gatt, att, lse, states, mid, gmid, gup, gdo, sums, bup, gains, dbias,
    h1, down, w_qkv,
):
    groups, rows, width = states.shape
    per = shards // parts
    wp = up128(3 * size)
    sp = q.shape[3]
    sds = jax.ShapeDtypeStruct
    tiny = 8 + bup.shape[1] // 128
    cols = width // parts
    return pl.pallas_call(
        functools.partial(rear_kernel, shards, size, ff, parts),
        out_shape=[
            sds((groups, rows, width), BF16), sds((groups, rows, width), BF16), sds((3, size, per * size), F32),
            sds((size, cols), F32), sds((3, size), F32), sds((2, size), F32), sds((2, size), F32),
            sds((size, per * ff), F32), sds((1, ff), F32), sds((ff, cols), F32), sds((1, size), F32),
        ],
        in_specs=[pl.BlockSpec(memory_space=pltpu.SMEM)]
        + [pl.BlockSpec(memory_space=VMEM)] * 15
        + [pl.BlockSpec(memory_space=pl.ANY)] * 3,
        out_specs=[pl.BlockSpec(memory_space=VMEM)] * 11,
        scratch_shapes=[
            VMEM(h1.shape, BF16), VMEM(down.shape, BF16), VMEM(w_qkv.shape, BF16),
            VMEM((shards * rows, sp), F32), VMEM((shards * rows, sp), F32),
            VMEM((shards, groups, rows, wp), BF16), VMEM((shards, groups, rows, wp), BF16),
            VMEM((groups * rows, 3 * width), BF16),
            VMEM((shards,) + gup.shape[1:2] + (wp,), BF16), VMEM((shards,) + gup.shape[1:2] + (wp,), BF16),
            VMEM(gup.shape, BF16), VMEM(gdo.shape, BF16),
            VMEM((shards, 8, 128), F32), VMEM((shards, 8, 128), F32), VMEM((parts, tiny, 128), F32),
        ]
        + [DMA((groups, shards))] * 2 + [DMA((shards,))] * 4 + [DMA((parts,))] * 2 + [DMA((shards,))] * 2
        + [DMA((parts,))] * 2 + [DMA((4,))]
        + scatter_scratch(shards, rows, width),
        name="rear",
        compiler_params=pltpu.CompilerParams(
            collective_id=1, has_side_effects=True, vmem_limit_bytes=56 << 20
        ),
    )(counts, q, k, v, gatt, att, lse, states, mid, gmid, gup, gdo, sums, bup, gains, dbias, h1, down, w_qkv)


def body(
    states, counts, cotangent, w_qkv, w_out, attn_bias, norm_gain, norm_bias,
    w_up, up_bias, w_down, down_bias,
):
    width = states.shape[2]
    shards = lax.axis_size("seq")
    parts = lax.axis_size("dp")
    me = lax.axis_index("seq")
    size = width // HEADS
    ff = w_up.shape[1] // shards

    def mine(x, axis, count):
        return lax.dynamic_slice_in_dim(x, me * count, count, axis)

    bu = pad_to(mine(up_bias, 0, ff)[None], 1, up128(ff))
    bq = pad_to(mine(attn_bias, 1, size), 1, up128(size))
    h1, q, k, v, att, lse, mid, gmid, gatt, gup, gdo, down, sums, bup = front(
        shards, size, ff, parts, counts, states, cotangent, norm_gain, norm_bias, attn_bias,
        mine(w_qkv, 2, size), bq, w_out, mine(w_out, 0, size), mine(w_up, 1, ff), mine(w_down, 0, ff), bu,
    )
    layer_out, state_grad, g_qkv, g_out, g_ab, g_gain, g_shift, g_up, g_ub, g_down, g_db = rear(
        shards, size, ff, parts, counts, q, k, v, gatt, att, lse, states, mid, gmid, gup, gdo, sums, bup,
        norm_gain, down_bias[None], h1, down, w_qkv,
    )
    return (
        layer_out, state_grad, g_qkv, g_out, g_ab, g_gain, g_shift, g_up,
        g_ub.reshape(ff), g_down, g_db.reshape(size),
    )


def solution(mesh):
    placed = (P("dp", "seq", None), P("dp", None), P("dp", "seq", None)) + (P(),) * 9
    return jax.shard_map(
        body,
        mesh=mesh,
        in_specs=placed,
        out_specs=(
            P("dp", "seq", None), P("dp", "seq", None), P(None, "seq", "dp"), P("seq", "dp"),
            P(None, "seq"), P(None, "seq"), P(None, "seq"), P("seq", "dp"), P("seq"),
            P("seq", "dp"), P("seq"),
        ),
        check_vma=False,
    )
```

```python
import functools
import math

import jax
import jax.numpy as jnp
from jax import lax
from jax.experimental import pallas as pl
from jax.experimental.pallas import tpu as pltpu
from jax.sharding import PartitionSpec as P

HEADS = 16
EPS = 1e-06
NEG = -1e30
F32 = jnp.float32
BF16 = jnp.bfloat16
MESH = pl.DeviceIdType.MESH
VMEM = pltpu.VMEM
DMA = pltpu.SemaphoreType.DMA


def mm(spec, a, b):
    return jnp.einsum(spec, a, b, preferred_element_type=F32)


def dot(a, b, ca=1, cb=0):
    return lax.dot_general(a, b, (((ca,), (cb,)), ((), ())), preferred_element_type=F32)


def pad_to(x, axis, size):
    pads = [(0, 0)] * x.ndim
    pads[axis] = (0, size - x.shape[axis])
    return jnp.pad(x, pads)


def up128(n):
    return -(-n // 128) * 128


def normalize(values):
    mean = jnp.mean(values, axis=-1, keepdims=True)
    centred = values - mean
    scale = lax.rsqrt(jnp.mean(centred * centred, axis=-1, keepdims=True) + EPS)
    return (centred * scale, scale)


def norm_back(grad_norm, normed, scale, gain):
    scaled = grad_norm * gain
    return scale * (
        scaled
        - jnp.mean(scaled, axis=-1, keepdims=True)
        - normed * jnp.mean(scaled * normed, axis=-1, keepdims=True)
    )


def gelu_both(v):
    c, a = 0.7978845608028654, 0.044715
    sq = v * v
    t = jnp.tanh(c * (v + a * v * sq))
    half = 0.5 * (1.0 + t)
    return v * half, half + 0.5 * v * (1.0 - t * t) * (c * (1.0 + 3.0 * a * sq))


def send(src, dst, s, r, dev):
    return pltpu.make_async_remote_copy(
        src_ref=src, dst_ref=dst, send_sem=s, recv_sem=r, device_id=dev, device_id_type=MESH
    )


class Place:
    def __init__(self, shards, parts):
        self.shards, self.parts = shards, parts
        self.members = shards // 2
        self.n = self.members // 2
        self.half = self.n // 2
        self.me = lax.axis_index("seq")
        self.dp = lax.axis_index("dp")
        self.side = self.me // self.members
        self.m = (self.me + (self.members // 2) * self.side) % self.members
        self.chip = self.m // 2
        self.core = self.m % 2
        odd = self.chip % 2
        self.pos = (1 - odd) * (self.chip // 2) + odd * (self.n - 1 - self.chip // 2)
        self.to = (self.at(1, 1) * 2 + self.core, self.at(1, 0) * 2 + self.core)
        self.sib = self.chip * 2 + 1 - self.core
        self.partner = {"seq": self.seq_of(1 - self.side, self.m)}

    def seq_of(self, side, m):
        return side * self.members + (m + (self.members // 2) * side) % self.members

    def dev(self, m):
        return {"seq": self.seq_of(self.side, m)}

    def at(self, k, d):
        p = (self.pos + (self.n - k if d == 0 else k)) % self.n
        hi = p // self.half
        return (1 - hi) * 2 * p + hi * (2 * (self.n - 1 - p) + 1)

    def others(self):
        return [
            ((self.dp + i) % self.parts, (self.me + j) % self.shards)
            for i in range(self.parts) for j in range(self.shards) if i + j > 0
        ]


def gather_sems(n):
    return [DMA((2, n // 2 + 1, 2))] * 4


class Gather:
    def __init__(self, place, buf, base, sems):
        self.place, self.buf, self.base = place, buf, base
        self.ring_s, self.ring_r, self.sib_s, self.sib_r = sems
        self.sent = []

    def copy(self, k, d, g, to_sib):
        p = self.place
        block = self.buf.at[self.base + p.at(k, d) * 2 + p.core, g]
        s, r = (self.sib_s, self.sib_r) if to_sib else (self.ring_s, self.ring_r)
        return send(block, block, s.at[d, k, g], r.at[d, k, g], p.dev(p.sib if to_sib else p.to[d]))

    def go(self, *args):
        c = self.copy(*args)
        c.start()
        self.sent.append(c)

    def units(self, k):
        if k == self.place.half:
            return [(0, 0), (1, 1)]
        return [(0, 0), (1, 1), (0, 1), (1, 0)]

    def passes(self, k, d, g):
        return k < self.place.half - 1 or (k == self.place.half - 1 and g == d)

    def start(self, g):
        for d in (g, 1 - g):
            if self.passes(0, d, g):
                self.go(0, d, g, False)
        self.go(0, g, g, True)

    def hop(self, k):
        for d, g in self.units(k):
            self.copy(k - 1, d, g, False).wait_recv()
            if self.passes(k, d, g):
                self.go(k, d, g, False)
            self.go(k, d, g, True)

    def ready(self, k):
        for d, g in self.units(k):
            if k > 0 or d == g:
                self.copy(k, d, g, True).wait_recv()

    def blocks(self, k):
        if k == 0 or k == self.place.half:
            return [self.place.at(k, 0)]
        return [self.place.at(k, 0), self.place.at(k, 1)]

    def finish(self):
        for c in self.sent:
            c.wait_send()


def scatter_scratch(n, rows, width):
    return [
        VMEM((n, 2, rows, width), BF16), VMEM((2, n // 2, 2, rows, width), BF16),
        DMA((n,)), DMA((n,)), DMA((2, n // 2, 2)), DMA((2, n // 2, 2)),
    ]


class Scatter:
    def __init__(self, place, part, base, scratch):
        self.place, self.part, self.base = place, part, base
        self.sib_land, self.land, self.sib_s, self.sib_r, self.ring_s, self.ring_r = scratch
        self.sent = []
        self.have = set()

    def slot(self, k, d):
        if k == 0:
            return 0
        return self.place.n - 1 if k == self.place.half else 2 * k - 1 + d

    def sib_copy(self, k, d):
        p, i = self.place, self.slot(k, d)
        src = self.part.at[self.base + p.at(k, d) * 2 + 1 - p.core]
        return send(src, self.sib_land.at[i], self.sib_s.at[i], self.sib_r.at[i], p.dev(p.sib))

    def give(self, k, d):
        c = self.sib_copy(k, d)
        c.start()
        self.sent.append(c)

    def from_sib(self, k, d):
        i = self.slot(k, d)
        if i not in self.have:
            self.have.add(i)
            self.sib_copy(k, d).wait_recv()
        return self.sib_land.at[i]

    def dist(self, h, d, g):
        return self.place.half - h if g == d else self.place.half - 1 - h

    def block(self, h, d, g):
        p = self.place
        return self.base + p.at(self.dist(h, d, g), 1 - d) * 2 + p.core

    def ring_copy(self, h, d, g):
        return send(
            self.part.at[self.block(h, d, g), g], self.land.at[d, h, g],
            self.ring_s.at[d, h, g], self.ring_r.at[d, h, g], self.place.dev(self.place.to[d]),
        )

    def hop(self, h):
        for d, g in [(0, 0), (1, 1), (0, 1), (1, 0)]:
            j = self.dist(h, d, g)
            if j == 0:
                continue
            own = self.block(h, d, g)
            val = self.part[own, g].astype(F32) + self.from_sib(j, 1 - d)[g].astype(F32)
            if h > 0:
                self.ring_copy(h - 1, d, g).wait_recv()
                val = val + self.land[d, h - 1, g].astype(F32)
            self.part[own, g] = val.astype(BF16)
            c = self.ring_copy(h, d, g)
            c.start()
            self.sent.append(c)

    def result(self):
        p = self.place
        out = []
        for g in range(2):
            val = self.part[self.base + p.m, g].astype(F32) + self.from_sib(0, 0)[g].astype(F32)
            for d in range(2):
                h = p.half - 1 if g == d else p.half - 2
                self.ring_copy(h, d, g).wait_recv()
                val = val + self.land[d, h, g].astype(F32)
            out.append(val)
        return jnp.concatenate(out, axis=0)

    def finish(self):
        for c in self.sent:
            c.wait_send()


def rows_scratch(shards, parts, rows, width):
    gs, per = 2 * shards // parts, shards // parts
    return [
        VMEM((parts, gs, rows, width), BF16), VMEM((parts, gs, rows, width), BF16), VMEM((2 * per, rows, width), BF16),
        DMA((parts,)), DMA((parts,)), DMA((gs,)), DMA((2 * per,)), DMA,
    ]


class Rows:
    def __init__(self, place, scratch):
        self.place = place
        self.buf, self.land, self.last, self.s1, self.r1, self.s2, self.r2, self.loc = scratch
        self.gs = self.buf.shape[1]
        self.hp = place.parts // 2
        self.per = place.shards // place.parts

    def put(self, i, s, rows, cols, val):
        at = i * self.place.shards + s
        self.buf[at // self.gs, at % self.gs, rows, cols] = val

    def share(self, j):
        p = self.place
        x = (p.dp + j) % p.parts
        return send(self.buf.at[x], self.land.at[p.dp], self.s1.at[j], self.r1.at[p.dp], (x, p.me))

    def first(self):
        for j in range(1, self.place.parts):
            self.share(j).start()

    def deliver(self, k, act, act_own):
        p = self.place
        unit = p.seq_of(p.dp // self.hp, p.m)
        keeper = unit // self.per
        owner = (p.dp % self.hp) * self.gs + k
        slot = (unit % self.per) * 2 + p.side
        away = (keeper != p.dp).astype(jnp.int32) + (owner != p.me).astype(jnp.int32)

        @pl.when(away > 0)
        def _():
            act(send(self.buf.at[p.dp, k], self.last.at[slot], self.s2.at[k], self.r2.at[slot], (keeper, owner)))

        if act_own:

            @pl.when(away == 0)
            def _():
                c = pltpu.make_async_copy(self.buf.at[p.dp, k], self.last.at[slot], self.loc)
                c.start()
                c.wait()

    def second(self):
        p = self.place
        for j in range(1, p.parts):
            x = (p.dp + j) % p.parts
            send(self.buf.at[x], self.land.at[x], self.s1.at[j], self.r1.at[x], (x, p.me)).wait_recv()
        for k in range(self.gs):
            val = self.buf[p.dp, k].astype(F32)
            for j in range(1, p.parts):
                val = val + self.land[(p.dp + j) % p.parts, k].astype(F32)
            self.buf[p.dp, k] = val.astype(BF16)
        for k in range(self.gs):
            self.deliver(k, lambda c: c.start(), True)

    def third(self):
        p = self.place
        for v in range(self.per):
            unit = p.dp * self.per + v
            i = unit // p.members
            m = (unit + (p.members // 2) * i) % p.members
            x = i * self.hp + p.me // self.gs
            for side in range(2):
                frm = p.seq_of(side, m)
                slot = 2 * v + side
                away = (x != p.dp).astype(jnp.int32) + (frm != p.me).astype(jnp.int32)

                @pl.when(away > 0)
                def _():
                    send(
                        self.buf.at[0, 0], self.last.at[slot], self.s2.at[0], self.r2.at[slot], (x, frm)
                    ).wait_recv()

    def total(self, v):
        return self.last[2 * v].astype(F32) + self.last[2 * v + 1].astype(F32)

    def finish(self):
        for j in range(1, self.place.parts):
            self.share(j).wait_send()
        for k in range(self.gs):
            self.deliver(k, lambda c: c.wait_send(), False)


def cols_scratch(parts, rows, width):
    return [
        VMEM((parts, 2, rows, width), BF16), VMEM((parts, 2, rows, width), BF16), VMEM((rows, width), BF16),
        DMA((parts,)), DMA((parts,)), DMA, DMA,
    ]


class Cols:
    def __init__(self, place, scratch):
        self.place = place
        self.buf, self.land, self.last, self.s1, self.r1, self.s2, self.r2 = scratch

    def put(self, i, val):
        p = self.place
        cols = val.shape[1] // p.parts
        val = val.astype(BF16)
        for x in range(p.parts):
            self.buf[x, i, : val.shape[0], :cols] = val[:, x * cols : (x + 1) * cols]

    def share(self, j):
        p = self.place
        x = (p.dp + j) % p.parts
        return send(self.buf.at[x], self.land.at[p.dp], self.s1.at[j], self.r1.at[p.dp], (x, p.me))

    def cross(self):
        p = self.place
        return send(self.buf.at[p.dp, 1 - p.side], self.last, self.s2, self.r2, p.partner)

    def first(self):
        for j in range(1, self.place.parts):
            self.share(j).start()

    def second(self):
        p = self.place
        for j in range(1, p.parts):
            x = (p.dp + j) % p.parts
            send(self.buf.at[x], self.land.at[x], self.s1.at[j], self.r1.at[x], (x, p.me)).wait_recv()
        for i in range(2):
            val = self.buf[p.dp, i].astype(F32)
            for j in range(1, p.parts):
                val = val + self.land[(p.dp + j) % p.parts, i].astype(F32)
            self.buf[p.dp, i] = val.astype(BF16)
        self.cross().start()

    def total(self):
        self.cross().wait_recv()
        p = self.place
        return self.buf[p.dp, p.side].astype(F32) + self.last[...].astype(F32)

    def finish(self):
        for j in range(1, self.place.parts):
            self.share(j).wait_send()
        self.cross().wait_send()


def chip_rows(ref, chip, base=0):
    val = ref[pl.ds(base + 2 * chip, 2)]
    return val.reshape(-1, val.shape[-1])


def chip_put(ref, chip, val, base=0):
    ref[pl.ds(base + 2 * chip, 2)] = val.astype(ref.dtype).reshape((2,) + ref.shape[1:])


def ids_at(positions, ends):
    total = (positions >= ends[0]).astype(jnp.int32)
    for end in ends[1:]:
        total = total + (positions >= end).astype(jnp.int32)
    return total


def log2(n):
    assert n & (n - 1) == 0
    return n.bit_length() - 1


QB = 256
LANES = 128


def layer_kernel(
    shards, size, ff, parts,
    counts_ref, x_ref, ct_ref, gain_ref, nbias_ref, abias_ref, dbias_ref, wq_ref, bq_ref, bu_ref,
    wout_hbm, wo_hbm, wu_hbm, wd_hbm, w_hbm,
    out_ref, sg_ref, qkv_ref, gout_ref, gab_ref, ggain_ref, gshift_ref, up_ref, gub_ref, gdown_ref, gdb_ref,
    pool, h_buf, m_buf, part2, x_buf, ct_buf, mid_buf, gmid_buf, qkv_buf, att_buf, att_b, att_land, lse_buf, mine_buf,
    act_buf, ghid_buf, gatt_buf, dk_acc, dv_acc, pre_buf, pre_land, wq_buf, wout_buf, wo_buf, wu_buf, wd_buf, row_buf,
    vec_buf, vec_land, bias_buf, bias_land, tiny_land, out_buf, out_land,
    ex_s, ex_r, att_s, att_r, pre_s, pre_r, vec_s, vec_r, bias_s, bias_r, tiny_s, tiny_r, loc, *rest,
):
    p = Place(shards, parts)
    me, dp, side, m = p.me, p.dp, p.side, p.m
    bar = pltpu.get_barrier_semaphore()
    for dev in p.others():
        pl.semaphore_signal(bar, inc=1, device_id=dev, device_id_type=MESH)
    loads = [
        pltpu.make_async_copy(src, dst, loc.at[1 + i])
        for i, (src, dst) in enumerate(
            ((wout_hbm, wout_buf), (wo_hbm, wo_buf), (wu_hbm, wu_buf), (wd_hbm, wd_buf))
        )
    ]
    for c in loads:
        c.start()
    rows, width = x_ref.shape[1:]
    members, half = p.members, p.half
    own = 2 * rows
    total = members * own
    sp = wo_buf.shape[0] // 2
    fp = wu_buf.shape[0] // 2
    factor = 1.0 / math.sqrt(size)
    at_part, at_h2, at_gy = 0, members, 2 * members
    gat1 = Gather(p, h_buf, 0, rest[0:4])
    gaty = Gather(p, pool, at_gy, rest[4:8])
    gat = Gather(p, pool, at_h2, rest[8:12])
    gat2 = Gather(p, m_buf, 0, rest[12:16])
    sca = Scatter(p, pool, at_part, rest[16:22])
    sca2 = Scatter(p, part2, 0, rest[22:28])
    g_up = Rows(p, rest[28:36])
    g_qkv = Rows(p, rest[36:44])
    g_down = Cols(p, rest[44:51])
    g_out = Cols(p, rest[51:58])

    ends = [counts_ref[side, 0]]
    for i in range(1, counts_ref.shape[1]):
        ends.append(ends[-1] + counts_ref[side, i])

    def ids_of(t):
        mem = lax.shift_right_logical(t, log2(own))
        rho = lax.shift_right_logical(t, log2(rows)) & 1
        sig = rho + side - 2 * rho * side
        seq = sig * members + ((mem + (members // 2) * sig) & (members - 1))
        return ids_at(seq * rows + (t & (rows - 1)), ends)

    def iota(shape, dim):
        return lax.broadcasted_iota(jnp.int32, shape, dim)

    valid = (ids_of(iota((own, 1), 0) + m * own) < counts_ref.shape[1]).astype(F32)

    def swap(src, dst, i):
        return send(src, dst, ex_s.at[i], ex_r.at[i], p.partner)

    def norm_one(g):
        normed, _ = normalize(x_buf[g].astype(F32))
        h_buf[m, g] = (normed * gain_ref[0:1] + nbias_ref[0:1]).astype(BF16)

    x_buf[0] = x_ref[side]
    norm_one(0)
    pl.semaphore_wait(bar, len(p.others()))
    swap_x = swap(x_ref.at[1 - side], x_buf.at[1], 0)
    swap_ct = swap(ct_ref.at[1 - side], ct_buf, 1)
    swap_x.start()
    gat1.start(0)
    swap_ct.start()
    pool[at_gy + m, 0] = (ct_ref[side].astype(F32) * valid[:rows]).astype(BF16)
    wq_buf[...] = jnp.zeros(wq_buf.shape, BF16)
    row_buf[...] = jnp.zeros(row_buf.shape, F32)
    for i in range(2):
        for c in range(3):
            lanes = slice((2 * c + i) * sp, (2 * c + i) * sp + size)
            wq_buf[:, lanes] = wq_ref[i, c]
            if c != 1:
                row_buf[0:1, lanes] = bq_ref[i, c // 2 : c // 2 + 1]
        row_buf[1:2, i * fp : i * fp + ff] = bu_ref[i]
    swap_x.wait_recv()
    norm_one(1)
    gat1.start(1)
    swap_ct.wait_recv()
    pool[at_gy + m, 1] = (ct_buf[...].astype(F32) * valid[rows:]).astype(BF16)

    def project(chip):
        out = dot(chip_rows(h_buf, chip), wq_buf[...]) + row_buf[0:1, : 6 * sp]
        out = jnp.concatenate([out[:, : 2 * sp] * factor, out[:, 2 * sp :]], axis=1)
        chip_put(qkv_buf, chip, out)

    for k in range(1, half + 1):
        gat1.hop(k)
        if k == half - 1:
            gaty.start(0)
            gaty.start(1)
        gat1.ready(k - 1)
        for chip in gat1.blocks(k - 1):
            project(chip)
    gat1.ready(half)
    project(p.at(half, 0))

    qn = QB // own

    def att_copy(to):
        return send(att_b.at[to], att_land.at[m], att_s.at[to], att_r.at[m], p.dev(to))

    def lanes_of(part, i):
        return slice((2 * part + i) * sp, (2 * part + i + 1) * sp)

    row_ids = ids_of(iota((1, total), 1))

    def attend(b):
        query_ids = ids_of(iota((QB, 1), 0) + b * QB)
        same = query_ids == row_ids
        for i in range(2):
            query = qkv_buf[pl.ds(b * qn, qn), :, :, lanes_of(0, i)].reshape(QB, sp)
            keys = qkv_buf[:, :, :, lanes_of(1, i)].reshape(total, sp)
            values = qkv_buf[:, :, :, lanes_of(2, i)].reshape(total, sp)
            scores = jnp.where(same, dot(query, keys, 1, 1), NEG)
            high = jnp.max(scores, axis=-1, keepdims=True)
            weights = jnp.exp(scores - high)
            sums = jnp.sum(weights, axis=-1, keepdims=True)
            out = (dot(weights.astype(BF16), values) / sums).reshape(qn, 2, rows, sp)
            att_buf[pl.ds(b * qn, qn), :, :, i * sp : (i + 1) * sp] = out
            att_b[pl.ds(b * qn, qn), :, :, i * sp : (i + 1) * sp] = out.astype(BF16)
            lse = jnp.broadcast_to(high + jnp.log(sums), (QB, LANES))
            lse_buf[i, b] = jnp.transpose(lse)[0:8]
        for t in range(qn):
            to = b * qn + t

            @pl.when(to != m)
            def _():
                att_copy(to).start()

    blocks = total // QB
    pl.loop(0, blocks // 2)(attend)
    gaty.hop(1)
    pl.loop(blocks // 2, blocks)(attend)
    for k in range(2, half + 1):
        gaty.hop(k)
    att_land[m] = att_b[m]
    for j in range(1, members):
        frm = (m + members - j) % members
        send(att_b.at[frm], att_land.at[frm], att_s.at[frm], att_r.at[frm], p.dev(frm)).wait_recv()
    for j in range(members):
        for i in range(2):
            at = p.seq_of(i, j) * size
            mine_buf[:, at : at + size] = att_land[j].reshape(own, 2 * sp)[:, i * sp : i * sp + size]
    for c in loads:
        c.wait()
    inputs = x_buf[...].reshape(own, width).astype(F32)
    mid = inputs + dot(mine_buf[:, :width], wout_buf[...]) + abias_ref[2:3]
    mid_buf[...] = mid
    normed, _ = normalize(mid)
    pool[at_h2 + m] = (normed * gain_ref[1:2] + nbias_ref[1:2]).astype(BF16).reshape(2, rows, width)
    gat.start(0)
    gat.start(1)

    def forward(chip):
        hidden = dot(chip_rows(pool, chip, at_h2), wu_buf[...], 1, 1) + row_buf[1:2, : 2 * fp]
        act, slope = gelu_both(hidden)
        chip_put(act_buf, chip, act)
        ghid = (dot(chip_rows(pool, chip, at_gy), wd_buf[...], 1, 1) * slope).astype(BF16)
        chip_put(ghid_buf, chip, ghid)
        chip_put(pool, chip, dot(ghid, wu_buf[...]), at_part)

    for k in range(half + 1):
        if k < half:
            gat.hop(k + 1)
        gaty.ready(k)
        gat.ready(k)
        for d, chip in enumerate(gat.blocks(k)):
            forward(chip)
            sca.give(k, d)

    def flat(val):
        return val.reshape(total, val.shape[-1])

    for h in range(half):
        sca.hop(h)
        if h == 0:
            gdown = dot(flat(act_buf[...]), flat(pool[at_gy : at_gy + members]), 0, 0)
            for i in range(2):
                g_down.put(i, gdown[i * fp : i * fp + (ff + 15) // 16 * 16])
            g_down.first()
    gup = dot(flat(ghid_buf[...]), flat(pool[at_h2 : at_h2 + members]), 0, 0)
    main, left = ff // LANES * LANES, ff % LANES
    low = (size + 15) // 16 * 16
    for i in range(2):
        tall = jnp.transpose(gup[i * fp : i * fp + main]).astype(BF16)
        flat_left = gup[i * fp + main : i * fp + main + (left + 15) // 16 * 16].astype(BF16)
        for s in range(shards):
            g_up.put(i, s, slice(0, size), slice(0, main), tall[s * size : (s + 1) * size])
            if left:
                g_up.put(i, s, slice(low, low + flat_left.shape[0]), slice(0, size), flat_left[:, s * size : (s + 1) * size])
    g_up.first()
    grad_h2 = sca.result()
    normed, scale = normalize(mid_buf[...])
    gy_own = pool[at_gy + m].reshape(own, width).astype(F32)
    gmid = gy_own + norm_back(grad_h2, normed, scale, gain_ref[1:2])
    gmid_buf[...] = gmid
    m_buf[m] = gmid.astype(BF16).reshape(2, rows, width)
    gat2.start(0)
    gat2.start(1)

    def over_rows(val):
        return jnp.sum(val, axis=0, keepdims=True)

    gain_two, shift_two, bias_out, bias_down = (
        over_rows(grad_h2 * normed), over_rows(grad_h2), over_rows(gmid), over_rows(gy_own)
    )
    bias_up = over_rows(flat(ghid_buf[...]).astype(F32))

    def down_part(chip):
        chip_put(part2, chip, dot(chip_rows(act_buf, chip), wd_buf[...]))

    def back(chip):
        block = chip_rows(m_buf, chip)
        chip_put(gatt_buf, chip, dot(block, wo_buf[...], 1, 1))
        return dot(chip_rows(att_b, chip), block, 0, 0)

    gout = None
    for k in range(half + 1):
        for d, chip in enumerate(gat.blocks(k)):
            down_part(chip)
            sca2.give(k, d)
        if k < half:
            gat2.hop(k + 1)
        gat2.ready(k)
        for chip in gat2.blocks(k):
            more = back(chip)
            gout = more if gout is None else gout + more
    for i in range(2):
        g_out.put(i, gout[i * sp : i * sp + low])
    g_out.first()
    for x in (gat, gaty, sca):
        x.finish()
    load_w = pltpu.make_async_copy(w_hbm, pool, loc.at[0])
    load_w.start()
    sca2.hop(0)
    g_down.second()

    col_ids = ids_of(iota((total, 1), 0))

    def pre_copy(i, j):
        to = (m + j) % members
        return send(pre_buf.at[i, to], pre_land.at[i, m], pre_s.at[i, j], pre_r.at[i, m], p.dev(to))

    pre_buf[:, :, :, :, 3 * size :] = jnp.zeros(pre_buf.shape[:4] + (pre_buf.shape[4] - 3 * size,), BF16)
    bias_buf[...] = jnp.zeros(bias_buf.shape, F32)
    for i in range(2):
        dk_acc[...] = jnp.zeros(dk_acc.shape, F32)
        dv_acc[...] = jnp.zeros(dv_acc.shape, F32)
        own_lanes = slice(i * sp, (i + 1) * sp)

        def attend_back(b):
            blk = pl.ds(b * qn, qn)
            query = qkv_buf[blk, :, :, lanes_of(0, i)].reshape(QB, sp)
            keys = qkv_buf[:, :, :, lanes_of(1, i)].reshape(total, sp)
            values = qkv_buf[:, :, :, lanes_of(2, i)].reshape(total, sp)
            grad = gatt_buf[blk, :, :, own_lanes].reshape(QB, sp)
            att = att_buf[blk, :, :, own_lanes].reshape(QB, sp)
            delta = jnp.sum(grad.astype(F32) * att, axis=-1, keepdims=True)
            delta = jnp.transpose(jnp.broadcast_to(delta, (QB, LANES)))[0:1]
            same = col_ids == ids_of(iota((1, QB), 1) + b * QB)
            probs = jnp.exp(jnp.where(same, dot(keys, query, 1, 1), NEG) - lse_buf[i, b][0:1])
            grad_scores = (probs * (dot(values, grad, 1, 1) - delta)).astype(BF16)
            dv_acc[...] += dot(probs.astype(BF16), grad)
            dk_acc[...] += dot(grad_scores, query)
            dq = (dot(grad_scores, keys, 0, 0) * factor).astype(BF16)
            pre_buf[i, blk, :, :, :size] = dq[:, :size].reshape(qn, 2, rows, size)
            bias_buf[i, 0:1] += over_rows(dq.astype(F32))

        for b in range(blocks):
            attend_back(b)
        dk = dk_acc[...].astype(BF16)
        dv = dv_acc[...].astype(BF16)
        bias_buf[i, 1:2] = over_rows(dv.astype(F32))
        for j in range(fp // LANES):
            bias_buf[i, 2 + j : 3 + j] = bias_up[:, i * fp + j * LANES : i * fp + (j + 1) * LANES]
        pre_buf[i, :, :, :, size : 2 * size] = dk[:, :size].reshape(members, 2, rows, size)
        pre_buf[i, :, :, :, 2 * size : 3 * size] = dv[:, :size].reshape(members, 2, rows, size)
        for j in range(1, members):
            pre_copy(i, j).start()
        if i == 0:
            for h in range(1, half):
                sca2.hop(h)
            g_up.second()
            g_out.second()

    for i in range(2):
        grad = dot(pre_buf[i].reshape(total, pre_buf.shape[4]), flat(h_buf[...]), 0, 0)
        grad = jnp.transpose(grad).astype(BF16)
        for s in range(shards):
            g_qkv.put(i, s, slice(0, size), slice(0, grad.shape[1]), grad[s * size : (s + 1) * size])
    g_qkv.first()

    def bias_copy(x, i):
        to = ((dp + x) % parts, p.seq_of(i, m))
        return send(
            bias_buf.at[i], bias_land.at[side * parts + dp], bias_s.at[x, i], bias_r.at[side * parts + dp], to
        )

    for x in range(parts):
        for i in range(2):
            if x > 0:
                bias_copy(x, i).start()
            else:

                @pl.when(side != i)
                def _():
                    bias_copy(0, i).start()

    down = sca2.result()
    out = ((mid_buf[...] + down + dbias_ref[...]) * valid).astype(BF16)
    out_ref[side] = out[:rows]
    out_buf[0] = out[rows:]
    swap_out = swap(out_buf.at[0], out_land.at[0], 2)
    swap_out.start()
    load_w.wait()
    for i in range(2):
        for j in range(1, members):
            frm = (m + members - j) % members
            send(pre_buf.at[i, frm], pre_land.at[i, frm], pre_s.at[i, j], pre_r.at[i, frm], p.dev(frm)).wait_recv()
        pre_land[i, m] = pre_buf[i, m]
        for j in range(members):
            block = pre_land[i, j].reshape(own, pre_land.shape[4])
            for c in range(3):
                at = c * width + p.seq_of(i, j) * size
                mine_buf[:, at : at + size] = block[:, c * size : (c + 1) * size]
    per_w = width // own
    grad_h1 = None
    for c in range(3):
        w = pool[c * per_w : (c + 1) * per_w].reshape(width, width)
        more = dot(mine_buf[:, c * width : (c + 1) * width], w, 1, 1)
        grad_h1 = more if grad_h1 is None else grad_h1 + more
    normed, scale = normalize(x_buf[...].reshape(own, width).astype(F32))
    sg = (gmid_buf[...] + norm_back(grad_h1, normed, scale, gain_ref[0:1])).astype(BF16)
    out_buf[1] = sg[rows:]
    swap_sg = swap(out_buf.at[1], out_land.at[1], 3)
    swap_sg.start()
    sg_ref[side] = sg[:rows]
    vecs = jnp.concatenate(
        [over_rows(grad_h1 * normed), gain_two, over_rows(grad_h1), shift_two, bias_out, bias_down, bias_out, bias_out],
        axis=0,
    )
    for s in range(shards):
        vec_buf[s, :, :size] = vecs[:, s * size : (s + 1) * size]
    per = shards // parts
    keeper = me // per

    def vec_copy(j, act):
        to = (me + j) % shards
        slot = (me % per) * parts + dp
        copy = lambda: act(send(vec_buf.at[to], vec_land.at[slot], vec_s.at[j], vec_r.at[slot], (keeper, to)))
        if j > 0:
            copy()
        else:
            pl.when(keeper != dp)(copy)

    for j in range(shards):
        vec_copy(j, lambda c: c.start())

    @pl.when(keeper == dp)
    def _():
        vec_land[(me % per) * parts + dp] = vec_buf[me]

    g_qkv.second()

    cols = width // parts
    gdown_ref[...] = g_down.total()[:ff, :cols]
    gout_ref[...] = g_out.total()[:size, :cols]
    g_up.third()
    for v in range(per):
        acc = g_up.total(v)
        up_ref[:, v * ff : v * ff + main] = acc[:size, :main]
        if left:
            tail = jnp.transpose(acc[low:, :LANES])
            up_ref[:, v * ff + main : (v + 1) * ff] = tail[:size, :left]
    for i in range(per):
        for x in range(parts):
            slot = i * parts + x
            frm = dp * per + i
            away = (frm != me).astype(jnp.int32) + (dp != x).astype(jnp.int32)

            @pl.when(away > 0)
            def _():
                send(vec_buf.at[0], vec_land.at[slot], vec_s.at[0], vec_r.at[slot], (x, frm)).wait_recv()

    acc = vec_land[0]
    for i in range(1, shards):
        acc = acc + vec_land[i]
    tiny_land[dp] = acc

    def tiny(j):
        x = (dp + j) % parts
        return send(tiny_land.at[dp], tiny_land.at[dp], tiny_s.at[j], tiny_r.at[dp], (x, me))

    for j in range(1, parts):
        tiny(j).start()
    bias_land[side * parts + dp] = bias_buf[side]
    for s in range(2):
        for x in range(parts):
            slot = s * parts + x
            away = (side != s).astype(jnp.int32) + (dp != x).astype(jnp.int32)

            @pl.when(away > 0)
            def _():
                send(
                    bias_buf.at[0], bias_land.at[slot], bias_s.at[0, 0], bias_r.at[slot], (x, p.seq_of(s, m))
                ).wait_recv()

    acc = bias_land[0]
    for i in range(1, 2 * parts):
        acc = acc + bias_land[i]
    gab_ref[0:2] = acc[0:2, :size]
    for j in range(fp // LANES):
        n = min(LANES, ff - j * LANES)
        gub_ref[:, j * LANES : j * LANES + n] = acc[2 + j : 3 + j, :n]
    g_qkv.third()
    for v in range(per):
        acc = g_qkv.total(v)
        for c in range(3):
            qkv_ref[c, :, v * size : (v + 1) * size] = acc[:size, c * size : (c + 1) * size]
    swap_out.wait_recv()
    out_ref[1 - side] = out_land[0]
    swap_sg.wait_recv()
    sg_ref[1 - side] = out_land[1]
    for j in range(1, parts):
        x = (dp + j) % parts
        send(tiny_land.at[x], tiny_land.at[x], tiny_s.at[j], tiny_r.at[x], (x, me)).wait_recv()
    acc = tiny_land[0]
    for i in range(1, parts):
        acc = acc + tiny_land[i]
    ggain_ref[...] = acc[0:2, :size]
    gshift_ref[...] = acc[2:4, :size]
    gab_ref[2:3] = acc[4:5, :size]
    gdb_ref[...] = acc[5:6, :size]

    for c in (swap_x, swap_ct, swap_out, swap_sg):
        c.wait_send()
    for j in range(1, members):
        att_copy((m + j) % members).wait_send()
        for i in range(2):
            pre_copy(i, j).wait_send()
    for x in range(parts):
        for i in range(2):
            if x > 0:
                bias_copy(x, i).wait_send()
            else:

                @pl.when(side != i)
                def _():
                    bias_copy(0, i).wait_send()

    for j in range(shards):
        vec_copy(j, lambda c: c.wait_send())
    for j in range(1, parts):
        tiny(j).wait_send()
    for x in (gat1, gat2, sca2, g_up, g_qkv, g_down, g_out):
        x.finish()


def layer(shards, size, ff, parts, counts, states, cotangent, gains, nbias, abias, dbias, wq, bq, bu, w_out, wo, wu, wd, w_qkv):
    rows, width = states.shape[1:]
    members = shards // 2
    n = members // 2
    sp, fp = up128(size), up128(ff)
    own = 2 * rows
    total = members * own
    per = shards // parts
    cols = width // parts
    r16 = lambda k: -(-k // 16) * 16
    sds = jax.ShapeDtypeStruct
    block = (members, 2, rows)
    wp = up128(3 * size)
    w4 = w_qkv.reshape(3 * width // own, 2, rows, width)
    up_rows = r16(size) + r16(ff % LANES)
    return pl.pallas_call(
        functools.partial(layer_kernel, shards, size, ff, parts),
        out_shape=[
            sds((2, rows, width), BF16), sds((2, rows, width), BF16), sds((3, size, per * size), F32),
            sds((size, cols), F32), sds((3, size), F32), sds((2, size), F32), sds((2, size), F32),
            sds((size, per * ff), F32), sds((1, ff), F32), sds((ff, cols), F32), sds((1, size), F32),
        ],
        in_specs=[pl.BlockSpec(memory_space=pltpu.SMEM)]
        + [pl.BlockSpec(memory_space=VMEM)] * 9
        + [pl.BlockSpec(memory_space=pl.ANY)] * 5,
        out_specs=[pl.BlockSpec(memory_space=VMEM)] * 11,
        scratch_shapes=[
            VMEM(w4.shape, BF16), VMEM(block + (width,), BF16), VMEM(block + (width,), BF16), VMEM(block + (width,), BF16),
            VMEM((2, rows, width), BF16), VMEM((rows, width), BF16), VMEM((own, width), F32), VMEM((own, width), F32),
            VMEM(block + (6 * sp,), BF16), VMEM(block + (2 * sp,), F32), VMEM(block + (2 * sp,), BF16),
            VMEM(block + (2 * sp,), BF16), VMEM((2, total // QB, 8, QB), F32), VMEM((own, 3 * width), BF16),
            VMEM(block + (2 * fp,), BF16), VMEM(block + (2 * fp,), BF16), VMEM(block + (2 * sp,), BF16),
            VMEM((total, sp), F32), VMEM((total, sp), F32), VMEM((2,) + block + (wp,), BF16), VMEM((2,) + block + (wp,), BF16),
            VMEM((width, 6 * sp), BF16), VMEM(w_out.shape, BF16), VMEM((2 * sp, width), BF16), VMEM((2 * fp, width), BF16),
            VMEM((2 * fp, width), BF16),
            VMEM((2, max(6 * sp, 2 * fp)), F32),
            VMEM((shards, 8, LANES), F32), VMEM((shards, 8, LANES), F32), VMEM((2, 8, LANES), F32),
            VMEM((2 * parts, 8, LANES), F32), VMEM((parts, 8, LANES), F32), VMEM((2, rows, width), BF16),
            VMEM((2, rows, width), BF16),
            DMA((4,)), DMA((4,)), DMA((members,)), DMA((members,)), DMA((2, members)), DMA((2, members)),
            DMA((shards,)), DMA((shards,)), DMA((parts, 2)), DMA((2 * parts,)), DMA((parts,)), DMA((parts,)), DMA((5,)),
        ]
        + gather_sems(n) * 4
        + scatter_scratch(n, rows, width) * 2
        + rows_scratch(shards, parts, up_rows, ff // LANES * LANES)
        + rows_scratch(shards, parts, r16(size), wp)
        + cols_scratch(parts, r16(ff), up128(cols))
        + cols_scratch(parts, r16(size), up128(cols)),
        name="layer",
        compiler_params=pltpu.CompilerParams(
            collective_id=0, has_side_effects=True, vmem_limit_bytes=63 << 20
        ),
    )(counts, states, cotangent, gains, nbias, abias, dbias, wq, bq, bu, w_out, wo, wu, wd, w4)


def body(
    states, counts, cotangent, w_qkv, w_out, attn_bias, norm_gain, norm_bias,
    w_up, up_bias, w_down, down_bias,
):
    width = states.shape[2]
    shards = lax.axis_size("seq")
    parts = lax.axis_size("dp")
    size = width // HEADS
    ff = w_up.shape[1] // shards
    members = shards // 2
    me = lax.axis_index("seq")
    m = (me + (members // 2) * (me // members)) % members
    units = (m, members + (m + members // 2) % members)

    def mine(x, axis, count):
        return jnp.stack([lax.dynamic_slice_in_dim(x, u * count, count, axis) for u in units])

    def mine_rows(x, count):
        return pad_to(mine(x, 0, count), 1, up128(count)).reshape(2 * up128(count), width)

    layer_out, state_grad, g_qkv, g_out, g_ab, g_gain, g_shift, g_up, g_ub, g_down, g_db = layer(
        shards, size, ff, parts, counts, states, cotangent, norm_gain, norm_bias, attn_bias, down_bias[None],
        mine(w_qkv, 2, size), mine(attn_bias, 1, size), mine(up_bias[None], 1, ff), w_out, mine_rows(w_out, size),
        mine_rows(w_up.T, ff), mine_rows(w_down, ff), w_qkv,
    )
    return (
        layer_out, state_grad, g_qkv, g_out, g_ab, g_gain, g_shift, g_up,
        g_ub.reshape(ff), g_down, g_db.reshape(size),
    )


def solution(mesh):
    placed = (P("dp", "seq", None), P("dp", None), P("dp", "seq", None)) + (P(),) * 9
    return jax.shard_map(
        body,
        mesh=mesh,
        in_specs=placed,
        out_specs=(
            P("dp", "seq", None), P("dp", "seq", None), P(None, "seq", "dp"), P("seq", "dp"),
            P(None, "seq"), P(None, "seq"), P(None, "seq"), P("seq", "dp"), P("seq"),
            P("seq", "dp"), P("seq"),
        ),
        check_vma=False,
    )
```

```python
import functools
import math

import jax
import jax.numpy as jnp
from jax import lax
from jax.experimental import pallas as pl
from jax.experimental.pallas import tpu as pltpu
from jax.sharding import PartitionSpec as P

HEADS = 16
EPS = 1e-06
NEG = -1e30
F32 = jnp.float32
BF16 = jnp.bfloat16
MESH = pl.DeviceIdType.MESH
VMEM = pltpu.VMEM
DMA = pltpu.SemaphoreType.DMA


def mm(spec, a, b):
    return jnp.einsum(spec, a, b, preferred_element_type=F32)


def dot(a, b, ca=1, cb=0):
    return lax.dot_general(a, b, (((ca,), (cb,)), ((), ())), preferred_element_type=F32)


def pad_to(x, axis, size):
    pads = [(0, 0)] * x.ndim
    pads[axis] = (0, size - x.shape[axis])
    return jnp.pad(x, pads)


def up128(n):
    return -(-n // 128) * 128


def normalize(values):
    mean = jnp.mean(values, axis=-1, keepdims=True)
    centred = values - mean
    scale = lax.rsqrt(jnp.mean(centred * centred, axis=-1, keepdims=True) + EPS)
    return (centred * scale, scale)


def norm_back(grad_norm, normed, scale, gain):
    scaled = grad_norm * gain
    return scale * (
        scaled
        - jnp.mean(scaled, axis=-1, keepdims=True)
        - normed * jnp.mean(scaled * normed, axis=-1, keepdims=True)
    )


def gelu_both(v):
    c, a = 0.7978845608028654, 0.044715
    sq = v * v
    t = jnp.tanh(c * (v + a * v * sq))
    half = 0.5 * (1.0 + t)
    return v * half, half + 0.5 * v * (1.0 - t * t) * (c * (1.0 + 3.0 * a * sq))


def send(src, dst, s, r, dev):
    return pltpu.make_async_remote_copy(
        src_ref=src, dst_ref=dst, send_sem=s, recv_sem=r, device_id=dev, device_id_type=MESH
    )


class Place:
    def __init__(self, shards, parts):
        self.shards, self.parts = shards, parts
        self.members = shards // 2
        self.n = self.members // 2
        self.half = self.n // 2
        self.me = lax.axis_index("seq")
        self.dp = lax.axis_index("dp")
        self.side = self.me // self.members
        self.m = (self.me + (self.members // 2) * self.side) % self.members
        self.chip = self.m // 2
        self.core = self.m % 2
        odd = self.chip % 2
        self.pos = (1 - odd) * (self.chip // 2) + odd * (self.n - 1 - self.chip // 2)
        self.to = (self.at(1, 1) * 2 + self.core, self.at(1, 0) * 2 + self.core)
        self.sib = self.chip * 2 + 1 - self.core
        self.partner = {"seq": self.seq_of(1 - self.side, self.m)}

    def seq_of(self, side, m):
        return side * self.members + (m + (self.members // 2) * side) % self.members

    def dev(self, m):
        return {"seq": self.seq_of(self.side, m)}

    def at(self, k, d):
        p = (self.pos + (self.n - k if d == 0 else k)) % self.n
        hi = p // self.half
        return (1 - hi) * 2 * p + hi * (2 * (self.n - 1 - p) + 1)

    def others(self):
        return [
            ((self.dp + i) % self.parts, (self.me + j) % self.shards)
            for i in range(self.parts) for j in range(self.shards) if i + j > 0
        ]


def gather_sems(n):
    return [DMA((2, n // 2 + 1, 2))] * 4


class Gather:
    def __init__(self, place, buf, base, sems):
        self.place, self.buf, self.base = place, buf, base
        self.ring_s, self.ring_r, self.sib_s, self.sib_r = sems
        self.sent = []

    def copy(self, k, d, g, to_sib):
        p = self.place
        block = self.buf.at[self.base + p.at(k, d) * 2 + p.core, g]
        s, r = (self.sib_s, self.sib_r) if to_sib else (self.ring_s, self.ring_r)
        return send(block, block, s.at[d, k, g], r.at[d, k, g], p.dev(p.sib if to_sib else p.to[d]))

    def go(self, *args):
        c = self.copy(*args)
        c.start()
        self.sent.append(c)

    def units(self, k):
        if k == self.place.half:
            return [(0, 0), (1, 1)]
        return [(0, 0), (1, 1), (0, 1), (1, 0)]

    def passes(self, k, d, g):
        return k < self.place.half - 1 or (k == self.place.half - 1 and g == d)

    def start(self, g):
        for d in (g, 1 - g):
            if self.passes(0, d, g):
                self.go(0, d, g, False)
        self.go(0, g, g, True)

    def start_both(self):
        for d, g in self.units(0):
            if self.passes(0, d, g):
                self.go(0, d, g, False)
        for g in range(2):
            self.go(0, g, g, True)

    def hop(self, k):
        for d, g in self.units(k):
            self.copy(k - 1, d, g, False).wait_recv()
            if self.passes(k, d, g):
                self.go(k, d, g, False)
            self.go(k, d, g, True)

    def ready(self, k):
        for d, g in self.units(k):
            if k > 0 or d == g:
                self.copy(k, d, g, True).wait_recv()

    def blocks(self, k):
        if k == 0 or k == self.place.half:
            return [self.place.at(k, 0)]
        return [self.place.at(k, 0), self.place.at(k, 1)]

    def finish(self):
        for c in self.sent:
            c.wait_send()


def scatter_scratch(n, rows, width):
    return [
        VMEM((n, 2, rows, width), BF16), VMEM((2, n // 2, 2, rows, width), BF16),
        DMA((n,)), DMA((n,)), DMA((2, n // 2, 2)), DMA((2, n // 2, 2)),
    ]


class Scatter:
    def __init__(self, place, part, base, scratch):
        self.place, self.part, self.base = place, part, base
        self.sib_land, self.land, self.sib_s, self.sib_r, self.ring_s, self.ring_r = scratch
        self.sent = []
        self.have = set()

    def slot(self, k, d):
        if k == 0:
            return 0
        return self.place.n - 1 if k == self.place.half else 2 * k - 1 + d

    def sib_copy(self, k, d):
        p, i = self.place, self.slot(k, d)
        src = self.part.at[self.base + p.at(k, d) * 2 + 1 - p.core]
        return send(src, self.sib_land.at[i], self.sib_s.at[i], self.sib_r.at[i], p.dev(p.sib))

    def give(self, k, d):
        c = self.sib_copy(k, d)
        c.start()
        self.sent.append(c)

    def from_sib(self, k, d):
        i = self.slot(k, d)
        if i not in self.have:
            self.have.add(i)
            self.sib_copy(k, d).wait_recv()
        return self.sib_land.at[i]

    def dist(self, h, d, g):
        return self.place.half - h if g == d else self.place.half - 1 - h

    def block(self, h, d, g):
        p = self.place
        return self.base + p.at(self.dist(h, d, g), 1 - d) * 2 + p.core

    def ring_copy(self, h, d, g):
        return send(
            self.part.at[self.block(h, d, g), g], self.land.at[d, h, g],
            self.ring_s.at[d, h, g], self.ring_r.at[d, h, g], self.place.dev(self.place.to[d]),
        )

    def hop(self, h):
        for d, g in [(0, 0), (1, 1), (0, 1), (1, 0)]:
            j = self.dist(h, d, g)
            if j == 0:
                continue
            own = self.block(h, d, g)
            val = self.part[own, g].astype(F32) + self.from_sib(j, 1 - d)[g].astype(F32)
            if h > 0:
                self.ring_copy(h - 1, d, g).wait_recv()
                val = val + self.land[d, h - 1, g].astype(F32)
            self.part[own, g] = val.astype(BF16)
            c = self.ring_copy(h, d, g)
            c.start()
            self.sent.append(c)

    def result(self):
        p = self.place
        out = []
        for g in range(2):
            val = self.part[self.base + p.m, g].astype(F32) + self.from_sib(0, 0)[g].astype(F32)
            for d in range(2):
                h = p.half - 1 if g == d else p.half - 2
                self.ring_copy(h, d, g).wait_recv()
                val = val + self.land[d, h, g].astype(F32)
            out.append(val)
        return jnp.concatenate(out, axis=0)

    def finish(self):
        for c in self.sent:
            c.wait_send()


def rows_scratch(shards, parts, rows, width):
    gs, per = 2 * shards // parts, shards // parts
    return [
        VMEM((parts, gs, rows, width), BF16), VMEM((parts, gs, rows, width), BF16), VMEM((2 * per, rows, width), BF16),
        DMA((parts,)), DMA((parts,)), DMA((gs,)), DMA((2 * per,)), DMA,
    ]


class Rows:
    def __init__(self, place, scratch):
        self.place = place
        self.buf, self.land, self.last, self.s1, self.r1, self.s2, self.r2, self.loc = scratch
        self.gs = self.buf.shape[1]
        self.hp = place.parts // 2
        self.per = place.shards // place.parts

    def put(self, i, s, rows, cols, val):
        at = i * self.place.shards + s
        self.buf[at // self.gs, at % self.gs, rows, cols] = val

    def share(self, j):
        p = self.place
        x = (p.dp + j) % p.parts
        return send(self.buf.at[x], self.land.at[p.dp], self.s1.at[j], self.r1.at[p.dp], (x, p.me))

    def first(self):
        for j in range(1, self.place.parts):
            self.share(j).start()

    def deliver(self, k, act, act_own):
        p = self.place
        unit = p.seq_of(p.dp // self.hp, p.m)
        keeper = unit // self.per
        owner = (p.dp % self.hp) * self.gs + k
        slot = (unit % self.per) * 2 + p.side
        away = (keeper != p.dp).astype(jnp.int32) + (owner != p.me).astype(jnp.int32)

        @pl.when(away > 0)
        def _():
            act(send(self.buf.at[p.dp, k], self.last.at[slot], self.s2.at[k], self.r2.at[slot], (keeper, owner)))

        if act_own:

            @pl.when(away == 0)
            def _():
                c = pltpu.make_async_copy(self.buf.at[p.dp, k], self.last.at[slot], self.loc)
                c.start()
                c.wait()

    def second(self):
        p = self.place
        for j in range(1, p.parts):
            x = (p.dp + j) % p.parts
            send(self.buf.at[x], self.land.at[x], self.s1.at[j], self.r1.at[x], (x, p.me)).wait_recv()
        for k in range(self.gs):
            val = self.buf[p.dp, k].astype(F32)
            for j in range(1, p.parts):
                val = val + self.land[(p.dp + j) % p.parts, k].astype(F32)
            self.buf[p.dp, k] = val.astype(BF16)
        for k in range(self.gs):
            self.deliver(k, lambda c: c.start(), True)

    def third(self):
        p = self.place
        for v in range(self.per):
            unit = p.dp * self.per + v
            i = unit // p.members
            m = (unit + (p.members // 2) * i) % p.members
            x = i * self.hp + p.me // self.gs
            for side in range(2):
                frm = p.seq_of(side, m)
                slot = 2 * v + side
                away = (x != p.dp).astype(jnp.int32) + (frm != p.me).astype(jnp.int32)

                @pl.when(away > 0)
                def _():
                    send(
                        self.buf.at[0, 0], self.last.at[slot], self.s2.at[0], self.r2.at[slot], (x, frm)
                    ).wait_recv()

    def total(self, v):
        return self.last[2 * v].astype(F32) + self.last[2 * v + 1].astype(F32)

    def finish(self):
        for j in range(1, self.place.parts):
            self.share(j).wait_send()
        for k in range(self.gs):
            self.deliver(k, lambda c: c.wait_send(), False)


def cols_scratch(parts, rows, width):
    return [
        VMEM((parts, 2, rows, width), BF16), VMEM((parts, 2, rows, width), BF16), VMEM((rows, width), BF16),
        DMA((parts,)), DMA((parts,)), DMA, DMA,
    ]


class Cols:
    def __init__(self, place, scratch):
        self.place = place
        self.buf, self.land, self.last, self.s1, self.r1, self.s2, self.r2 = scratch

    def put(self, i, val):
        p = self.place
        cols = val.shape[1] // p.parts
        val = val.astype(BF16)
        for x in range(p.parts):
            self.buf[x, i, : val.shape[0], :cols] = val[:, x * cols : (x + 1) * cols]

    def share(self, j):
        p = self.place
        x = (p.dp + j) % p.parts
        return send(self.buf.at[x], self.land.at[p.dp], self.s1.at[j], self.r1.at[p.dp], (x, p.me))

    def cross(self):
        p = self.place
        return send(self.buf.at[p.dp, 1 - p.side], self.last, self.s2, self.r2, p.partner)

    def first(self):
        for j in range(1, self.place.parts):
            self.share(j).start()

    def second(self):
        p = self.place
        for j in range(1, p.parts):
            x = (p.dp + j) % p.parts
            send(self.buf.at[x], self.land.at[x], self.s1.at[j], self.r1.at[x], (x, p.me)).wait_recv()
        for i in range(2):
            val = self.buf[p.dp, i].astype(F32)
            for j in range(1, p.parts):
                val = val + self.land[(p.dp + j) % p.parts, i].astype(F32)
            self.buf[p.dp, i] = val.astype(BF16)
        self.cross().start()

    def total(self):
        self.cross().wait_recv()
        p = self.place
        return self.buf[p.dp, p.side].astype(F32) + self.last[...].astype(F32)

    def finish(self):
        for j in range(1, self.place.parts):
            self.share(j).wait_send()
        self.cross().wait_send()


def chip_rows(ref, chip, base=0):
    val = ref[pl.ds(base + 2 * chip, 2)]
    return val.reshape(-1, val.shape[-1])


def chip_put(ref, chip, val, base=0):
    ref[pl.ds(base + 2 * chip, 2)] = val.astype(ref.dtype).reshape((2,) + ref.shape[1:])


def ids_at(positions, ends):
    total = (positions >= ends[0]).astype(jnp.int32)
    for end in ends[1:]:
        total = total + (positions >= end).astype(jnp.int32)
    return total


def log2(n):
    assert n & (n - 1) == 0
    return n.bit_length() - 1


QB = 256
LANES = 128


def layer_kernel(
    shards, size, ff, parts,
    counts_ref, x_ref, ct_ref, gain_ref, nbias_ref, abias_ref, dbias_ref, bu_ref, wout_hbm, wu_hbm, wd_hbm, w_hbm,
    out_ref, sg_ref, qkv_ref, gout_ref, gab_ref, ggain_ref, gshift_ref, up_ref, gub_ref, gdown_ref, gdb_ref,
    pool, h_buf, m_buf, part2, x_buf, ct_buf, mid_buf, gmid_buf, qkv_buf, att_buf, att_b, att_land, lse_buf, mine_buf,
    act_buf, ghid_buf, gatt_buf, dk_acc, dv_acc, pre_buf, pre_land, wq_buf, wout_buf, wo_buf, wu_buf, wd_buf, row_buf,
    vec_buf, vec_land, bias_buf, bias_land, out_buf, out_land,
    ex_s, ex_r, att_s, att_r, pre_s, pre_r, vec_s, vec_r, bias_s, bias_r, loc, *rest,
):
    p = Place(shards, parts)
    me, dp, side, m = p.me, p.dp, p.side, p.m
    bar = pltpu.get_barrier_semaphore()
    for dev in p.others():
        pl.semaphore_signal(bar, inc=1, device_id=dev, device_id_type=MESH)
    rows, width = x_ref.shape[1:]
    members, half = p.members, p.half
    own = 2 * rows
    total = members * own
    sp = wo_buf.shape[0] // 2
    fp = wu_buf.shape[0] // 2
    units = [p.seq_of(i, m) for i in range(2)]

    span = (ff + 15) // 16 * 16 + 16
    windows = [u * ff // 16 * 16 - 16 * (u // (shards - 1)) for u in units]
    load_w0 = pltpu.make_async_copy(w_hbm, pool, loc.at[0])
    load_out = pltpu.make_async_copy(wout_hbm, wout_buf, loc.at[1])
    loads = [
        pltpu.make_async_copy(
            hbm.at[pl.ds(pl.multiple_of(windows[i], 16), span)], buf.at[pl.ds(i * fp, span)], loc.at[2 + 2 * i + j]
        )
        for j, (hbm, buf) in enumerate(((wu_hbm, wu_buf), (wd_hbm, wd_buf)))
        for i in range(2)
    ]
    load_w0.start()
    load_out.start()
    for c in loads:
        c.start()
    factor = 1.0 / math.sqrt(size)
    at_part, at_h2, at_gy = 0, members, 2 * members
    gat1 = Gather(p, h_buf, 0, rest[0:4])
    gaty = Gather(p, pool, at_gy, rest[4:8])
    gat = Gather(p, pool, at_h2, rest[8:12])
    gat2 = Gather(p, m_buf, 0, rest[12:16])
    sca = Scatter(p, pool, at_part, rest[16:22])
    sca2 = Scatter(p, part2, 0, rest[22:28])
    g_up = Rows(p, rest[28:36])
    g_qkv = Rows(p, rest[36:44])
    g_down = Cols(p, rest[44:51])
    g_out = Cols(p, rest[51:58])

    ends = [counts_ref[side, 0]]
    for i in range(1, counts_ref.shape[1]):
        ends.append(ends[-1] + counts_ref[side, i])

    def ids_of(t):
        mem = lax.shift_right_logical(t, log2(own))
        rho = lax.shift_right_logical(t, log2(rows)) & 1
        sig = rho + side - 2 * rho * side
        seq = sig * members + ((mem + (members // 2) * sig) & (members - 1))
        return ids_at(seq * rows + (t & (rows - 1)), ends)

    def iota(shape, dim):
        return lax.broadcasted_iota(jnp.int32, shape, dim)

    valid = (ids_of(iota((own, 1), 0) + m * own) < counts_ref.shape[1]).astype(F32)

    def swap(src, dst, i):
        return send(src, dst, ex_s.at[i], ex_r.at[i], p.partner)

    def norm_one(g):
        normed, _ = normalize(x_buf[g].astype(F32))
        h_buf[m, g] = (normed * gain_ref[0:1] + nbias_ref[0:1]).astype(BF16)

    x_buf[0] = x_ref[side]
    norm_one(0)
    pl.semaphore_wait(bar, len(p.others()))
    swap_x = swap(x_ref.at[1 - side], x_buf.at[1], 0)
    swap_ct = swap(ct_ref.at[1 - side], ct_buf, 1)
    swap_x.start()
    gat1.start(0)
    swap_ct.start()

    def iota2(shape):
        return iota(shape, 0), iota(shape, 1)

    def one_hot(hit, kind):
        return jnp.where(hit, 1.0, 0.0).astype(kind)

    at, lane = iota2((width, sp))
    pick = [jnp.logical_and(at == lane + u * size, lane < size) for u in units]
    exact = lax.dot_general(
        abias_ref[...], jnp.concatenate([one_hot(h, F32) for h in pick], axis=1), (((1,), (0,)), ((), ())),
        preferred_element_type=F32, precision=lax.Precision.HIGHEST,
    )
    row_buf[...] = jnp.zeros(row_buf.shape, F32)
    row_buf[0:1, : 2 * sp] = exact[0:1]
    row_buf[0:1, 4 * sp : 6 * sp] = exact[1:2]
    for i in range(2):
        row_buf[1:2, i * fp : i * fp + ff] = bu_ref[i]
    pick = jnp.concatenate([one_hot(h, BF16) for h in pick], axis=1)
    load_w0.wait()
    per_w = width // own
    for c in range(3):
        w = pool[c * per_w : (c + 1) * per_w].reshape(width, width)
        wq_buf[:, 2 * c * sp : 2 * (c + 1) * sp] = dot(w, pick).astype(BF16)
    swap_x.wait_recv()
    norm_one(1)
    gat1.start(1)
    pool[at_gy + m, 0] = (ct_ref[side].astype(F32) * valid[:rows]).astype(BF16)
    swap_ct.wait_recv()
    pool[at_gy + m, 1] = (ct_buf[...].astype(F32) * valid[rows:]).astype(BF16)
    load_out.wait()
    at, lane = iota2((sp, width))
    for i in range(2):
        hit = jnp.logical_and(lane == at + units[i] * size, at < size)
        wo_buf[i * sp : (i + 1) * sp] = dot(one_hot(hit, BF16), wout_buf[...]).astype(BF16)
    for c in loads:
        c.wait()
    at, lane = iota2((fp, span))
    for i in range(2):
        hit = jnp.logical_and(lane == at + (units[i] * ff - windows[i]), at < ff)
        for buf in (wu_buf, wd_buf):
            cut = dot(one_hot(hit, BF16), buf[i * fp : i * fp + span])
            buf[i * fp : (i + 1) * fp] = cut.astype(BF16)

    def project(chip):
        out = dot(chip_rows(h_buf, chip), wq_buf[...]) + row_buf[0:1, : 6 * sp]
        out = jnp.concatenate([out[:, : 2 * sp] * factor, out[:, 2 * sp :]], axis=1)
        chip_put(qkv_buf, chip, out)

    for k in range(1, half + 1):
        gat1.hop(k)
        gat1.ready(k - 1)
        if k == half - 1:
            gaty.start_both()
        for chip in gat1.blocks(k - 1):
            project(chip)
    gat1.ready(half)
    project(p.at(half, 0))

    qn = QB // own

    def att_copy(to):
        return send(att_b.at[to], att_land.at[m], att_s.at[to], att_r.at[m], p.dev(to))

    def lanes_of(part, i):
        return slice((2 * part + i) * sp, (2 * part + i + 1) * sp)

    row_ids = ids_of(iota((1, total), 1))

    def attend(b):
        query_ids = ids_of(iota((QB, 1), 0) + b * QB)
        same = query_ids == row_ids
        for i in range(2):
            query = qkv_buf[pl.ds(b * qn, qn), :, :, lanes_of(0, i)].reshape(QB, sp)
            keys = qkv_buf[:, :, :, lanes_of(1, i)].reshape(total, sp)
            values = qkv_buf[:, :, :, lanes_of(2, i)].reshape(total, sp)
            scores = jnp.where(same, dot(query, keys, 1, 1), NEG)
            high = jnp.max(scores, axis=-1, keepdims=True)
            weights = jnp.exp(scores - high)
            sums = jnp.sum(weights, axis=-1, keepdims=True)
            out = (dot(weights.astype(BF16), values) / sums).reshape(qn, 2, rows, sp)
            att_buf[pl.ds(b * qn, qn), :, :, i * sp : (i + 1) * sp] = out
            att_b[pl.ds(b * qn, qn), :, :, i * sp : (i + 1) * sp] = out.astype(BF16)
            lse = jnp.broadcast_to(high + jnp.log(sums), (QB, LANES))
            lse_buf[i, b] = jnp.transpose(lse)[0:8]
        for t in range(qn):
            to = b * qn + t

            @pl.when(to != m)
            def _():
                att_copy(to).start()

    blocks = total // QB
    pl.loop(0, blocks // 2)(attend)
    gaty.hop(1)
    pl.loop(blocks // 2, blocks)(attend)
    for k in range(2, half + 1):
        gaty.hop(k)
    att_land[m] = att_b[m]
    for j in range(1, members):
        frm = (m + members - j) % members
        send(att_b.at[frm], att_land.at[frm], att_s.at[frm], att_r.at[frm], p.dev(frm)).wait_recv()
    for j in range(members):
        for i in range(2):
            at = p.seq_of(i, j) * size
            mine_buf[:, at : at + size] = att_land[j].reshape(own, 2 * sp)[:, i * sp : i * sp + size]
    inputs = x_buf[...].reshape(own, width).astype(F32)
    mid = inputs + dot(mine_buf[:, :width], wout_buf[...]) + abias_ref[2:3]
    mid_buf[...] = mid
    normed, _ = normalize(mid)
    pool[at_h2 + m] = (normed * gain_ref[1:2] + nbias_ref[1:2]).astype(BF16).reshape(2, rows, width)
    gat.start_both()

    def forward(chip):
        hidden = dot(chip_rows(pool, chip, at_h2), wu_buf[...], 1, 1) + row_buf[1:2, : 2 * fp]
        act, slope = gelu_both(hidden)
        chip_put(act_buf, chip, act)
        ghid = (dot(chip_rows(pool, chip, at_gy), wd_buf[...], 1, 1) * slope).astype(BF16)
        chip_put(ghid_buf, chip, ghid)
        chip_put(pool, chip, dot(ghid, wu_buf[...]), at_part)

    for k in range(half + 1):
        if k < half:
            gat.hop(k + 1)
        gaty.ready(k)
        gat.ready(k)
        for d, chip in enumerate(gat.blocks(k)):
            forward(chip)
            sca.give(k, d)

    def flat(val):
        return val.reshape(total, val.shape[-1])

    for h in range(half):
        sca.hop(h)
        if h == 0:
            gdown = dot(flat(act_buf[...]), flat(pool[at_gy : at_gy + members]), 0, 0)
            for i in range(2):
                g_down.put(i, gdown[i * fp : i * fp + (ff + 15) // 16 * 16])
            g_down.first()
    gup = dot(flat(ghid_buf[...]), flat(pool[at_h2 : at_h2 + members]), 0, 0)
    main, left = ff // LANES * LANES, ff % LANES
    low = (size + 15) // 16 * 16
    for i in range(2):
        tall = jnp.transpose(gup[i * fp : i * fp + main]).astype(BF16)
        flat_left = gup[i * fp + main : i * fp + main + (left + 15) // 16 * 16].astype(BF16)
        for s in range(shards):
            g_up.put(i, s, slice(0, size), slice(0, main), tall[s * size : (s + 1) * size])
            if left:
                g_up.put(i, s, slice(low, low + flat_left.shape[0]), slice(0, size), flat_left[:, s * size : (s + 1) * size])
    g_up.first()
    grad_h2 = sca.result()
    normed, scale = normalize(mid_buf[...])
    gy_own = pool[at_gy + m].reshape(own, width).astype(F32)
    gmid = gy_own + norm_back(grad_h2, normed, scale, gain_ref[1:2])
    gmid_buf[...] = gmid
    m_buf[m] = gmid.astype(BF16).reshape(2, rows, width)
    gat2.start_both()

    def over_rows(val):
        return jnp.sum(val, axis=0, keepdims=True)

    gain_two, shift_two, bias_out, bias_down = (
        over_rows(grad_h2 * normed), over_rows(grad_h2), over_rows(gmid), over_rows(gy_own)
    )
    bias_up = over_rows(flat(ghid_buf[...]).astype(F32))

    def down_part(chip):
        chip_put(part2, chip, dot(chip_rows(act_buf, chip), wd_buf[...]))

    def back(chip):
        block = chip_rows(m_buf, chip)
        chip_put(gatt_buf, chip, dot(block, wo_buf[...], 1, 1))
        return dot(chip_rows(att_b, chip), block, 0, 0)

    gout = None
    for k in range(half + 1):
        for d, chip in enumerate(gat.blocks(k)):
            down_part(chip)
            sca2.give(k, d)
        if k < half:
            gat2.hop(k + 1)
        gat2.ready(k)
        for chip in gat2.blocks(k):
            more = back(chip)
            gout = more if gout is None else gout + more
    for i in range(2):
        g_out.put(i, gout[i * sp : i * sp + low])
    g_out.first()
    for x in (gat, gaty, sca):
        x.finish()
    load_w = pltpu.make_async_copy(w_hbm, pool, loc.at[0])
    load_w.start()
    sca2.hop(0)
    g_down.second()

    col_ids = ids_of(iota((total, 1), 0))

    def pre_copy(i, j):
        to = (m + j) % members
        return send(pre_buf.at[i, to], pre_land.at[i, m], pre_s.at[i, j], pre_r.at[i, m], p.dev(to))

    pre_buf[:, :, :, :, 3 * size :] = jnp.zeros(pre_buf.shape[:4] + (pre_buf.shape[4] - 3 * size,), BF16)
    bias_buf[...] = jnp.zeros(bias_buf.shape, F32)
    for i in range(2):
        dk_acc[...] = jnp.zeros(dk_acc.shape, F32)
        dv_acc[...] = jnp.zeros(dv_acc.shape, F32)
        own_lanes = slice(i * sp, (i + 1) * sp)

        def attend_back(b):
            blk = pl.ds(b * qn, qn)
            query = qkv_buf[blk, :, :, lanes_of(0, i)].reshape(QB, sp)
            keys = qkv_buf[:, :, :, lanes_of(1, i)].reshape(total, sp)
            values = qkv_buf[:, :, :, lanes_of(2, i)].reshape(total, sp)
            grad = gatt_buf[blk, :, :, own_lanes].reshape(QB, sp)
            att = att_buf[blk, :, :, own_lanes].reshape(QB, sp)
            delta = jnp.sum(grad.astype(F32) * att, axis=-1, keepdims=True)
            delta = jnp.transpose(jnp.broadcast_to(delta, (QB, LANES)))[0:1]
            same = col_ids == ids_of(iota((1, QB), 1) + b * QB)
            probs = jnp.exp(jnp.where(same, dot(keys, query, 1, 1), NEG) - lse_buf[i, b][0:1])
            grad_scores = (probs * (dot(values, grad, 1, 1) - delta)).astype(BF16)
            dv_acc[...] += dot(probs.astype(BF16), grad)
            dk_acc[...] += dot(grad_scores, query)
            dq = (dot(grad_scores, keys, 0, 0) * factor).astype(BF16)
            pre_buf[i, blk, :, :, :size] = dq[:, :size].reshape(qn, 2, rows, size)
            bias_buf[i, 0:1] += over_rows(dq.astype(F32))

        for b in range(blocks):
            attend_back(b)
        dk = dk_acc[...].astype(BF16)
        dv = dv_acc[...].astype(BF16)
        bias_buf[i, 1:2] = over_rows(dv.astype(F32))
        for j in range(fp // LANES):
            bias_buf[i, 2 + j : 3 + j] = bias_up[:, i * fp + j * LANES : i * fp + (j + 1) * LANES]
        pre_buf[i, :, :, :, size : 2 * size] = dk[:, :size].reshape(members, 2, rows, size)
        pre_buf[i, :, :, :, 2 * size : 3 * size] = dv[:, :size].reshape(members, 2, rows, size)
        for j in range(1, members):
            pre_copy(i, j).start()
        if i == 0:
            for h in range(1, half):
                sca2.hop(h)
            g_up.second()
            g_out.second()

    for i in range(2):
        grad = dot(pre_buf[i].reshape(total, pre_buf.shape[4]), flat(h_buf[...]), 0, 0)
        grad = jnp.transpose(grad).astype(BF16)
        for s in range(shards):
            g_qkv.put(i, s, slice(0, size), slice(0, grad.shape[1]), grad[s * size : (s + 1) * size])
    g_qkv.first()

    def bias_copy(x, i):
        to = ((dp + x) % parts, p.seq_of(i, m))
        return send(
            bias_buf.at[i], bias_land.at[side * parts + dp], bias_s.at[x, i], bias_r.at[side * parts + dp], to
        )

    for x in range(parts):
        for i in range(2):
            if x > 0:
                bias_copy(x, i).start()
            else:

                @pl.when(side != i)
                def _():
                    bias_copy(0, i).start()

    down = sca2.result()
    out = ((mid_buf[...] + down + dbias_ref[...]) * valid).astype(BF16)
    out_ref[side] = out[:rows]
    out_buf[0] = out[rows:]
    swap_out = swap(out_buf.at[0], out_land.at[0], 2)
    swap_out.start()
    load_w.wait()
    for i in range(2):
        for j in range(1, members):
            frm = (m + members - j) % members
            send(pre_buf.at[i, frm], pre_land.at[i, frm], pre_s.at[i, j], pre_r.at[i, frm], p.dev(frm)).wait_recv()
        pre_land[i, m] = pre_buf[i, m]
        for j in range(members):
            block = pre_land[i, j].reshape(own, pre_land.shape[4])
            for c in range(3):
                at = c * width + p.seq_of(i, j) * size
                mine_buf[:, at : at + size] = block[:, c * size : (c + 1) * size]
    grad_h1 = None
    for c in range(3):
        w = pool[c * per_w : (c + 1) * per_w].reshape(width, width)
        more = dot(mine_buf[:, c * width : (c + 1) * width], w, 1, 1)
        grad_h1 = more if grad_h1 is None else grad_h1 + more
    normed, scale = normalize(x_buf[...].reshape(own, width).astype(F32))
    sg = (gmid_buf[...] + norm_back(grad_h1, normed, scale, gain_ref[0:1])).astype(BF16)
    out_buf[1] = sg[rows:]
    swap_sg = swap(out_buf.at[1], out_land.at[1], 3)
    swap_sg.start()
    sg_ref[side] = sg[:rows]
    vecs = jnp.concatenate(
        [over_rows(grad_h1 * normed), gain_two, over_rows(grad_h1), shift_two, bias_out, bias_down, bias_out, bias_out],
        axis=0,
    )
    for s in range(shards):
        vec_buf[s, :, :size] = vecs[:, s * size : (s + 1) * size]
    per = shards // parts
    pairs = [(i, j) for i in range(parts) for j in range(shards) if i + j > 0]

    def vec_copy(i, j):
        to = (me + j) % shards
        slot = dp * shards + me
        return send(vec_buf.at[to], vec_land.at[slot], vec_s.at[i, j], vec_r.at[slot], ((dp + i) % parts, to))

    def vec_wait(i, j):
        frm = (me + j) % shards
        x = (dp + i) % parts
        slot = x * shards + frm
        send(vec_buf.at[0], vec_land.at[slot], vec_s.at[i, j], vec_r.at[slot], (x, frm)).wait_recv()

    for i, j in pairs:
        vec_copy(i, j).start()
    vec_land[dp * shards + me] = vec_buf[me]
    g_qkv.second()

    cols = width // parts
    gdown_ref[...] = g_down.total()[:ff, :cols]
    gout_ref[...] = g_out.total()[:size, :cols]
    g_up.third()
    for v in range(per):
        acc = g_up.total(v)
        up_ref[:, v * ff : v * ff + main] = acc[:size, :main]
        if left:
            tail = jnp.transpose(acc[low:, :LANES])
            up_ref[:, v * ff + main : (v + 1) * ff] = tail[:size, :left]
    bias_land[side * parts + dp] = bias_buf[side]
    for s in range(2):
        for x in range(parts):
            slot = s * parts + x
            away = (side != s).astype(jnp.int32) + (dp != x).astype(jnp.int32)

            @pl.when(away > 0)
            def _():
                send(
                    bias_buf.at[0], bias_land.at[slot], bias_s.at[0, 0], bias_r.at[slot], (x, p.seq_of(s, m))
                ).wait_recv()

    acc = bias_land[0]
    for i in range(1, 2 * parts):
        acc = acc + bias_land[i]
    gab_ref[0:2] = acc[0:2, :size]
    for j in range(fp // LANES):
        n = min(LANES, ff - j * LANES)
        gub_ref[:, j * LANES : j * LANES + n] = acc[2 + j : 3 + j, :n]
    g_qkv.third()
    for v in range(per):
        acc = g_qkv.total(v)
        for c in range(3):
            qkv_ref[c, :, v * size : (v + 1) * size] = acc[:size, c * size : (c + 1) * size]
    swap_out.wait_recv()
    out_ref[1 - side] = out_land[0]
    swap_sg.wait_recv()
    sg_ref[1 - side] = out_land[1]
    for i, j in pairs:
        vec_wait(i, j)
    acc = vec_land[0]
    for i in range(1, shards * parts):
        acc = acc + vec_land[i]
    ggain_ref[...] = acc[0:2, :size]
    gshift_ref[...] = acc[2:4, :size]
    gab_ref[2:3] = acc[4:5, :size]
    gdb_ref[...] = acc[5:6, :size]

    for c in (swap_x, swap_ct, swap_out, swap_sg):
        c.wait_send()
    for j in range(1, members):
        att_copy((m + j) % members).wait_send()
        for i in range(2):
            pre_copy(i, j).wait_send()
    for x in range(parts):
        for i in range(2):
            if x > 0:
                bias_copy(x, i).wait_send()
            else:

                @pl.when(side != i)
                def _():
                    bias_copy(0, i).wait_send()

    for i, j in pairs:
        vec_copy(i, j).wait_send()
    for x in (gat1, gat2, sca2, g_up, g_qkv, g_down, g_out):
        x.finish()


def layer(shards, size, ff, parts, counts, states, cotangent, gains, nbias, abias, dbias, bu, w_out, w_up, w_down, w_qkv):
    rows, width = states.shape[1:]
    members = shards // 2
    n = members // 2
    sp, fp = up128(size), up128(ff)
    own = 2 * rows
    total = members * own
    per = shards // parts
    cols = width // parts
    r16 = lambda k: -(-k // 16) * 16
    sds = jax.ShapeDtypeStruct
    block = (members, 2, rows)
    wp = up128(3 * size)
    w4 = w_qkv.reshape(3 * width // own, 2, rows, width)
    up_rows = r16(size) + r16(ff % LANES)
    return pl.pallas_call(
        functools.partial(layer_kernel, shards, size, ff, parts),
        out_shape=[
            sds((2, rows, width), BF16), sds((2, rows, width), BF16), sds((3, size, per * size), F32),
            sds((size, cols), F32), sds((3, size), F32), sds((2, size), F32), sds((2, size), F32),
            sds((size, per * ff), F32), sds((1, ff), F32), sds((ff, cols), F32), sds((1, size), F32),
        ],
        in_specs=[pl.BlockSpec(memory_space=pltpu.SMEM)]
        + [pl.BlockSpec(memory_space=VMEM)] * 7
        + [pl.BlockSpec(memory_space=pl.ANY)] * 4,
        out_specs=[pl.BlockSpec(memory_space=VMEM)] * 11,
        scratch_shapes=[
            VMEM(w4.shape, BF16), VMEM(block + (width,), BF16), VMEM(block + (width,), BF16), VMEM(block + (width,), BF16),
            VMEM((2, rows, width), BF16), VMEM((rows, width), BF16), VMEM((own, width), F32), VMEM((own, width), F32),
            VMEM(block + (6 * sp,), BF16), VMEM(block + (2 * sp,), F32), VMEM(block + (2 * sp,), BF16),
            VMEM(block + (2 * sp,), BF16), VMEM((2, total // QB, 8, QB), F32), VMEM((own, 3 * width), BF16),
            VMEM(block + (2 * fp,), BF16), VMEM(block + (2 * fp,), BF16), VMEM(block + (2 * sp,), BF16),
            VMEM((total, sp), F32), VMEM((total, sp), F32), VMEM((2,) + block + (wp,), BF16), VMEM((2,) + block + (wp,), BF16),
            VMEM((width, 6 * sp), BF16), VMEM(w_out.shape, BF16), VMEM((2 * sp, width), BF16), VMEM((2 * fp, width), BF16),
            VMEM((2 * fp, width), BF16),
            VMEM((2, max(6 * sp, 2 * fp)), F32),
            VMEM((shards, 8, LANES), F32), VMEM((shards * parts, 8, LANES), F32), VMEM((2, 8, LANES), F32),
            VMEM((2 * parts, 8, LANES), F32), VMEM((2, rows, width), BF16),
            VMEM((2, rows, width), BF16),
            DMA((4,)), DMA((4,)), DMA((members,)), DMA((members,)), DMA((2, members)), DMA((2, members)),
            DMA((parts, shards)), DMA((parts * shards,)), DMA((parts, 2)), DMA((2 * parts,)), DMA((6,)),
        ]
        + gather_sems(n) * 4
        + scatter_scratch(n, rows, width) * 2
        + rows_scratch(shards, parts, up_rows, ff // LANES * LANES)
        + rows_scratch(shards, parts, r16(size), wp)
        + cols_scratch(parts, r16(ff), up128(cols))
        + cols_scratch(parts, r16(size), up128(cols)),
        name="layer",
        compiler_params=pltpu.CompilerParams(
            collective_id=0, has_side_effects=True, vmem_limit_bytes=63 << 20
        ),
    )(counts, states, cotangent, gains, nbias, abias, dbias, bu, w_out, w_up, w_down, w4)


def deliver_kernel(*refs):
    count = len(refs) // 2
    for i in range(count):
        refs[count + i][...] = refs[i][...]


def deliver(*arrays):
    return pl.pallas_call(
        deliver_kernel,
        out_shape=[jax.ShapeDtypeStruct(x.shape, x.dtype) for x in arrays],
        in_specs=[pl.BlockSpec(memory_space=VMEM)] * len(arrays),
        out_specs=[pl.BlockSpec(memory_space=VMEM)] * len(arrays),
        name="deliver",
    )(*arrays)


def body(
    states, counts, cotangent, w_qkv, w_out, attn_bias, norm_gain, norm_bias,
    w_up, up_bias, w_down, down_bias,
):
    width = states.shape[2]
    shards = lax.axis_size("seq")
    parts = lax.axis_size("dp")
    size = width // HEADS
    ff = w_up.shape[1] // shards
    members = shards // 2
    me = lax.axis_index("seq")
    m = (me + (members // 2) * (me // members)) % members
    units = (m, members + (m + members // 2) % members)

    def mine(x, axis, count):
        return jnp.stack([lax.dynamic_slice_in_dim(x, u * count, count, axis) for u in units])

    layer_out, state_grad, g_qkv, g_out, g_ab, g_gain, g_shift, g_up, g_ub, g_down, g_db = deliver(
        *layer(
            shards, size, ff, parts, counts, states, cotangent, norm_gain, norm_bias, attn_bias, down_bias[None],
            mine(up_bias[None], 1, ff), w_out, w_up.T, w_down, w_qkv,
        )
    )
    return (
        layer_out, state_grad, g_qkv, g_out, g_ab, g_gain, g_shift, g_up,
        g_ub.reshape(ff), g_down, g_db.reshape(size),
    )


def solution(mesh):
    placed = (P("dp", "seq", None), P("dp", None), P("dp", "seq", None)) + (P(),) * 9
    return jax.shard_map(
        body,
        mesh=mesh,
        in_specs=placed,
        out_specs=(
            P("dp", "seq", None), P("dp", "seq", None), P(None, "seq", "dp"), P("seq", "dp"),
            P(None, "seq"), P(None, "seq"), P(None, "seq"), P("seq", "dp"), P("seq"),
            P("seq", "dp"), P("seq"),
        ),
        check_vma=False,
    )
```

```python
import functools
import math

import jax
import jax.numpy as jnp
from jax import lax
from jax.experimental import pallas as pl
from jax.experimental.pallas import tpu as pltpu
from jax.sharding import PartitionSpec as P

HEADS = 16
EPS = 1e-06
NEG = -1e30
F32 = jnp.float32
BF16 = jnp.bfloat16
MESH = pl.DeviceIdType.MESH
VMEM = pltpu.VMEM
DMA = pltpu.SemaphoreType.DMA


def mm(spec, a, b):
    return jnp.einsum(spec, a, b, preferred_element_type=F32)


def dot(a, b, ca=1, cb=0):
    return lax.dot_general(a, b, (((ca,), (cb,)), ((), ())), preferred_element_type=F32)


def pad_to(x, axis, size):
    pads = [(0, 0)] * x.ndim
    pads[axis] = (0, size - x.shape[axis])
    return jnp.pad(x, pads)


def up128(n):
    return -(-n // 128) * 128


def normalize(values):
    mean = jnp.mean(values, axis=-1, keepdims=True)
    centred = values - mean
    scale = lax.rsqrt(jnp.mean(centred * centred, axis=-1, keepdims=True) + EPS)
    return (centred * scale, scale)


def norm_back(grad_norm, normed, scale, gain):
    scaled = grad_norm * gain
    return scale * (
        scaled
        - jnp.mean(scaled, axis=-1, keepdims=True)
        - normed * jnp.mean(scaled * normed, axis=-1, keepdims=True)
    )


def gelu_both(v):
    c, a = 0.7978845608028654, 0.044715
    sq = v * v
    t = jnp.tanh(c * (v + a * v * sq))
    half = 0.5 * (1.0 + t)
    return v * half, half + 0.5 * v * (1.0 - t * t) * (c * (1.0 + 3.0 * a * sq))


def send(src, dst, s, r, dev):
    return pltpu.make_async_remote_copy(
        src_ref=src, dst_ref=dst, send_sem=s, recv_sem=r, device_id=dev, device_id_type=MESH
    )


class Place:
    def __init__(self, shards, parts):
        self.shards, self.parts = shards, parts
        self.members = shards // 2
        self.n = self.members // 2
        self.half = self.n // 2
        self.me = lax.axis_index("seq")
        self.dp = lax.axis_index("dp")
        self.side = self.me // self.members
        self.m = (self.me + (self.members // 2) * self.side) % self.members
        self.chip = self.m // 2
        self.core = self.m % 2
        odd = self.chip % 2
        self.pos = (1 - odd) * (self.chip // 2) + odd * (self.n - 1 - self.chip // 2)
        self.to = (self.at(1, 1) * 2 + self.core, self.at(1, 0) * 2 + self.core)
        self.sib = self.chip * 2 + 1 - self.core
        self.partner = {"seq": self.seq_of(1 - self.side, self.m)}

    def seq_of(self, side, m):
        return side * self.members + (m + (self.members // 2) * side) % self.members

    def dev(self, m):
        return {"seq": self.seq_of(self.side, m)}

    def at(self, k, d):
        p = (self.pos + (self.n - k if d == 0 else k)) % self.n
        hi = p // self.half
        return (1 - hi) * 2 * p + hi * (2 * (self.n - 1 - p) + 1)

    def others(self):
        return [
            ((self.dp + i) % self.parts, (self.me + j) % self.shards)
            for i in range(self.parts) for j in range(self.shards) if i + j > 0
        ]


def gather_sems(n):
    return [DMA((2, n // 2 + 1, 2))] * 4


class Gather:
    def __init__(self, place, buf, base, sems):
        self.place, self.buf, self.base = place, buf, base
        self.ring_s, self.ring_r, self.sib_s, self.sib_r = sems
        self.sent = []

    def copy(self, k, d, g, to_sib):
        p = self.place
        block = self.buf.at[self.base + p.at(k, d) * 2 + p.core, g]
        s, r = (self.sib_s, self.sib_r) if to_sib else (self.ring_s, self.ring_r)
        return send(block, block, s.at[d, k, g], r.at[d, k, g], p.dev(p.sib if to_sib else p.to[d]))

    def go(self, *args):
        c = self.copy(*args)
        c.start()
        self.sent.append(c)

    def units(self, k):
        if k == self.place.half:
            return [(0, 0), (1, 1)]
        return [(0, 0), (1, 1), (0, 1), (1, 0)]

    def passes(self, k, d, g):
        return k < self.place.half - 1 or (k == self.place.half - 1 and g == d)

    def start(self, g):
        for d in (g, 1 - g):
            if self.passes(0, d, g):
                self.go(0, d, g, False)
        self.go(0, g, g, True)

    def start_both(self):
        for d, g in self.units(0):
            if self.passes(0, d, g):
                self.go(0, d, g, False)
        for g in range(2):
            self.go(0, g, g, True)

    def hop(self, k):
        for d, g in self.units(k):
            self.copy(k - 1, d, g, False).wait_recv()
            if self.passes(k, d, g):
                self.go(k, d, g, False)
            self.go(k, d, g, True)

    def ready(self, k):
        for d, g in self.units(k):
            if k > 0 or d == g:
                self.copy(k, d, g, True).wait_recv()

    def blocks(self, k):
        if k == 0 or k == self.place.half:
            return [self.place.at(k, 0)]
        return [self.place.at(k, 0), self.place.at(k, 1)]

    def finish(self):
        for c in self.sent:
            c.wait_send()


def scatter_scratch(n, rows, width):
    return [
        VMEM((n, 2, rows, width), BF16), VMEM((2, n // 2, 2, rows, width), BF16),
        DMA((n,)), DMA((n,)), DMA((2, n // 2, 2)), DMA((2, n // 2, 2)),
    ]


class Scatter:
    def __init__(self, place, part, base, scratch):
        self.place, self.part, self.base = place, part, base
        self.sib_land, self.land, self.sib_s, self.sib_r, self.ring_s, self.ring_r = scratch
        self.sent = []
        self.have = set()

    def slot(self, k, d):
        if k == 0:
            return 0
        return self.place.n - 1 if k == self.place.half else 2 * k - 1 + d

    def sib_copy(self, k, d):
        p, i = self.place, self.slot(k, d)
        src = self.part.at[self.base + p.at(k, d) * 2 + 1 - p.core]
        return send(src, self.sib_land.at[i], self.sib_s.at[i], self.sib_r.at[i], p.dev(p.sib))

    def give(self, k, d):
        c = self.sib_copy(k, d)
        c.start()
        self.sent.append(c)

    def from_sib(self, k, d):
        i = self.slot(k, d)
        if i not in self.have:
            self.have.add(i)
            self.sib_copy(k, d).wait_recv()
        return self.sib_land.at[i]

    def dist(self, h, d, g):
        return self.place.half - h if g == d else self.place.half - 1 - h

    def block(self, h, d, g):
        p = self.place
        return self.base + p.at(self.dist(h, d, g), 1 - d) * 2 + p.core

    def ring_copy(self, h, d, g):
        return send(
            self.part.at[self.block(h, d, g), g], self.land.at[d, h, g],
            self.ring_s.at[d, h, g], self.ring_r.at[d, h, g], self.place.dev(self.place.to[d]),
        )

    def hop(self, h):
        for d, g in [(0, 0), (1, 1), (0, 1), (1, 0)]:
            j = self.dist(h, d, g)
            if j == 0:
                continue
            own = self.block(h, d, g)
            val = self.part[own, g].astype(F32) + self.from_sib(j, 1 - d)[g].astype(F32)
            if h > 0:
                self.ring_copy(h - 1, d, g).wait_recv()
                val = val + self.land[d, h - 1, g].astype(F32)
            self.part[own, g] = val.astype(BF16)
            c = self.ring_copy(h, d, g)
            c.start()
            self.sent.append(c)

    def result(self):
        p = self.place
        out = []
        for g in range(2):
            val = self.part[self.base + p.m, g].astype(F32) + self.from_sib(0, 0)[g].astype(F32)
            for d in range(2):
                h = p.half - 1 if g == d else p.half - 2
                self.ring_copy(h, d, g).wait_recv()
                val = val + self.land[d, h, g].astype(F32)
            out.append(val)
        return jnp.concatenate(out, axis=0)

    def finish(self):
        for c in self.sent:
            c.wait_send()


def rows_scratch(shards, parts, rows, width):
    gh, per = shards // parts, shards // parts
    return [
        VMEM((parts, 2, gh, rows, width), BF16), VMEM((parts, 2, gh, rows, width), BF16), VMEM((gh, rows, width), BF16),
        VMEM((per, rows, width), BF16),
        DMA((parts,)), DMA((parts,)), DMA((2,)), DMA((gh,)), DMA((per,)), DMA,
    ]


class Rows:
    def __init__(self, place, scratch):
        self.place = place
        self.buf, self.land, self.met, self.last, self.s1, self.r1, self.sc, self.s2, self.r2, self.loc = scratch
        self.gh = self.buf.shape[2]
        self.hp = place.parts // 2
        self.per = place.shards // place.parts

    def put(self, i, s, rows, cols, val):
        p = self.place
        side = s // p.members
        m = p.seq_of(side, s % p.members) % p.members
        self.buf[i * self.hp + m // self.gh, side, m % self.gh, rows, cols] = val

    def share(self, j):
        p = self.place
        x = (p.dp + j) % p.parts
        return send(self.buf.at[x], self.land.at[p.dp], self.s1.at[j], self.r1.at[p.dp], (x, p.me))

    def first(self, unit=None):
        p = self.place
        for j in range(1, p.parts):
            if unit is None:
                self.share(j).start()
            else:

                @pl.when((p.dp + j) % p.parts // self.hp == unit)
                def _():
                    self.share(j).start()

    def cross(self):
        p = self.place
        return send(self.buf.at[p.dp, 1 - p.side], self.met, self.sc.at[0], self.sc.at[1], p.partner)

    def add(self, side, others):
        p = self.place
        for k in range(self.gh):
            val = self.buf[p.dp, side, k].astype(F32)
            for other in others:
                val = val + other(k).astype(F32)
            self.buf[p.dp, side, k] = val.astype(BF16)

    def second(self):
        p = self.place
        for j in range(1, p.parts):
            x = (p.dp + j) % p.parts
            send(self.buf.at[x], self.land.at[x], self.s1.at[j], self.r1.at[x], (x, p.me)).wait_recv()
        dp_copies = lambda side: [
            lambda k, j=j: self.land[(p.dp + j) % p.parts, side, k] for j in range(1, p.parts)
        ]
        self.add(1 - p.side, dp_copies(1 - p.side))
        self.cross().start()
        self.add(p.side, dp_copies(p.side))

    def deliver(self, k, act, act_own):
        p = self.place
        unit = p.seq_of(p.dp // self.hp, p.m)
        keeper = unit // self.per
        owner = (p.dp % self.hp) * self.gh + k
        slot = unit % self.per
        away = (keeper != p.dp).astype(jnp.int32) + (owner != p.m).astype(jnp.int32)
        block = self.buf.at[p.dp, p.side, k]

        @pl.when(away > 0)
        def _():
            to = (keeper, p.seq_of(p.side, owner))
            act(send(block, self.last.at[slot], self.s2.at[k], self.r2.at[slot], to))

        if act_own:

            @pl.when(away == 0)
            def _():
                c = pltpu.make_async_copy(block, self.last.at[slot], self.loc)
                c.start()
                c.wait()

    def meet(self):
        self.cross().wait_recv()
        self.add(self.place.side, [lambda k: self.met[k]])
        for k in range(self.gh):
            self.deliver(k, lambda c: c.start(), True)

    def third(self):
        p = self.place
        for v in range(self.per):
            unit = p.dp * self.per + v
            i = unit // p.members
            m = (unit + (p.members // 2) * i) % p.members
            x = i * self.hp + p.m // self.gh
            away = (x != p.dp).astype(jnp.int32) + (m != p.m).astype(jnp.int32)

            @pl.when(away > 0)
            def _():
                frm = (x, p.seq_of(p.side, m))
                send(self.buf.at[0, 0, 0], self.last.at[v], self.s2.at[0], self.r2.at[v], frm).wait_recv()

    def total(self, v):
        return self.last[v].astype(F32)

    def finish(self):
        for j in range(1, self.place.parts):
            self.share(j).wait_send()
        self.cross().wait_send()
        for k in range(self.gh):
            self.deliver(k, lambda c: c.wait_send(), False)


def cols_scratch(parts, rows, width):
    return [
        VMEM((parts, 2, rows, width), BF16), VMEM((parts, 2, rows, width), BF16), VMEM((rows, width), BF16),
        DMA((parts,)), DMA((parts,)), DMA, DMA,
    ]


class Cols:
    def __init__(self, place, scratch):
        self.place = place
        self.buf, self.land, self.last, self.s1, self.r1, self.s2, self.r2 = scratch

    def put(self, i, val):
        p = self.place
        cols = val.shape[1] // p.parts
        val = val.astype(BF16)
        for x in range(p.parts):
            self.buf[x, i, : val.shape[0], :cols] = val[:, x * cols : (x + 1) * cols]

    def share(self, j):
        p = self.place
        x = (p.dp + j) % p.parts
        return send(self.buf.at[x], self.land.at[p.dp], self.s1.at[j], self.r1.at[p.dp], (x, p.me))

    def cross(self):
        p = self.place
        return send(self.buf.at[p.dp, 1 - p.side], self.last, self.s2, self.r2, p.partner)

    def first(self):
        for j in range(1, self.place.parts):
            self.share(j).start()

    def second(self):
        p = self.place
        for j in range(1, p.parts):
            x = (p.dp + j) % p.parts
            send(self.buf.at[x], self.land.at[x], self.s1.at[j], self.r1.at[x], (x, p.me)).wait_recv()
        for i in range(2):
            val = self.buf[p.dp, i].astype(F32)
            for j in range(1, p.parts):
                val = val + self.land[(p.dp + j) % p.parts, i].astype(F32)
            self.buf[p.dp, i] = val.astype(BF16)
        self.cross().start()

    def total(self):
        self.cross().wait_recv()
        p = self.place
        return self.buf[p.dp, p.side].astype(F32) + self.last[...].astype(F32)

    def finish(self):
        for j in range(1, self.place.parts):
            self.share(j).wait_send()
        self.cross().wait_send()


def chip_rows(ref, chip, base=0):
    val = ref[pl.ds(base + 2 * chip, 2)]
    return val.reshape(-1, val.shape[-1])


def chip_put(ref, chip, val, base=0):
    ref[pl.ds(base + 2 * chip, 2)] = val.astype(ref.dtype).reshape((2,) + ref.shape[1:])


def ids_at(positions, ends):
    total = (positions >= ends[0]).astype(jnp.int32)
    for end in ends[1:]:
        total = total + (positions >= end).astype(jnp.int32)
    return total


def log2(n):
    assert n & (n - 1) == 0
    return n.bit_length() - 1


QB = 256
LANES = 128


def layer_kernel(
    shards, size, ff, parts,
    counts_ref, x_ref, ct_ref, gain_ref, nbias_ref, abias_ref, dbias_ref, bu_ref, wout_hbm, wu_hbm, wd_hbm, w_hbm,
    out_ref, sg_ref, qkv_ref, gout_ref, gab_ref, ggain_ref, gshift_ref, up_ref, gub_ref, gdown_ref, gdb_ref,
    pool, h_buf, m_buf, part2, x_buf, ct_buf, mid_buf, gmid_buf, qkv_buf, att_buf, att_b, att_land, lse_buf, mine_buf,
    act_buf, ghid_buf, gatt_buf, dk_acc, dv_acc, pre_buf, pre_land, wq_buf, wout_buf, wo_buf, wu_buf, wd_buf, row_buf,
    vec_buf, vec_land, bias_buf, bias_land, out_buf, out_land,
    ex_s, ex_r, att_s, att_r, pre_s, pre_r, vec_s, vec_r, bias_s, bias_r, loc, *rest,
):
    p = Place(shards, parts)
    me, dp, side, m = p.me, p.dp, p.side, p.m
    bar = pltpu.get_barrier_semaphore()
    for dev in p.others():
        pl.semaphore_signal(bar, inc=1, device_id=dev, device_id_type=MESH)
    rows, width = x_ref.shape[1:]
    members, half = p.members, p.half
    own = 2 * rows
    total = members * own
    sp = wo_buf.shape[0] // 2
    fp = wu_buf.shape[0] // 2
    units = [p.seq_of(i, m) for i in range(2)]

    span = (ff + 15) // 16 * 16 + 16
    windows = [u * ff // 16 * 16 - 16 * (u // (shards - 1)) for u in units]
    load_w0 = pltpu.make_async_copy(w_hbm, pool, loc.at[0])
    load_out = pltpu.make_async_copy(wout_hbm, wout_buf, loc.at[1])
    loads = [
        pltpu.make_async_copy(
            hbm.at[pl.ds(pl.multiple_of(windows[i], 16), span)], buf.at[pl.ds(i * fp, span)], loc.at[2 + 2 * i + j]
        )
        for j, (hbm, buf) in enumerate(((wu_hbm, wu_buf), (wd_hbm, wd_buf)))
        for i in range(2)
    ]
    load_w0.start()
    load_out.start()
    for c in loads:
        c.start()
    factor = 1.0 / math.sqrt(size)
    at_part, at_h2, at_gy = 0, members, 2 * members
    gat1 = Gather(p, h_buf, 0, rest[0:4])
    gaty = Gather(p, pool, at_gy, rest[4:8])
    gat = Gather(p, pool, at_h2, rest[8:12])
    gat2 = Gather(p, m_buf, 0, rest[12:16])
    sca = Scatter(p, pool, at_part, rest[16:22])
    sca2 = Scatter(p, part2, 0, rest[22:28])
    g_up = Rows(p, rest[28:38])
    g_qkv = Rows(p, rest[38:48])
    g_down = Cols(p, rest[48:55])
    g_out = Cols(p, rest[55:62])

    ends = [counts_ref[side, 0]]
    for i in range(1, counts_ref.shape[1]):
        ends.append(ends[-1] + counts_ref[side, i])

    def ids_of(t):
        mem = lax.shift_right_logical(t, log2(own))
        rho = lax.shift_right_logical(t, log2(rows)) & 1
        sig = rho + side - 2 * rho * side
        seq = sig * members + ((mem + (members // 2) * sig) & (members - 1))
        return ids_at(seq * rows + (t & (rows - 1)), ends)

    def iota(shape, dim):
        return lax.broadcasted_iota(jnp.int32, shape, dim)

    valid = (ids_of(iota((own, 1), 0) + m * own) < counts_ref.shape[1]).astype(F32)

    def swap(src, dst, i):
        return send(src, dst, ex_s.at[i], ex_r.at[i], p.partner)

    def norm_one(g):
        normed, _ = normalize(x_buf[g].astype(F32))
        h_buf[m, g] = (normed * gain_ref[0:1] + nbias_ref[0:1]).astype(BF16)

    x_buf[0] = x_ref[side]
    norm_one(0)
    pl.semaphore_wait(bar, len(p.others()))
    swap_x = swap(x_ref.at[1 - side], x_buf.at[1], 0)
    swap_ct = swap(ct_ref.at[1 - side], ct_buf, 1)
    swap_x.start()
    gat1.start(0)
    swap_ct.start()

    def iota2(shape):
        return iota(shape, 0), iota(shape, 1)

    def one_hot(hit, kind):
        return jnp.where(hit, 1.0, 0.0).astype(kind)

    at, lane = iota2((width, sp))
    pick = [jnp.logical_and(at == lane + u * size, lane < size) for u in units]
    exact = lax.dot_general(
        abias_ref[...], jnp.concatenate([one_hot(h, F32) for h in pick], axis=1), (((1,), (0,)), ((), ())),
        preferred_element_type=F32, precision=lax.Precision.HIGHEST,
    )
    row_buf[...] = jnp.zeros(row_buf.shape, F32)
    row_buf[0:1, : 2 * sp] = exact[0:1]
    row_buf[0:1, 4 * sp : 6 * sp] = exact[1:2]
    for i in range(2):
        row_buf[1:2, i * fp : i * fp + ff] = bu_ref[i]
    pick = jnp.concatenate([one_hot(h, BF16) for h in pick], axis=1)
    load_w0.wait()
    per_w = width // own
    for c in range(3):
        w = pool[c * per_w : (c + 1) * per_w].reshape(width, width)
        wq_buf[:, 2 * c * sp : 2 * (c + 1) * sp] = dot(w, pick).astype(BF16)
    swap_x.wait_recv()
    norm_one(1)
    gat1.start(1)
    pool[at_gy + m, 0] = (ct_ref[side].astype(F32) * valid[:rows]).astype(BF16)
    swap_ct.wait_recv()
    pool[at_gy + m, 1] = (ct_buf[...].astype(F32) * valid[rows:]).astype(BF16)
    load_out.wait()
    at, lane = iota2((sp, width))
    for i in range(2):
        hit = jnp.logical_and(lane == at + units[i] * size, at < size)
        wo_buf[i * sp : (i + 1) * sp] = dot(one_hot(hit, BF16), wout_buf[...]).astype(BF16)
    for c in loads:
        c.wait()
    at, lane = iota2((fp, span))
    for i in range(2):
        hit = jnp.logical_and(lane == at + (units[i] * ff - windows[i]), at < ff)
        for buf in (wu_buf, wd_buf):
            cut = dot(one_hot(hit, BF16), buf[i * fp : i * fp + span])
            buf[i * fp : (i + 1) * fp] = cut.astype(BF16)

    def project(chip):
        out = dot(chip_rows(h_buf, chip), wq_buf[...]) + row_buf[0:1, : 6 * sp]
        out = jnp.concatenate([out[:, : 2 * sp] * factor, out[:, 2 * sp :]], axis=1)
        chip_put(qkv_buf, chip, out)

    for k in range(1, half + 1):
        gat1.hop(k)
        gat1.ready(k - 1)
        if k == half - 1:
            gaty.start_both()
        for chip in gat1.blocks(k - 1):
            project(chip)
    gat1.ready(half)
    project(p.at(half, 0))

    qn = QB // own

    def att_copy(to):
        return send(att_b.at[to], att_land.at[m], att_s.at[to], att_r.at[m], p.dev(to))

    def lanes_of(part, i):
        return slice((2 * part + i) * sp, (2 * part + i + 1) * sp)

    row_ids = ids_of(iota((1, total), 1))

    def attend(b):
        query_ids = ids_of(iota((QB, 1), 0) + b * QB)
        same = query_ids == row_ids
        for i in range(2):
            query = qkv_buf[pl.ds(b * qn, qn), :, :, lanes_of(0, i)].reshape(QB, sp)
            keys = qkv_buf[:, :, :, lanes_of(1, i)].reshape(total, sp)
            values = qkv_buf[:, :, :, lanes_of(2, i)].reshape(total, sp)
            scores = jnp.where(same, dot(query, keys, 1, 1), NEG)
            high = jnp.max(scores, axis=-1, keepdims=True)
            weights = jnp.exp(scores - high)
            sums = jnp.sum(weights, axis=-1, keepdims=True)
            out = (dot(weights.astype(BF16), values) / sums).reshape(qn, 2, rows, sp)
            att_buf[pl.ds(b * qn, qn), :, :, i * sp : (i + 1) * sp] = out
            att_b[pl.ds(b * qn, qn), :, :, i * sp : (i + 1) * sp] = out.astype(BF16)
            lse = jnp.broadcast_to(high + jnp.log(sums), (QB, LANES))
            lse_buf[i, b] = jnp.transpose(lse)[0:8]
        for t in range(qn):
            to = b * qn + t

            @pl.when(to != m)
            def _():
                att_copy(to).start()

    blocks = total // QB
    pl.loop(0, blocks // 2)(attend)
    gaty.hop(1)
    pl.loop(blocks // 2, blocks)(attend)
    for k in range(2, half + 1):
        gaty.hop(k)
    att_land[m] = att_b[m]
    for j in range(1, members):
        frm = (m + members - j) % members
        send(att_b.at[frm], att_land.at[frm], att_s.at[frm], att_r.at[frm], p.dev(frm)).wait_recv()
    for j in range(members):
        for i in range(2):
            at = p.seq_of(i, j) * size
            mine_buf[:, at : at + size] = att_land[j].reshape(own, 2 * sp)[:, i * sp : i * sp + size]
    inputs = x_buf[...].reshape(own, width).astype(F32)
    mid = inputs + dot(mine_buf[:, :width], wout_buf[...]) + abias_ref[2:3]
    mid_buf[...] = mid
    normed, _ = normalize(mid)
    pool[at_h2 + m] = (normed * gain_ref[1:2] + nbias_ref[1:2]).astype(BF16).reshape(2, rows, width)
    gat.start_both()

    def forward(chip):
        hidden = dot(chip_rows(pool, chip, at_h2), wu_buf[...], 1, 1) + row_buf[1:2, : 2 * fp]
        act, slope = gelu_both(hidden)
        chip_put(act_buf, chip, act)
        ghid = (dot(chip_rows(pool, chip, at_gy), wd_buf[...], 1, 1) * slope).astype(BF16)
        chip_put(ghid_buf, chip, ghid)
        chip_put(pool, chip, dot(ghid, wu_buf[...]), at_part)

    for k in range(half + 1):
        if k < half:
            gat.hop(k + 1)
        gaty.ready(k)
        gat.ready(k)
        for d, chip in enumerate(gat.blocks(k)):
            forward(chip)
            sca.give(k, d)

    def flat(val):
        return val.reshape(total, val.shape[-1])

    for h in range(half):
        sca.hop(h)
        if h == 0:
            gdown = dot(flat(act_buf[...]), flat(pool[at_gy : at_gy + members]), 0, 0)
            for i in range(2):
                g_down.put(i, gdown[i * fp : i * fp + (ff + 15) // 16 * 16])
            g_down.first()
    gup = dot(flat(ghid_buf[...]), flat(pool[at_h2 : at_h2 + members]), 0, 0)
    main, left = ff // LANES * LANES, ff % LANES
    low = (size + 15) // 16 * 16
    for i in range(2):
        tall = jnp.transpose(gup[i * fp : i * fp + main]).astype(BF16)
        flat_left = gup[i * fp + main : i * fp + main + (left + 15) // 16 * 16].astype(BF16)
        for s in range(shards):
            g_up.put(i, s, slice(0, size), slice(0, main), tall[s * size : (s + 1) * size])
            if left:
                g_up.put(i, s, slice(low, low + flat_left.shape[0]), slice(0, size), flat_left[:, s * size : (s + 1) * size])
    g_up.first()
    grad_h2 = sca.result()
    normed, scale = normalize(mid_buf[...])
    gy_own = pool[at_gy + m].reshape(own, width).astype(F32)
    gmid = gy_own + norm_back(grad_h2, normed, scale, gain_ref[1:2])
    gmid_buf[...] = gmid
    m_buf[m] = gmid.astype(BF16).reshape(2, rows, width)
    gat2.start_both()

    def over_rows(val):
        return jnp.sum(val, axis=0, keepdims=True)

    gain_two, shift_two, bias_out, bias_down = (
        over_rows(grad_h2 * normed), over_rows(grad_h2), over_rows(gmid), over_rows(gy_own)
    )
    bias_up = over_rows(flat(ghid_buf[...]).astype(F32))

    def down_part(chip):
        chip_put(part2, chip, dot(chip_rows(act_buf, chip), wd_buf[...]))

    def back(chip):
        block = chip_rows(m_buf, chip)
        chip_put(gatt_buf, chip, dot(block, wo_buf[...], 1, 1))
        return dot(chip_rows(att_b, chip), block, 0, 0)

    gout = None
    for k in range(half + 1):
        for d, chip in enumerate(gat.blocks(k)):
            down_part(chip)
            sca2.give(k, d)
        if k < half:
            gat2.hop(k + 1)
        if k == half - 1:
            g_down.second()
        gat2.ready(k)
        for chip in gat2.blocks(k):
            more = back(chip)
            gout = more if gout is None else gout + more
    for i in range(2):
        g_out.put(i, gout[i * sp : i * sp + low])
    g_out.first()
    for x in (gat, gaty, sca):
        x.finish()
    load_w = pltpu.make_async_copy(w_hbm, pool, loc.at[0])
    load_w.start()
    sca2.hop(0)

    col_ids = ids_of(iota((total, 1), 0))

    def pre_copy(i, j):
        to = (m + j) % members
        return send(pre_buf.at[i, to], pre_land.at[i, m], pre_s.at[i, j], pre_r.at[i, m], p.dev(to))

    pre_buf[:, :, :, :, 3 * size :] = jnp.zeros(pre_buf.shape[:4] + (pre_buf.shape[4] - 3 * size,), BF16)
    bias_buf[...] = jnp.zeros(bias_buf.shape, F32)
    for i in range(2):
        for j in range(fp // LANES):
            bias_buf[i, 2 + j : 3 + j] = bias_up[:, i * fp + j * LANES : i * fp + (j + 1) * LANES]

    def lanes_at(k):
        return pl.ds(pl.multiple_of(k * sp, LANES), sp)

    mine_last = dp // g_qkv.hp
    for step in range(2):
        i = mine_last if step == 1 else 1 - mine_last
        dk_acc[...] = jnp.zeros(dk_acc.shape, F32)
        dv_acc[...] = jnp.zeros(dv_acc.shape, F32)

        def attend_back(b):
            blk = pl.ds(b * qn, qn)
            query = qkv_buf[blk, :, :, lanes_at(i)].reshape(QB, sp)
            keys = qkv_buf[:, :, :, lanes_at(2 + i)].reshape(total, sp)
            values = qkv_buf[:, :, :, lanes_at(4 + i)].reshape(total, sp)
            grad = gatt_buf[blk, :, :, lanes_at(i)].reshape(QB, sp)
            att = att_buf[blk, :, :, lanes_at(i)].reshape(QB, sp)
            delta = jnp.sum(grad.astype(F32) * att, axis=-1, keepdims=True)
            delta = jnp.transpose(jnp.broadcast_to(delta, (QB, LANES)))[0:1]
            same = col_ids == ids_of(iota((1, QB), 1) + b * QB)
            probs = jnp.exp(jnp.where(same, dot(keys, query, 1, 1), NEG) - lse_buf[i, b][0:1])
            grad_scores = (probs * (dot(values, grad, 1, 1) - delta)).astype(BF16)
            dv_acc[...] += dot(probs.astype(BF16), grad)
            dk_acc[...] += dot(grad_scores, query)
            dq = (dot(grad_scores, keys, 0, 0) * factor).astype(BF16)
            pre_buf[i, blk, :, :, :size] = dq[:, :size].reshape(qn, 2, rows, size)
            bias_buf[i, 0:1] += over_rows(dq.astype(F32))

        for b in range(blocks):
            attend_back(b)
            if step == 0 and b == blocks - 1:
                g_up.second()
        dk = dk_acc[...].astype(BF16)
        dv = dv_acc[...].astype(BF16)
        bias_buf[i, 1:2] = over_rows(dv.astype(F32))
        pre_buf[i, :, :, :, size : 2 * size] = dk[:, :size].reshape(members, 2, rows, size)
        pre_buf[i, :, :, :, 2 * size : 3 * size] = dv[:, :size].reshape(members, 2, rows, size)
        for j in range(1, members):
            pre_copy(i, j).start()
        grad = dot(pre_buf[i].reshape(total, pre_buf.shape[4]), flat(h_buf[...]), 0, 0)
        grad = jnp.transpose(grad).astype(BF16)
        for s in range(shards):
            g_qkv.put(i, s, slice(0, size), slice(0, grad.shape[1]), grad[s * size : (s + 1) * size])
        g_qkv.first(i)
        if step == 0:
            for h in range(1, half):
                sca2.hop(h)
    def bias_copy(x, i):
        to = ((dp + x) % parts, p.seq_of(i, m))
        return send(
            bias_buf.at[i], bias_land.at[side * parts + dp], bias_s.at[x, i], bias_r.at[side * parts + dp], to
        )

    for x in range(parts):
        for i in range(2):
            if x > 0:
                bias_copy(x, i).start()
            else:

                @pl.when(side != i)
                def _():
                    bias_copy(0, i).start()

    down = sca2.result()
    out = ((mid_buf[...] + down + dbias_ref[...]) * valid).astype(BF16)
    out_ref[side] = out[:rows]
    out_buf[0] = out[rows:]
    g_qkv.second()
    g_out.second()
    swap_out = swap(out_buf.at[0], out_land.at[0], 2)
    swap_out.start()
    g_up.meet()
    load_w.wait()
    for i in range(2):
        for j in range(1, members):
            frm = (m + members - j) % members
            send(pre_buf.at[i, frm], pre_land.at[i, frm], pre_s.at[i, j], pre_r.at[i, frm], p.dev(frm)).wait_recv()
        pre_land[i, m] = pre_buf[i, m]
        for j in range(members):
            block = pre_land[i, j].reshape(own, pre_land.shape[4])
            for c in range(3):
                at = c * width + p.seq_of(i, j) * size
                mine_buf[:, at : at + size] = block[:, c * size : (c + 1) * size]
    grad_h1 = None
    for c in range(3):
        w = pool[c * per_w : (c + 1) * per_w].reshape(width, width)
        more = dot(mine_buf[:, c * width : (c + 1) * width], w, 1, 1)
        grad_h1 = more if grad_h1 is None else grad_h1 + more
    normed, scale = normalize(x_buf[...].reshape(own, width).astype(F32))
    sg = (gmid_buf[...] + norm_back(grad_h1, normed, scale, gain_ref[0:1])).astype(BF16)
    out_buf[1] = sg[rows:]
    swap_sg = swap(out_buf.at[1], out_land.at[1], 3)
    swap_sg.start()
    sg_ref[side] = sg[:rows]
    vecs = jnp.concatenate(
        [over_rows(grad_h1 * normed), gain_two, over_rows(grad_h1), shift_two, bias_out, bias_down, bias_out, bias_out],
        axis=0,
    )
    for s in range(shards):
        vec_buf[s, :, :size] = vecs[:, s * size : (s + 1) * size]
    per = shards // parts
    pairs = [(i, j) for i in range(parts) for j in range(shards) if i + j > 0]

    def vec_copy(i, j):
        to = (me + j) % shards
        slot = dp * shards + me
        return send(vec_buf.at[to], vec_land.at[slot], vec_s.at[i, j], vec_r.at[slot], ((dp + i) % parts, to))

    def vec_wait(i, j):
        frm = (me + j) % shards
        x = (dp + i) % parts
        slot = x * shards + frm
        send(vec_buf.at[0], vec_land.at[slot], vec_s.at[i, j], vec_r.at[slot], (x, frm)).wait_recv()

    for i, j in pairs:
        vec_copy(i, j).start()
    vec_land[dp * shards + me] = vec_buf[me]
    g_qkv.meet()

    cols = width // parts
    gdown_ref[...] = g_down.total()[:ff, :cols]
    gout_ref[...] = g_out.total()[:size, :cols]
    g_up.third()
    for v in range(per):
        acc = g_up.total(v)
        up_ref[:, v * ff : v * ff + main] = acc[:size, :main]
        if left:
            tail = jnp.transpose(acc[low:, :LANES])
            up_ref[:, v * ff + main : (v + 1) * ff] = tail[:size, :left]
    bias_land[side * parts + dp] = bias_buf[side]
    for s in range(2):
        for x in range(parts):
            slot = s * parts + x
            away = (side != s).astype(jnp.int32) + (dp != x).astype(jnp.int32)

            @pl.when(away > 0)
            def _():
                send(
                    bias_buf.at[0], bias_land.at[slot], bias_s.at[0, 0], bias_r.at[slot], (x, p.seq_of(s, m))
                ).wait_recv()

    acc = bias_land[0]
    for i in range(1, 2 * parts):
        acc = acc + bias_land[i]
    gab_ref[0:2] = acc[0:2, :size]
    for j in range(fp // LANES):
        n = min(LANES, ff - j * LANES)
        gub_ref[:, j * LANES : j * LANES + n] = acc[2 + j : 3 + j, :n]
    g_qkv.third()
    for v in range(per):
        acc = g_qkv.total(v)
        for c in range(3):
            qkv_ref[c, :, v * size : (v + 1) * size] = acc[:size, c * size : (c + 1) * size]
    swap_out.wait_recv()
    out_ref[1 - side] = out_land[0]
    swap_sg.wait_recv()
    sg_ref[1 - side] = out_land[1]
    for i, j in pairs:
        vec_wait(i, j)
    acc = vec_land[0]
    for i in range(1, shards * parts):
        acc = acc + vec_land[i]
    ggain_ref[...] = acc[0:2, :size]
    gshift_ref[...] = acc[2:4, :size]
    gab_ref[2:3] = acc[4:5, :size]
    gdb_ref[...] = acc[5:6, :size]

    for c in (swap_x, swap_ct, swap_out, swap_sg):
        c.wait_send()
    for j in range(1, members):
        att_copy((m + j) % members).wait_send()
        for i in range(2):
            pre_copy(i, j).wait_send()
    for x in range(parts):
        for i in range(2):
            if x > 0:
                bias_copy(x, i).wait_send()
            else:

                @pl.when(side != i)
                def _():
                    bias_copy(0, i).wait_send()

    for i, j in pairs:
        vec_copy(i, j).wait_send()
    for x in (gat1, gat2, sca2, g_up, g_qkv, g_down, g_out):
        x.finish()


def layer(shards, size, ff, parts, counts, states, cotangent, gains, nbias, abias, dbias, bu, w_out, w_up, w_down, w_qkv):
    rows, width = states.shape[1:]
    members = shards // 2
    n = members // 2
    sp, fp = up128(size), up128(ff)
    own = 2 * rows
    total = members * own
    per = shards // parts
    cols = width // parts
    r16 = lambda k: -(-k // 16) * 16
    sds = jax.ShapeDtypeStruct
    block = (members, 2, rows)
    wp = up128(3 * size)
    w4 = w_qkv.reshape(3 * width // own, 2, rows, width)
    up_rows = r16(size) + r16(ff % LANES)
    return pl.pallas_call(
        functools.partial(layer_kernel, shards, size, ff, parts),
        out_shape=[
            sds((2, rows, width), BF16), sds((2, rows, width), BF16), sds((3, size, per * size), F32),
            sds((size, cols), F32), sds((3, size), F32), sds((2, size), F32), sds((2, size), F32),
            sds((size, per * ff), F32), sds((1, ff), F32), sds((ff, cols), F32), sds((1, size), F32),
        ],
        in_specs=[pl.BlockSpec(memory_space=pltpu.SMEM)]
        + [pl.BlockSpec(memory_space=VMEM)] * 7
        + [pl.BlockSpec(memory_space=pl.ANY)] * 4,
        out_specs=[pl.BlockSpec(memory_space=VMEM)] * 11,
        scratch_shapes=[
            VMEM(w4.shape, BF16), VMEM(block + (width,), BF16), VMEM(block + (width,), BF16), VMEM(block + (width,), BF16),
            VMEM((2, rows, width), BF16), VMEM((rows, width), BF16), VMEM((own, width), F32), VMEM((own, width), F32),
            VMEM(block + (6 * sp,), BF16), VMEM(block + (2 * sp,), F32), VMEM(block + (2 * sp,), BF16),
            VMEM(block + (2 * sp,), BF16), VMEM((2, total // QB, 8, QB), F32), VMEM((own, 3 * width), BF16),
            VMEM(block + (2 * fp,), BF16), VMEM(block + (2 * fp,), BF16), VMEM(block + (2 * sp,), BF16),
            VMEM((total, sp), F32), VMEM((total, sp), F32), VMEM((2,) + block + (wp,), BF16), VMEM((2,) + block + (wp,), BF16),
            VMEM((width, 6 * sp), BF16), VMEM(w_out.shape, BF16), VMEM((2 * sp, width), BF16), VMEM((2 * fp, width), BF16),
            VMEM((2 * fp, width), BF16),
            VMEM((2, max(6 * sp, 2 * fp)), F32),
            VMEM((shards, 8, LANES), F32), VMEM((shards * parts, 8, LANES), F32), VMEM((2, 8, LANES), F32),
            VMEM((2 * parts, 8, LANES), F32), VMEM((2, rows, width), BF16),
            VMEM((2, rows, width), BF16),
            DMA((4,)), DMA((4,)), DMA((members,)), DMA((members,)), DMA((2, members)), DMA((2, members)),
            DMA((parts, shards)), DMA((parts * shards,)), DMA((parts, 2)), DMA((2 * parts,)), DMA((6,)),
        ]
        + gather_sems(n) * 4
        + scatter_scratch(n, rows, width) * 2
        + rows_scratch(shards, parts, up_rows, ff // LANES * LANES)
        + rows_scratch(shards, parts, r16(size), wp)
        + cols_scratch(parts, r16(ff), up128(cols))
        + cols_scratch(parts, r16(size), up128(cols)),
        name="layer",
        compiler_params=pltpu.CompilerParams(
            collective_id=0, has_side_effects=True, vmem_limit_bytes=63 << 20
        ),
    )(counts, states, cotangent, gains, nbias, abias, dbias, bu, w_out, w_up, w_down, w4)


def deliver_kernel(*refs):
    count = len(refs) // 2
    for i in range(count):
        refs[count + i][...] = refs[i][...]


def deliver(*arrays):
    return pl.pallas_call(
        deliver_kernel,
        out_shape=[jax.ShapeDtypeStruct(x.shape, x.dtype) for x in arrays],
        in_specs=[pl.BlockSpec(memory_space=VMEM)] * len(arrays),
        out_specs=[pl.BlockSpec(memory_space=VMEM)] * len(arrays),
        name="deliver",
    )(*arrays)


def body(
    states, counts, cotangent, w_qkv, w_out, attn_bias, norm_gain, norm_bias,
    w_up, up_bias, w_down, down_bias,
):
    width = states.shape[2]
    shards = lax.axis_size("seq")
    parts = lax.axis_size("dp")
    size = width // HEADS
    ff = w_up.shape[1] // shards
    members = shards // 2
    me = lax.axis_index("seq")
    m = (me + (members // 2) * (me // members)) % members
    units = (m, members + (m + members // 2) % members)

    def mine(x, axis, count):
        return jnp.stack([lax.dynamic_slice_in_dim(x, u * count, count, axis) for u in units])

    layer_out, state_grad, g_qkv, g_out, g_ab, g_gain, g_shift, g_up, g_ub, g_down, g_db = deliver(
        *layer(
            shards, size, ff, parts, counts, states, cotangent, norm_gain, norm_bias, attn_bias, down_bias[None],
            mine(up_bias[None], 1, ff), w_out, w_up.T, w_down, w_qkv,
        )
    )
    return (
        layer_out, state_grad, g_qkv, g_out, g_ab, g_gain, g_shift, g_up,
        g_ub.reshape(ff), g_down, g_db.reshape(size),
    )


def solution(mesh):
    placed = (P("dp", "seq", None), P("dp", None), P("dp", "seq", None)) + (P(),) * 9
    return jax.shard_map(
        body,
        mesh=mesh,
        in_specs=placed,
        out_specs=(
            P("dp", "seq", None), P("dp", "seq", None), P(None, "seq", "dp"), P("seq", "dp"),
            P(None, "seq"), P(None, "seq"), P(None, "seq"), P("seq", "dp"), P("seq"),
            P("seq", "dp"), P("seq"),
        ),
        check_vma=False,
    )
```

```python
import functools
import math

import jax
import jax.numpy as jnp
from jax import lax
from jax.experimental import pallas as pl
from jax.experimental.pallas import tpu as pltpu
from jax.sharding import PartitionSpec as P

HEADS = 16
EPS = 1e-06
NEG = -1e30
F32 = jnp.float32
BF16 = jnp.bfloat16
MESH = pl.DeviceIdType.MESH
VMEM = pltpu.VMEM
DMA = pltpu.SemaphoreType.DMA


def mm(spec, a, b):
    return jnp.einsum(spec, a, b, preferred_element_type=F32)


def dot(a, b, ca=1, cb=0):
    return lax.dot_general(a, b, (((ca,), (cb,)), ((), ())), preferred_element_type=F32)


def pad_to(x, axis, size):
    pads = [(0, 0)] * x.ndim
    pads[axis] = (0, size - x.shape[axis])
    return jnp.pad(x, pads)


def up128(n):
    return -(-n // 128) * 128


def normalize(values):
    mean = jnp.mean(values, axis=-1, keepdims=True)
    centred = values - mean
    scale = lax.rsqrt(jnp.mean(centred * centred, axis=-1, keepdims=True) + EPS)
    return (centred * scale, scale)


def norm_back(grad_norm, normed, scale, gain):
    scaled = grad_norm * gain
    return scale * (
        scaled
        - jnp.mean(scaled, axis=-1, keepdims=True)
        - normed * jnp.mean(scaled * normed, axis=-1, keepdims=True)
    )


def gelu_both(v):
    c, a = 0.7978845608028654, 0.044715
    sq = v * v
    t = jnp.tanh(c * (v + a * v * sq))
    half = 0.5 * (1.0 + t)
    return v * half, half + 0.5 * v * (1.0 - t * t) * (c * (1.0 + 3.0 * a * sq))


def send(src, dst, s, r, dev):
    return pltpu.make_async_remote_copy(
        src_ref=src, dst_ref=dst, send_sem=s, recv_sem=r, device_id=dev, device_id_type=MESH
    )


class Place:
    def __init__(self, shards, parts):
        self.shards, self.parts = shards, parts
        self.members = shards // 2
        self.n = self.members // 2
        self.half = self.n // 2
        self.me = lax.axis_index("seq")
        self.dp = lax.axis_index("dp")
        self.side = self.me // self.members
        self.m = (self.me + (self.members // 2) * self.side) % self.members
        self.chip = self.m // 2
        self.core = self.m % 2
        odd = self.chip % 2
        self.pos = (1 - odd) * (self.chip // 2) + odd * (self.n - 1 - self.chip // 2)
        self.to = (self.at(1, 1) * 2 + self.core, self.at(1, 0) * 2 + self.core)
        self.sib = self.chip * 2 + 1 - self.core
        self.partner = {"seq": self.seq_of(1 - self.side, self.m)}

    def seq_of(self, side, m):
        return side * self.members + (m + (self.members // 2) * side) % self.members

    def dev(self, m):
        return {"seq": self.seq_of(self.side, m)}

    def at(self, k, d):
        p = (self.pos + (self.n - k if d == 0 else k)) % self.n
        hi = p // self.half
        return (1 - hi) * 2 * p + hi * (2 * (self.n - 1 - p) + 1)

    def others(self):
        return [
            ((self.dp + i) % self.parts, (self.me + j) % self.shards)
            for i in range(self.parts) for j in range(self.shards) if i + j > 0
        ]


def gather_sems(n):
    return [DMA((2, n // 2 + 1, 2))] * 4


class Gather:
    def __init__(self, place, buf, base, sems):
        self.place, self.buf, self.base = place, buf, base
        self.ring_s, self.ring_r, self.sib_s, self.sib_r = sems
        self.sent = []

    def copy(self, k, d, g, to_sib):
        p = self.place
        block = self.buf.at[self.base + p.at(k, d) * 2 + p.core, g]
        s, r = (self.sib_s, self.sib_r) if to_sib else (self.ring_s, self.ring_r)
        return send(block, block, s.at[d, k, g], r.at[d, k, g], p.dev(p.sib if to_sib else p.to[d]))

    def go(self, *args):
        c = self.copy(*args)
        c.start()
        self.sent.append(c)

    def units(self, k):
        if k == self.place.half:
            return [(0, 0), (1, 1)]
        return [(0, 0), (1, 1), (0, 1), (1, 0)]

    def passes(self, k, d, g):
        return k < self.place.half - 1 or (k == self.place.half - 1 and g == d)

    def start(self, g):
        for d in (g, 1 - g):
            if self.passes(0, d, g):
                self.go(0, d, g, False)
        self.go(0, g, g, True)

    def start_both(self):
        for d, g in self.units(0):
            if self.passes(0, d, g):
                self.go(0, d, g, False)
        for g in range(2):
            self.go(0, g, g, True)

    def hop(self, k):
        for d, g in self.units(k):
            self.copy(k - 1, d, g, False).wait_recv()
            if self.passes(k, d, g):
                self.go(k, d, g, False)
            self.go(k, d, g, True)

    def ready(self, k):
        for d, g in self.units(k):
            if k > 0 or d == g:
                self.copy(k, d, g, True).wait_recv()

    def blocks(self, k):
        if k == 0 or k == self.place.half:
            return [self.place.at(k, 0)]
        return [self.place.at(k, 0), self.place.at(k, 1)]

    def finish(self):
        for c in self.sent:
            c.wait_send()


def scatter_scratch(n, rows, width):
    return [
        VMEM((n, 2, rows, width), BF16), VMEM((2, n // 2, 2, rows, width), BF16),
        DMA((n,)), DMA((n,)), DMA((2, n // 2, 2)), DMA((2, n // 2, 2)),
    ]


class Scatter:
    def __init__(self, place, part, base, scratch):
        self.place, self.part, self.base = place, part, base
        self.sib_land, self.land, self.sib_s, self.sib_r, self.ring_s, self.ring_r = scratch
        self.sent = []
        self.have = set()

    def slot(self, k, d):
        if k == 0:
            return 0
        return self.place.n - 1 if k == self.place.half else 2 * k - 1 + d

    def sib_copy(self, k, d):
        p, i = self.place, self.slot(k, d)
        src = self.part.at[self.base + p.at(k, d) * 2 + 1 - p.core]
        return send(src, self.sib_land.at[i], self.sib_s.at[i], self.sib_r.at[i], p.dev(p.sib))

    def give(self, k, d):
        c = self.sib_copy(k, d)
        c.start()
        self.sent.append(c)

    def from_sib(self, k, d):
        i = self.slot(k, d)
        if i not in self.have:
            self.have.add(i)
            self.sib_copy(k, d).wait_recv()
        return self.sib_land.at[i]

    def dist(self, h, d, g):
        return self.place.half - h if g == d else self.place.half - 1 - h

    def block(self, h, d, g):
        p = self.place
        return self.base + p.at(self.dist(h, d, g), 1 - d) * 2 + p.core

    def ring_copy(self, h, d, g):
        return send(
            self.part.at[self.block(h, d, g), g], self.land.at[d, h, g],
            self.ring_s.at[d, h, g], self.ring_r.at[d, h, g], self.place.dev(self.place.to[d]),
        )

    def hop(self, h):
        for d, g in [(0, 0), (1, 1), (0, 1), (1, 0)]:
            j = self.dist(h, d, g)
            if j == 0:
                continue
            own = self.block(h, d, g)
            val = self.part[own, g].astype(F32) + self.from_sib(j, 1 - d)[g].astype(F32)
            if h > 0:
                self.ring_copy(h - 1, d, g).wait_recv()
                val = val + self.land[d, h - 1, g].astype(F32)
            self.part[own, g] = val.astype(BF16)
            c = self.ring_copy(h, d, g)
            c.start()
            self.sent.append(c)

    def result(self):
        p = self.place
        out = []
        for g in range(2):
            val = self.part[self.base + p.m, g].astype(F32) + self.from_sib(0, 0)[g].astype(F32)
            for d in range(2):
                h = p.half - 1 if g == d else p.half - 2
                self.ring_copy(h, d, g).wait_recv()
                val = val + self.land[d, h, g].astype(F32)
            out.append(val)
        return jnp.concatenate(out, axis=0)

    def finish(self):
        for c in self.sent:
            c.wait_send()


def rows_scratch(shards, parts, size, width, left):
    gh, per = shards // parts, shards // parts
    r16 = lambda k: -(-k // 16) * 16
    packed = r16(gh * size) + r16(left) * -(-gh * size // width)
    rows = r16(size) + r16(left)
    return [
        VMEM((parts, 2, packed, width), BF16), VMEM((parts, 2, packed, width), BF16), VMEM((packed, width), BF16),
        VMEM((gh, rows, width), BF16), VMEM((per, rows, width), BF16),
        DMA((parts, 2)), DMA((parts, 2)), DMA((2,)), DMA((gh,)), DMA((per,)), DMA,
    ]


class Rows:
    def __init__(self, place, size, scratch):
        self.place, self.size = place, size
        self.buf, self.land, self.met, self.out, self.last = scratch[:5]
        self.s1, self.r1, self.sc, self.s2, self.r2, self.loc = scratch[5:]
        self.gh = self.out.shape[0]
        self.hp = place.parts // 2
        self.per = place.shards // place.parts
        self.below = (self.gh * size + 15) // 16 * 16
        self.low = (size + 15) // 16 * 16

    def fill(self, i, tall, turned=None):
        p, n, width = self.place, self.gh * self.size, self.buf.shape[3]
        for side in range(2):
            for q in range(self.hp):
                at = (side * p.members + q * self.gh) * self.size
                self.buf[i * self.hp + q, side, :n, : tall.shape[1]] = tall[at : at + n].astype(BF16)
                if turned is not None:
                    high = turned.shape[0]
                    for c in range(0, n, width):
                        to = self.below + c // width * high
                        cut = turned[:, at + c : at + min(c + width, n)].astype(BF16)
                        self.buf[i * self.hp + q, side, to : to + high, : cut.shape[1]] = cut

    def share(self, j, side):
        p = self.place
        x = (p.dp + j) % p.parts
        return send(
            self.buf.at[x, side], self.land.at[p.dp, side], self.s1.at[j, side], self.r1.at[p.dp, side], (x, p.me)
        )

    def first(self, side, unit=None):
        p = self.place
        for j in range(1, p.parts):
            if unit is None:
                self.share(j, side).start()
            else:

                @pl.when((p.dp + j) % p.parts // self.hp == unit)
                def _():
                    self.share(j, side).start()

    def shares(self, side):
        p = self.place
        for j in range(1, p.parts):
            x = (p.dp + j) % p.parts
            send(
                self.buf.at[x, side], self.land.at[x, side], self.s1.at[j, side], self.r1.at[x, side], (x, p.me)
            ).wait_recv()
        total = self.buf[p.dp, side].astype(F32)
        for j in range(1, p.parts):
            total = total + self.land[(p.dp + j) % p.parts, side].astype(F32)
        return total

    def cross(self):
        p = self.place
        return send(self.buf.at[p.dp, 1 - p.side], self.met, self.sc.at[0], self.sc.at[1], p.partner)

    def second(self):
        away = 1 - self.place.side
        self.buf[self.place.dp, away] = self.shares(away).astype(BF16)
        self.cross().start()

    def deliver(self, k, act, act_own):
        p = self.place
        unit = p.seq_of(p.dp // self.hp, p.m)
        keeper = unit // self.per
        owner = p.side * p.members + (p.dp % self.hp) * self.gh + k
        slot = unit % self.per
        away = (keeper != p.dp).astype(jnp.int32) + (owner != p.me).astype(jnp.int32)
        block = self.out.at[k]

        @pl.when(away > 0)
        def _():
            act(send(block, self.last.at[slot], self.s2.at[k], self.r2.at[slot], (keeper, owner)))

        if act_own:

            @pl.when(away == 0)
            def _():
                c = pltpu.make_async_copy(block, self.last.at[slot], self.loc)
                c.start()
                c.wait()

    def meet(self):
        total = self.shares(self.place.side)
        self.cross().wait_recv()
        total = total + self.met[...].astype(F32)
        size, high = self.size, self.out.shape[1] - self.low
        if high:
            parts = range(self.below, total.shape[0], high)
            turned = jnp.concatenate([total[at : at + high] for at in parts], axis=1)
        for k in range(self.gh):
            self.out[k, :size] = total[k * size : (k + 1) * size].astype(BF16)
            if high:
                self.out[k, self.low :, :size] = turned[:, k * size : (k + 1) * size].astype(BF16)
            self.deliver(k, lambda c: c.start(), True)

    def third(self):
        p = self.place
        for v in range(self.per):
            unit = p.dp * self.per + v
            i = unit // p.members
            m = (unit + (p.members // 2) * i) % p.members
            x = i * self.hp + p.me % p.members // self.gh
            away = (x != p.dp).astype(jnp.int32) + (m != p.m).astype(jnp.int32)

            @pl.when(away > 0)
            def _():
                frm = (x, p.seq_of(p.side, m))
                send(self.out.at[0], self.last.at[v], self.s2.at[0], self.r2.at[v], frm).wait_recv()

    def total(self, v):
        return self.last[v].astype(F32)

    def finish(self):
        for j in range(1, self.place.parts):
            for side in range(2):
                self.share(j, side).wait_send()
        self.cross().wait_send()
        for k in range(self.gh):
            self.deliver(k, lambda c: c.wait_send(), False)


def cols_scratch(parts, rows, width):
    return [
        VMEM((parts, 2, rows, width), BF16), VMEM((parts, 2, rows, width), BF16), VMEM((rows, width), BF16),
        DMA((parts, 2)), DMA((parts, 2)), DMA, DMA,
    ]


class Cols:
    def __init__(self, place, scratch):
        self.place = place
        self.buf, self.land, self.last, self.s1, self.r1, self.s2, self.r2 = scratch

    def put(self, i, val):
        p = self.place
        cols = val.shape[1] // p.parts
        val = val.astype(BF16)
        for x in range(p.parts):
            self.buf[x, i, : val.shape[0], :cols] = val[:, x * cols : (x + 1) * cols]

    def share(self, j, i):
        p = self.place
        x = (p.dp + j) % p.parts
        return send(self.buf.at[x, i], self.land.at[p.dp, i], self.s1.at[j, i], self.r1.at[p.dp, i], (x, p.me))

    def cross(self):
        p = self.place
        return send(self.buf.at[p.dp, 1 - p.side], self.last, self.s2, self.r2, p.partner)

    def first(self, i):
        for j in range(1, self.place.parts):
            self.share(j, i).start()

    def dp_sum(self, i):
        p = self.place
        val = self.buf[p.dp, i].astype(F32)
        for j in range(1, p.parts):
            x = (p.dp + j) % p.parts
            send(self.buf.at[x, i], self.land.at[x, i], self.s1.at[j, i], self.r1.at[x, i], (x, p.me)).wait_recv()
            val = val + self.land[x, i].astype(F32)
        return val

    def second(self):
        p = self.place
        self.buf[p.dp, 1 - p.side] = self.dp_sum(1 - p.side).astype(BF16)
        self.cross().start()

    def total(self):
        val = self.dp_sum(self.place.side)
        self.cross().wait_recv()
        return val + self.last[...].astype(F32)

    def finish(self):
        for j in range(1, self.place.parts):
            for i in range(2):
                self.share(j, i).wait_send()
        self.cross().wait_send()


def chip_rows(ref, chip, base=0):
    val = ref[pl.ds(base + 2 * chip, 2)]
    return val.reshape(-1, val.shape[-1])


def chip_put(ref, chip, val, base=0):
    ref[pl.ds(base + 2 * chip, 2)] = val.astype(ref.dtype).reshape((2,) + ref.shape[1:])


def ids_at(positions, ends):
    total = (positions >= ends[0]).astype(jnp.int32)
    for end in ends[1:]:
        total = total + (positions >= end).astype(jnp.int32)
    return total


def log2(n):
    assert n & (n - 1) == 0
    return n.bit_length() - 1


QB = 256
LANES = 128


def layer_kernel(
    shards, size, ff, parts,
    counts_ref, x_ref, ct_ref, gain_ref, nbias_ref, abias_ref, dbias_ref, bu_ref, wout_hbm, wu_hbm, wd_hbm, w_hbm,
    out_ref, sg_ref, qkv_ref, gout_ref, gab_ref, ggain_ref, gshift_ref, up_ref, gub_ref, gdown_ref, gdb_ref,
    pool, h_buf, m_buf, part2, x_buf, ct_buf, mid_buf, gmid_buf, qkv_buf, att_buf, att_b, att_land, lse_buf, mine_buf,
    act_buf, ghid_buf, gatt_buf, dk_acc, dv_acc, pre_buf, pre_land, wq_buf, wout_buf, wo_buf, wu_buf, wd_buf, row_buf,
    vec_buf, vec_land, bias_buf, bias_land, out_buf, out_land,
    ex_s, ex_r, att_s, att_r, pre_s, pre_r, vec_s, vec_r, bias_s, bias_r, loc, *rest,
):
    p = Place(shards, parts)
    me, dp, side, m = p.me, p.dp, p.side, p.m
    bar = pltpu.get_barrier_semaphore()
    for dev in p.others():
        pl.semaphore_signal(bar, inc=1, device_id=dev, device_id_type=MESH)
    rows, width = x_ref.shape[1:]
    members, half = p.members, p.half
    own = 2 * rows
    total = members * own
    sp = wo_buf.shape[0] // 2
    fp = wu_buf.shape[0] // 2
    units = [p.seq_of(i, m) for i in range(2)]

    span = (ff + 15) // 16 * 16 + 16
    windows = [u * ff // 16 * 16 - 16 * (u // (shards - 1)) for u in units]
    load_w0 = pltpu.make_async_copy(w_hbm, pool, loc.at[0])
    load_out = pltpu.make_async_copy(wout_hbm, wout_buf, loc.at[1])
    loads = [
        pltpu.make_async_copy(
            hbm.at[pl.ds(pl.multiple_of(windows[i], 16), span)], buf.at[pl.ds(i * fp, span)], loc.at[2 + 2 * i + j]
        )
        for j, (hbm, buf) in enumerate(((wu_hbm, wu_buf), (wd_hbm, wd_buf)))
        for i in range(2)
    ]
    load_w0.start()
    load_out.start()
    for c in loads:
        c.start()
    factor = 1.0 / math.sqrt(size)
    at_part, at_h2, at_gy = 0, members, 2 * members
    gat1 = Gather(p, h_buf, 0, rest[0:4])
    gaty = Gather(p, pool, at_gy, rest[4:8])
    gat = Gather(p, pool, at_h2, rest[8:12])
    gat2 = Gather(p, m_buf, 0, rest[12:16])
    sca = Scatter(p, pool, at_part, rest[16:22])
    sca2 = Scatter(p, part2, 0, rest[22:28])
    g_up = Rows(p, size, rest[28:39])
    g_qkv = Rows(p, size, rest[39:50])
    g_down = Cols(p, rest[50:57])
    g_out = Cols(p, rest[57:64])

    ends = [counts_ref[side, 0]]
    for i in range(1, counts_ref.shape[1]):
        ends.append(ends[-1] + counts_ref[side, i])

    def ids_of(t):
        mem = lax.shift_right_logical(t, log2(own))
        rho = lax.shift_right_logical(t, log2(rows)) & 1
        sig = rho + side - 2 * rho * side
        seq = sig * members + ((mem + (members // 2) * sig) & (members - 1))
        return ids_at(seq * rows + (t & (rows - 1)), ends)

    def iota(shape, dim):
        return lax.broadcasted_iota(jnp.int32, shape, dim)

    valid = (ids_of(iota((own, 1), 0) + m * own) < counts_ref.shape[1]).astype(F32)

    def swap(src, dst, i):
        return send(src, dst, ex_s.at[i], ex_r.at[i], p.partner)

    def norm_one(g):
        normed, _ = normalize(x_buf[g].astype(F32))
        h_buf[m, g] = (normed * gain_ref[0:1] + nbias_ref[0:1]).astype(BF16)

    x_buf[0] = x_ref[side]
    norm_one(0)
    pl.semaphore_wait(bar, len(p.others()))
    swap_x = swap(x_ref.at[1 - side], x_buf.at[1], 0)
    swap_ct = swap(ct_ref.at[1 - side], ct_buf, 1)
    swap_x.start()
    gat1.start(0)
    swap_ct.start()

    def iota2(shape):
        return iota(shape, 0), iota(shape, 1)

    def one_hot(hit, kind):
        return jnp.where(hit, 1.0, 0.0).astype(kind)

    at, lane = iota2((width, sp))
    pick = [jnp.logical_and(at == lane + u * size, lane < size) for u in units]
    exact = lax.dot_general(
        abias_ref[...], jnp.concatenate([one_hot(h, F32) for h in pick], axis=1), (((1,), (0,)), ((), ())),
        preferred_element_type=F32, precision=lax.Precision.HIGHEST,
    )
    row_buf[...] = jnp.zeros(row_buf.shape, F32)
    row_buf[0:1, : 2 * sp] = exact[0:1]
    row_buf[0:1, 4 * sp : 6 * sp] = exact[1:2]
    for i in range(2):
        row_buf[1:2, i * fp : i * fp + ff] = bu_ref[i]
    pick = jnp.concatenate([one_hot(h, BF16) for h in pick], axis=1)
    load_w0.wait()
    per_w = width // own
    for c in range(3):
        w = pool[c * per_w : (c + 1) * per_w].reshape(width, width)
        wq_buf[:, 2 * c * sp : 2 * (c + 1) * sp] = dot(w, pick).astype(BF16)
    swap_x.wait_recv()
    norm_one(1)
    gat1.start(1)
    pool[at_gy + m, 0] = (ct_ref[side].astype(F32) * valid[:rows]).astype(BF16)
    swap_ct.wait_recv()
    pool[at_gy + m, 1] = (ct_buf[...].astype(F32) * valid[rows:]).astype(BF16)
    load_out.wait()
    at, lane = iota2((sp, width))
    for i in range(2):
        hit = jnp.logical_and(lane == at + units[i] * size, at < size)
        wo_buf[i * sp : (i + 1) * sp] = dot(one_hot(hit, BF16), wout_buf[...]).astype(BF16)
    for c in loads:
        c.wait()
    at, lane = iota2((fp, span))
    for i in range(2):
        hit = jnp.logical_and(lane == at + (units[i] * ff - windows[i]), at < ff)
        for buf in (wu_buf, wd_buf):
            cut = dot(one_hot(hit, BF16), buf[i * fp : i * fp + span])
            buf[i * fp : (i + 1) * fp] = cut.astype(BF16)

    def project(chip):
        out = dot(chip_rows(h_buf, chip), wq_buf[...]) + row_buf[0:1, : 6 * sp]
        out = jnp.concatenate([out[:, : 2 * sp] * factor, out[:, 2 * sp :]], axis=1)
        chip_put(qkv_buf, chip, out)

    for k in range(1, half + 1):
        gat1.hop(k)
        gat1.ready(k - 1)
        if k == half - 1:
            gaty.start_both()
        for chip in gat1.blocks(k - 1):
            project(chip)
    gat1.ready(half)
    project(p.at(half, 0))

    qn = QB // own

    def att_copy(to):
        return send(att_b.at[to], att_land.at[m], att_s.at[to], att_r.at[m], p.dev(to))

    def lanes_of(part, i):
        return slice((2 * part + i) * sp, (2 * part + i + 1) * sp)

    row_ids = ids_of(iota((1, total), 1))

    def attend(b):
        query_ids = ids_of(iota((QB, 1), 0) + b * QB)
        same = query_ids == row_ids
        for i in range(2):
            query = qkv_buf[pl.ds(b * qn, qn), :, :, lanes_of(0, i)].reshape(QB, sp)
            keys = qkv_buf[:, :, :, lanes_of(1, i)].reshape(total, sp)
            values = qkv_buf[:, :, :, lanes_of(2, i)].reshape(total, sp)
            scores = jnp.where(same, dot(query, keys, 1, 1), NEG)
            high = jnp.max(scores, axis=-1, keepdims=True)
            weights = jnp.exp(scores - high)
            sums = jnp.sum(weights, axis=-1, keepdims=True)
            out = (dot(weights.astype(BF16), values) / sums).reshape(qn, 2, rows, sp)
            att_buf[pl.ds(b * qn, qn), :, :, i * sp : (i + 1) * sp] = out
            att_b[pl.ds(b * qn, qn), :, :, i * sp : (i + 1) * sp] = out.astype(BF16)
            lse = jnp.broadcast_to(high + jnp.log(sums), (QB, LANES))
            lse_buf[i, b] = jnp.transpose(lse)[0:8]
        for t in range(qn):
            to = b * qn + t

            @pl.when(to != m)
            def _():
                att_copy(to).start()

    blocks = total // QB
    pl.loop(0, blocks // 2)(attend)
    gaty.hop(1)
    pl.loop(blocks // 2, blocks)(attend)
    for k in range(2, half + 1):
        gaty.hop(k)
    att_land[m] = att_b[m]
    for j in range(1, members):
        frm = (m + members - j) % members
        send(att_b.at[frm], att_land.at[frm], att_s.at[frm], att_r.at[frm], p.dev(frm)).wait_recv()
    for j in range(members):
        for i in range(2):
            at = p.seq_of(i, j) * size
            mine_buf[:, at : at + size] = att_land[j].reshape(own, 2 * sp)[:, i * sp : i * sp + size]
    inputs = x_buf[...].reshape(own, width).astype(F32)
    mid = inputs + dot(mine_buf[:, :width], wout_buf[...]) + abias_ref[2:3]
    mid_buf[...] = mid
    normed, _ = normalize(mid)
    pool[at_h2 + m] = (normed * gain_ref[1:2] + nbias_ref[1:2]).astype(BF16).reshape(2, rows, width)
    gat.start_both()

    def forward(chip):
        hidden = dot(chip_rows(pool, chip, at_h2), wu_buf[...], 1, 1) + row_buf[1:2, : 2 * fp]
        act, slope = gelu_both(hidden)
        chip_put(act_buf, chip, act)
        ghid = (dot(chip_rows(pool, chip, at_gy), wd_buf[...], 1, 1) * slope).astype(BF16)
        chip_put(ghid_buf, chip, ghid)
        chip_put(pool, chip, dot(ghid, wu_buf[...]), at_part)

    for k in range(half + 1):
        if k < half:
            gat.hop(k + 1)
        gaty.ready(k)
        gat.ready(k)
        for d, chip in enumerate(gat.blocks(k)):
            forward(chip)
            sca.give(k, d)

    def flat(val):
        return val.reshape(total, val.shape[-1])

    for h in range(half):
        sca.hop(h)
        if h == 0:
            gdown = dot(flat(act_buf[...]), flat(pool[at_gy : at_gy + members]), 0, 0)
            for i in range(2):
                g_down.put(i, gdown[i * fp : i * fp + (ff + 15) // 16 * 16])
            g_down.first(1 - side)
    gup = dot(flat(ghid_buf[...]), flat(pool[at_h2 : at_h2 + members]), 0, 0)
    main, left = ff // LANES * LANES, ff % LANES
    low = (size + 15) // 16 * 16
    for i in range(2):
        turned = gup[i * fp + main : i * fp + main + (left + 15) // 16 * 16] if left else None
        g_up.fill(i, jnp.transpose(gup[i * fp : i * fp + main]), turned)
    g_up.first(1 - side)
    g_down.first(side)
    grad_h2 = sca.result()
    normed, scale = normalize(mid_buf[...])
    gy_own = pool[at_gy + m].reshape(own, width).astype(F32)
    gmid = gy_own + norm_back(grad_h2, normed, scale, gain_ref[1:2])
    gmid_buf[...] = gmid
    m_buf[m] = gmid.astype(BF16).reshape(2, rows, width)
    gat2.start_both()
    g_up.first(side)

    def over_rows(val):
        return jnp.sum(val, axis=0, keepdims=True)

    gain_two, shift_two, bias_out, bias_down = (
        over_rows(grad_h2 * normed), over_rows(grad_h2), over_rows(gmid), over_rows(gy_own)
    )
    bias_up = over_rows(flat(ghid_buf[...]).astype(F32))

    def down_part(chip):
        chip_put(part2, chip, dot(chip_rows(act_buf, chip), wd_buf[...]))

    def back(chip):
        block = chip_rows(m_buf, chip)
        chip_put(gatt_buf, chip, dot(block, wo_buf[...], 1, 1))
        return dot(chip_rows(att_b, chip), block, 0, 0)

    gout = None
    for k in range(half + 1):
        for d, chip in enumerate(gat.blocks(k)):
            down_part(chip)
            sca2.give(k, d)
        if k < half:
            gat2.hop(k + 1)
        if k == half - 1:
            g_down.second()
        gat2.ready(k)
        for chip in gat2.blocks(k):
            more = back(chip)
            gout = more if gout is None else gout + more
    for i in range(2):
        g_out.put(i, gout[i * sp : i * sp + low])
    for i in (1 - side, side):
        g_out.first(i)
    for x in (gat, gaty, sca):
        x.finish()
    load_w = pltpu.make_async_copy(w_hbm, pool, loc.at[0])
    load_w.start()
    sca2.hop(0)

    col_ids = ids_of(iota((total, 1), 0))

    def pre_copy(i, j):
        to = (m + j) % members
        return send(pre_buf.at[i, to], pre_land.at[i, m], pre_s.at[i, j], pre_r.at[i, m], p.dev(to))

    pre_buf[:, :, :, :, 3 * size :] = jnp.zeros(pre_buf.shape[:4] + (pre_buf.shape[4] - 3 * size,), BF16)
    bias_buf[...] = jnp.zeros(bias_buf.shape, F32)
    for i in range(2):
        for j in range(fp // LANES):
            bias_buf[i, 2 + j : 3 + j] = bias_up[:, i * fp + j * LANES : i * fp + (j + 1) * LANES]

    def lanes_at(k):
        return pl.ds(pl.multiple_of(k * sp, LANES), sp)

    mine_last = dp // g_qkv.hp
    for step in range(2):
        i = mine_last if step == 1 else 1 - mine_last
        dk_acc[...] = jnp.zeros(dk_acc.shape, F32)
        dv_acc[...] = jnp.zeros(dv_acc.shape, F32)

        def attend_back(b):
            blk = pl.ds(b * qn, qn)
            query = qkv_buf[blk, :, :, lanes_at(i)].reshape(QB, sp)
            keys = qkv_buf[:, :, :, lanes_at(2 + i)].reshape(total, sp)
            values = qkv_buf[:, :, :, lanes_at(4 + i)].reshape(total, sp)
            grad = gatt_buf[blk, :, :, lanes_at(i)].reshape(QB, sp)
            att = att_buf[blk, :, :, lanes_at(i)].reshape(QB, sp)
            delta = jnp.sum(grad.astype(F32) * att, axis=-1, keepdims=True)
            delta = jnp.transpose(jnp.broadcast_to(delta, (QB, LANES)))[0:1]
            same = col_ids == ids_of(iota((1, QB), 1) + b * QB)
            probs = jnp.exp(jnp.where(same, dot(keys, query, 1, 1), NEG) - lse_buf[i, b][0:1])
            grad_scores = (probs * (dot(values, grad, 1, 1) - delta)).astype(BF16)
            dv_acc[...] += dot(probs.astype(BF16), grad)
            dk_acc[...] += dot(grad_scores, query)
            dq = (dot(grad_scores, keys, 0, 0) * factor).astype(BF16)
            pre_buf[i, blk, :, :, :size] = dq[:, :size].reshape(qn, 2, rows, size)
            bias_buf[i, 0:1] += over_rows(dq.astype(F32))

        for b in range(blocks):
            attend_back(b)
            if step == 0 and b == 0:
                g_up.second()
        dk = dk_acc[...].astype(BF16)
        dv = dv_acc[...].astype(BF16)
        bias_buf[i, 1:2] = over_rows(dv.astype(F32))
        pre_buf[i, :, :, :, size : 2 * size] = dk[:, :size].reshape(members, 2, rows, size)
        pre_buf[i, :, :, :, 2 * size : 3 * size] = dv[:, :size].reshape(members, 2, rows, size)
        for j in range(1, members):
            pre_copy(i, j).start()
        grad = dot(pre_buf[i].reshape(total, pre_buf.shape[4]), flat(h_buf[...]), 0, 0)
        g_qkv.fill(i, jnp.transpose(grad))
        for owners in (1 - side, side):
            g_qkv.first(owners, i)
        if step == 0:
            for h in range(1, half):
                sca2.hop(h)
    def bias_copy(x, i):
        to = ((dp + x) % parts, p.seq_of(i, m))
        return send(
            bias_buf.at[i], bias_land.at[side * parts + dp], bias_s.at[x, i], bias_r.at[side * parts + dp], to
        )

    for x in range(parts):
        for i in range(2):
            if x > 0:
                bias_copy(x, i).start()
            else:

                @pl.when(side != i)
                def _():
                    bias_copy(0, i).start()

    down = sca2.result()
    out = ((mid_buf[...] + down + dbias_ref[...]) * valid).astype(BF16)
    out_ref[side] = out[:rows]
    out_buf[0] = out[rows:]
    g_qkv.second()
    g_out.second()
    swap_out = swap(out_buf.at[0], out_land.at[0], 2)
    swap_out.start()
    g_up.meet()
    load_w.wait()
    for i in range(2):
        for j in range(1, members):
            frm = (m + members - j) % members
            send(pre_buf.at[i, frm], pre_land.at[i, frm], pre_s.at[i, j], pre_r.at[i, frm], p.dev(frm)).wait_recv()
        pre_land[i, m] = pre_buf[i, m]
        for j in range(members):
            block = pre_land[i, j].reshape(own, pre_land.shape[4])
            for c in range(3):
                at = c * width + p.seq_of(i, j) * size
                mine_buf[:, at : at + size] = block[:, c * size : (c + 1) * size]
    grad_h1 = None
    for c in range(3):
        w = pool[c * per_w : (c + 1) * per_w].reshape(width, width)
        more = dot(mine_buf[:, c * width : (c + 1) * width], w, 1, 1)
        grad_h1 = more if grad_h1 is None else grad_h1 + more
    normed, scale = normalize(x_buf[...].reshape(own, width).astype(F32))
    sg = (gmid_buf[...] + norm_back(grad_h1, normed, scale, gain_ref[0:1])).astype(BF16)
    out_buf[1] = sg[rows:]
    swap_sg = swap(out_buf.at[1], out_land.at[1], 3)
    swap_sg.start()
    sg_ref[side] = sg[:rows]
    vecs = jnp.concatenate(
        [over_rows(grad_h1 * normed), gain_two, over_rows(grad_h1), shift_two, bias_out, bias_down, bias_out, bias_out],
        axis=0,
    )
    for s in range(shards):
        vec_buf[s, :, :size] = vecs[:, s * size : (s + 1) * size]
    per = shards // parts
    pairs = [(i, j) for i in range(parts) for j in range(shards) if i + j > 0]

    def vec_copy(i, j):
        to = (me + j) % shards
        slot = dp * shards + me
        return send(vec_buf.at[to], vec_land.at[slot], vec_s.at[i, j], vec_r.at[slot], ((dp + i) % parts, to))

    def vec_wait(i, j):
        frm = (me + j) % shards
        x = (dp + i) % parts
        slot = x * shards + frm
        send(vec_buf.at[0], vec_land.at[slot], vec_s.at[i, j], vec_r.at[slot], (x, frm)).wait_recv()

    for i, j in pairs:
        vec_copy(i, j).start()
    vec_land[dp * shards + me] = vec_buf[me]
    g_qkv.meet()

    cols = width // parts
    gdown_ref[...] = g_down.total()[:ff, :cols]
    gout_ref[...] = g_out.total()[:size, :cols]
    g_up.third()
    for v in range(per):
        acc = g_up.total(v)
        up_ref[:, v * ff : v * ff + main] = acc[:size, :main]
        if left:
            tail = jnp.transpose(acc[low:, :LANES])
            up_ref[:, v * ff + main : (v + 1) * ff] = tail[:size, :left]
    bias_land[side * parts + dp] = bias_buf[side]
    for s in range(2):
        for x in range(parts):
            slot = s * parts + x
            away = (side != s).astype(jnp.int32) + (dp != x).astype(jnp.int32)

            @pl.when(away > 0)
            def _():
                send(
                    bias_buf.at[0], bias_land.at[slot], bias_s.at[0, 0], bias_r.at[slot], (x, p.seq_of(s, m))
                ).wait_recv()

    acc = bias_land[0]
    for i in range(1, 2 * parts):
        acc = acc + bias_land[i]
    gab_ref[0:2] = acc[0:2, :size]
    for j in range(fp // LANES):
        n = min(LANES, ff - j * LANES)
        gub_ref[:, j * LANES : j * LANES + n] = acc[2 + j : 3 + j, :n]
    g_qkv.third()
    for v in range(per):
        acc = g_qkv.total(v)
        for c in range(3):
            qkv_ref[c, :, v * size : (v + 1) * size] = acc[:size, c * size : (c + 1) * size]
    swap_out.wait_recv()
    out_ref[1 - side] = out_land[0]
    swap_sg.wait_recv()
    sg_ref[1 - side] = out_land[1]
    for i, j in pairs:
        vec_wait(i, j)
    acc = vec_land[0]
    for i in range(1, shards * parts):
        acc = acc + vec_land[i]
    ggain_ref[...] = acc[0:2, :size]
    gshift_ref[...] = acc[2:4, :size]
    gab_ref[2:3] = acc[4:5, :size]
    gdb_ref[...] = acc[5:6, :size]

    for c in (swap_x, swap_ct, swap_out, swap_sg):
        c.wait_send()
    for j in range(1, members):
        att_copy((m + j) % members).wait_send()
        for i in range(2):
            pre_copy(i, j).wait_send()
    for x in range(parts):
        for i in range(2):
            if x > 0:
                bias_copy(x, i).wait_send()
            else:

                @pl.when(side != i)
                def _():
                    bias_copy(0, i).wait_send()

    for i, j in pairs:
        vec_copy(i, j).wait_send()
    for x in (gat1, gat2, sca2, g_up, g_qkv, g_down, g_out):
        x.finish()


def layer(shards, size, ff, parts, counts, states, cotangent, gains, nbias, abias, dbias, bu, w_out, w_up, w_down, w_qkv):
    rows, width = states.shape[1:]
    members = shards // 2
    n = members // 2
    sp, fp = up128(size), up128(ff)
    own = 2 * rows
    total = members * own
    per = shards // parts
    cols = width // parts
    r16 = lambda k: -(-k // 16) * 16
    sds = jax.ShapeDtypeStruct
    block = (members, 2, rows)
    wp = up128(3 * size)
    w4 = w_qkv.reshape(3 * width // own, 2, rows, width)
    return pl.pallas_call(
        functools.partial(layer_kernel, shards, size, ff, parts),
        out_shape=[
            sds((2, rows, width), BF16), sds((2, rows, width), BF16), sds((3, size, per * size), F32),
            sds((size, cols), F32), sds((3, size), F32), sds((2, size), F32), sds((2, size), F32),
            sds((size, per * ff), F32), sds((1, ff), F32), sds((ff, cols), F32), sds((1, size), F32),
        ],
        in_specs=[pl.BlockSpec(memory_space=pltpu.SMEM)]
        + [pl.BlockSpec(memory_space=VMEM)] * 7
        + [pl.BlockSpec(memory_space=pl.ANY)] * 4,
        out_specs=[pl.BlockSpec(memory_space=VMEM)] * 11,
        scratch_shapes=[
            VMEM(w4.shape, BF16), VMEM(block + (width,), BF16), VMEM(block + (width,), BF16), VMEM(block + (width,), BF16),
            VMEM((2, rows, width), BF16), VMEM((rows, width), BF16), VMEM((own, width), F32), VMEM((own, width), F32),
            VMEM(block + (6 * sp,), BF16), VMEM(block + (2 * sp,), F32), VMEM(block + (2 * sp,), BF16),
            VMEM(block + (2 * sp,), BF16), VMEM((2, total // QB, 8, QB), F32), VMEM((own, 3 * width), BF16),
            VMEM(block + (2 * fp,), BF16), VMEM(block + (2 * fp,), BF16), VMEM(block + (2 * sp,), BF16),
            VMEM((total, sp), F32), VMEM((total, sp), F32), VMEM((2,) + block + (wp,), BF16), VMEM((2,) + block + (wp,), BF16),
            VMEM((width, 6 * sp), BF16), VMEM(w_out.shape, BF16), VMEM((2 * sp, width), BF16), VMEM((2 * fp, width), BF16),
            VMEM((2 * fp, width), BF16),
            VMEM((2, max(6 * sp, 2 * fp)), F32),
            VMEM((shards, 8, LANES), F32), VMEM((shards * parts, 8, LANES), F32), VMEM((2, 8, LANES), F32),
            VMEM((2 * parts, 8, LANES), F32), VMEM((2, rows, width), BF16),
            VMEM((2, rows, width), BF16),
            DMA((4,)), DMA((4,)), DMA((members,)), DMA((members,)), DMA((2, members)), DMA((2, members)),
            DMA((parts, shards)), DMA((parts * shards,)), DMA((parts, 2)), DMA((2 * parts,)), DMA((6,)),
        ]
        + gather_sems(n) * 4
        + scatter_scratch(n, rows, width) * 2
        + rows_scratch(shards, parts, size, ff // LANES * LANES, ff % LANES)
        + rows_scratch(shards, parts, size, wp, 0)
        + cols_scratch(parts, r16(ff), up128(cols))
        + cols_scratch(parts, r16(size), up128(cols)),
        name="layer",
        compiler_params=pltpu.CompilerParams(
            collective_id=0, has_side_effects=True, vmem_limit_bytes=63 << 20
        ),
    )(counts, states, cotangent, gains, nbias, abias, dbias, bu, w_out, w_up, w_down, w4)


def deliver_kernel(*refs):
    count = len(refs) // 2
    for i in range(count):
        refs[count + i][...] = refs[i][...]


def deliver(*arrays):
    return pl.pallas_call(
        deliver_kernel,
        out_shape=[jax.ShapeDtypeStruct(x.shape, x.dtype) for x in arrays],
        in_specs=[pl.BlockSpec(memory_space=VMEM)] * len(arrays),
        out_specs=[pl.BlockSpec(memory_space=VMEM)] * len(arrays),
        name="deliver",
    )(*arrays)


def body(
    states, counts, cotangent, w_qkv, w_out, attn_bias, norm_gain, norm_bias,
    w_up, up_bias, w_down, down_bias,
):
    width = states.shape[2]
    shards = lax.axis_size("seq")
    parts = lax.axis_size("dp")
    size = width // HEADS
    ff = w_up.shape[1] // shards
    members = shards // 2
    me = lax.axis_index("seq")
    m = (me + (members // 2) * (me // members)) % members
    units = (m, members + (m + members // 2) % members)

    def mine(x, axis, count):
        return jnp.stack([lax.dynamic_slice_in_dim(x, u * count, count, axis) for u in units])

    layer_out, state_grad, g_qkv, g_out, g_ab, g_gain, g_shift, g_up, g_ub, g_down, g_db = deliver(
        *layer(
            shards, size, ff, parts, counts, states, cotangent, norm_gain, norm_bias, attn_bias, down_bias[None],
            mine(up_bias[None], 1, ff), w_out, w_up.T, w_down, w_qkv,
        )
    )
    return (
        layer_out, state_grad, g_qkv, g_out, g_ab, g_gain, g_shift, g_up,
        g_ub.reshape(ff), g_down, g_db.reshape(size),
    )


def solution(mesh):
    placed = (P("dp", "seq", None), P("dp", None), P("dp", "seq", None)) + (P(),) * 9
    return jax.shard_map(
        body,
        mesh=mesh,
        in_specs=placed,
        out_specs=(
            P("dp", "seq", None), P("dp", "seq", None), P(None, "seq", "dp"), P("seq", "dp"),
            P(None, "seq"), P(None, "seq"), P(None, "seq"), P("seq", "dp"), P("seq"),
            P("seq", "dp"), P("seq"),
        ),
        check_vma=False,
    )
```

```python
import functools
import math

import jax
import jax.numpy as jnp
from jax import lax
from jax.experimental import pallas as pl
from jax.experimental.pallas import tpu as pltpu
from jax.sharding import PartitionSpec as P

HEADS = 16
EPS = 1e-06
NEG = -1e30
F32 = jnp.float32
BF16 = jnp.bfloat16
MESH = pl.DeviceIdType.MESH
VMEM = pltpu.VMEM
DMA = pltpu.SemaphoreType.DMA


def mm(spec, a, b):
    return jnp.einsum(spec, a, b, preferred_element_type=F32)


def dot(a, b, ca=1, cb=0):
    return lax.dot_general(a, b, (((ca,), (cb,)), ((), ())), preferred_element_type=F32)


def pad_to(x, axis, size):
    pads = [(0, 0)] * x.ndim
    pads[axis] = (0, size - x.shape[axis])
    return jnp.pad(x, pads)


def up128(n):
    return -(-n // 128) * 128


def normalize(values):
    mean = jnp.mean(values, axis=-1, keepdims=True)
    centred = values - mean
    scale = lax.rsqrt(jnp.mean(centred * centred, axis=-1, keepdims=True) + EPS)
    return (centred * scale, scale)


def norm_back(grad_norm, normed, scale, gain):
    scaled = grad_norm * gain
    return scale * (
        scaled
        - jnp.mean(scaled, axis=-1, keepdims=True)
        - normed * jnp.mean(scaled * normed, axis=-1, keepdims=True)
    )


def gelu_both(v):
    c, a = 0.7978845608028654, 0.044715
    sq = v * v
    t = jnp.tanh(c * (v + a * v * sq))
    half = 0.5 * (1.0 + t)
    return v * half, half + 0.5 * v * (1.0 - t * t) * (c * (1.0 + 3.0 * a * sq))


def send(src, dst, s, r, dev):
    return pltpu.make_async_remote_copy(
        src_ref=src, dst_ref=dst, send_sem=s, recv_sem=r, device_id=dev, device_id_type=MESH
    )


class Place:
    def __init__(self, shards, parts):
        self.shards, self.parts = shards, parts
        self.members = shards // 2
        self.n = self.members // 2
        self.half = self.n // 2
        self.me = lax.axis_index("seq")
        self.dp = lax.axis_index("dp")
        self.side = self.me // self.members
        self.m = (self.me + (self.members // 2) * self.side) % self.members
        self.chip = self.m // 2
        self.core = self.m % 2
        odd = self.chip % 2
        self.pos = (1 - odd) * (self.chip // 2) + odd * (self.n - 1 - self.chip // 2)
        self.to = (self.at(1, 1) * 2 + self.core, self.at(1, 0) * 2 + self.core)
        self.sib = self.chip * 2 + 1 - self.core
        self.partner = {"seq": self.seq_of(1 - self.side, self.m)}

    def seq_of(self, side, m):
        return side * self.members + (m + (self.members // 2) * side) % self.members

    def dev(self, m):
        return {"seq": self.seq_of(self.side, m)}

    def at(self, k, d):
        p = (self.pos + (self.n - k if d == 0 else k)) % self.n
        hi = p // self.half
        return (1 - hi) * 2 * p + hi * (2 * (self.n - 1 - p) + 1)

    def others(self):
        return [
            ((self.dp + i) % self.parts, (self.me + j) % self.shards)
            for i in range(self.parts) for j in range(self.shards) if i + j > 0
        ]


def gather_sems(n):
    return [DMA((2, n // 2 + 1, 2))] * 4


class Gather:
    def __init__(self, place, buf, base, sems):
        self.place, self.buf, self.base = place, buf, base
        self.ring_s, self.ring_r, self.sib_s, self.sib_r = sems
        self.sent = []

    def copy(self, k, d, g, to_sib):
        p = self.place
        block = self.buf.at[self.base + p.at(k, d) * 2 + p.core, g]
        s, r = (self.sib_s, self.sib_r) if to_sib else (self.ring_s, self.ring_r)
        return send(block, block, s.at[d, k, g], r.at[d, k, g], p.dev(p.sib if to_sib else p.to[d]))

    def go(self, *args):
        c = self.copy(*args)
        c.start()
        self.sent.append(c)

    def units(self, k):
        if k == self.place.half:
            return [(0, 0), (1, 1)]
        return [(0, 0), (1, 1), (0, 1), (1, 0)]

    def passes(self, k, d, g):
        return k < self.place.half - 1 or (k == self.place.half - 1 and g == d)

    def start(self, g):
        for d in (g, 1 - g):
            if self.passes(0, d, g):
                self.go(0, d, g, False)
        self.go(0, g, g, True)

    def start_both(self):
        for d, g in self.units(0):
            if self.passes(0, d, g):
                self.go(0, d, g, False)
        for g in range(2):
            self.go(0, g, g, True)

    def hop(self, k):
        for d, g in self.units(k):
            self.copy(k - 1, d, g, False).wait_recv()
            if self.passes(k, d, g):
                self.go(k, d, g, False)
            self.go(k, d, g, True)

    def ready(self, k):
        for d, g in self.units(k):
            if k > 0 or d == g:
                self.copy(k, d, g, True).wait_recv()

    def blocks(self, k):
        if k == 0 or k == self.place.half:
            return [self.place.at(k, 0)]
        return [self.place.at(k, 0), self.place.at(k, 1)]

    def finish(self):
        for c in self.sent:
            c.wait_send()


def scatter_scratch(n, rows, width):
    return [
        VMEM((n, 2, rows, width), BF16), VMEM((2, n // 2, 2, rows, width), BF16),
        DMA((n,)), DMA((n,)), DMA((2, n // 2, 2)), DMA((2, n // 2, 2)),
    ]


class Scatter:
    def __init__(self, place, part, base, scratch):
        self.place, self.part, self.base = place, part, base
        self.sib_land, self.land, self.sib_s, self.sib_r, self.ring_s, self.ring_r = scratch
        self.sent = []
        self.have = set()

    def slot(self, k, d):
        if k == 0:
            return 0
        return self.place.n - 1 if k == self.place.half else 2 * k - 1 + d

    def sib_copy(self, k, d):
        p, i = self.place, self.slot(k, d)
        src = self.part.at[self.base + p.at(k, d) * 2 + 1 - p.core]
        return send(src, self.sib_land.at[i], self.sib_s.at[i], self.sib_r.at[i], p.dev(p.sib))

    def give(self, k, d):
        c = self.sib_copy(k, d)
        c.start()
        self.sent.append(c)

    def from_sib(self, k, d):
        i = self.slot(k, d)
        if i not in self.have:
            self.have.add(i)
            self.sib_copy(k, d).wait_recv()
        return self.sib_land.at[i]

    def dist(self, h, d, g):
        return self.place.half - h if g == d else self.place.half - 1 - h

    def block(self, h, d, g):
        p = self.place
        return self.base + p.at(self.dist(h, d, g), 1 - d) * 2 + p.core

    def ring_copy(self, h, d, g):
        return send(
            self.part.at[self.block(h, d, g), g], self.land.at[d, h, g],
            self.ring_s.at[d, h, g], self.ring_r.at[d, h, g], self.place.dev(self.place.to[d]),
        )

    def hop(self, h):
        for d, g in [(0, 0), (1, 1), (0, 1), (1, 0)]:
            j = self.dist(h, d, g)
            if j == 0:
                continue
            own = self.block(h, d, g)
            val = self.part[own, g].astype(F32) + self.from_sib(j, 1 - d)[g].astype(F32)
            if h > 0:
                self.ring_copy(h - 1, d, g).wait_recv()
                val = val + self.land[d, h - 1, g].astype(F32)
            self.part[own, g] = val.astype(BF16)
            c = self.ring_copy(h, d, g)
            c.start()
            self.sent.append(c)

    def result(self):
        p = self.place
        out = []
        for g in range(2):
            val = self.part[self.base + p.m, g].astype(F32) + self.from_sib(0, 0)[g].astype(F32)
            for d in range(2):
                h = p.half - 1 if g == d else p.half - 2
                self.ring_copy(h, d, g).wait_recv()
                val = val + self.land[d, h, g].astype(F32)
            out.append(val)
        return jnp.concatenate(out, axis=0)

    def finish(self):
        for c in self.sent:
            c.wait_send()


def rows_scratch(shards, parts, size, width, left):
    gh, per = shards // parts, shards // parts
    r16 = lambda k: -(-k // 16) * 16
    packed = r16(gh * size) + r16(left) * -(-gh * size // width)
    rows = r16(size) + r16(left)
    return [
        VMEM((parts, 2, packed, width), BF16), VMEM((parts, 2, packed, width), BF16), VMEM((packed, width), BF16),
        VMEM((gh, rows, width), BF16), VMEM((per, rows, width), BF16),
        DMA((parts, 2)), DMA((parts, 2)), DMA((2,)), DMA((gh,)), DMA((per,)), DMA,
    ]


class Rows:
    def __init__(self, place, size, scratch):
        self.place, self.size = place, size
        self.buf, self.land, self.met, self.out, self.last = scratch[:5]
        self.s1, self.r1, self.sc, self.s2, self.r2, self.loc = scratch[5:]
        self.gh = self.out.shape[0]
        self.hp = place.parts // 2
        self.per = place.shards // place.parts
        self.below = (self.gh * size + 15) // 16 * 16
        self.low = (size + 15) // 16 * 16

    def fill(self, i, tall, turned=None):
        p, n, width = self.place, self.gh * self.size, self.buf.shape[3]
        for side in range(2):
            for q in range(self.hp):
                at = (side * p.members + q * self.gh) * self.size
                self.buf[i * self.hp + q, side, :n, : tall.shape[1]] = tall[at : at + n].astype(BF16)
                if turned is not None:
                    high = turned.shape[0]
                    for c in range(0, n, width):
                        to = self.below + c // width * high
                        cut = turned[:, at + c : at + min(c + width, n)].astype(BF16)
                        self.buf[i * self.hp + q, side, to : to + high, : cut.shape[1]] = cut

    def share(self, j, side):
        p = self.place
        x = (p.dp + j) % p.parts
        return send(
            self.buf.at[x, side], self.land.at[p.dp, side], self.s1.at[j, side], self.r1.at[p.dp, side], (x, p.me)
        )

    def first(self, side, unit=None):
        p = self.place
        for j in range(1, p.parts):
            if unit is None:
                self.share(j, side).start()
            else:

                @pl.when((p.dp + j) % p.parts // self.hp == unit)
                def _():
                    self.share(j, side).start()

    def shares(self, side):
        p = self.place
        for j in range(1, p.parts):
            x = (p.dp + j) % p.parts
            send(
                self.buf.at[x, side], self.land.at[x, side], self.s1.at[j, side], self.r1.at[x, side], (x, p.me)
            ).wait_recv()
        total = self.buf[p.dp, side].astype(F32)
        for j in range(1, p.parts):
            total = total + self.land[(p.dp + j) % p.parts, side].astype(F32)
        return total

    def cross(self):
        p = self.place
        return send(self.buf.at[p.dp, 1 - p.side], self.met, self.sc.at[0], self.sc.at[1], p.partner)

    def second(self):
        away = 1 - self.place.side
        self.buf[self.place.dp, away] = self.shares(away).astype(BF16)
        self.cross().start()

    def deliver(self, k, act, act_own):
        p = self.place
        unit = p.seq_of(p.dp // self.hp, p.m)
        keeper = unit // self.per
        owner = p.side * p.members + (p.dp % self.hp) * self.gh + k
        slot = unit % self.per
        away = (keeper != p.dp).astype(jnp.int32) + (owner != p.me).astype(jnp.int32)
        block = self.out.at[k]

        @pl.when(away > 0)
        def _():
            act(send(block, self.last.at[slot], self.s2.at[k], self.r2.at[slot], (keeper, owner)))

        if act_own:

            @pl.when(away == 0)
            def _():
                c = pltpu.make_async_copy(block, self.last.at[slot], self.loc)
                c.start()
                c.wait()

    def meet(self):
        total = self.shares(self.place.side)
        self.cross().wait_recv()
        total = total + self.met[...].astype(F32)
        size, high = self.size, self.out.shape[1] - self.low
        if high:
            parts = range(self.below, total.shape[0], high)
            turned = jnp.concatenate([total[at : at + high] for at in parts], axis=1)
        for k in range(self.gh):
            self.out[k, :size] = total[k * size : (k + 1) * size].astype(BF16)
            if high:
                self.out[k, self.low :, :size] = turned[:, k * size : (k + 1) * size].astype(BF16)
            self.deliver(k, lambda c: c.start(), True)

    def third(self):
        p = self.place
        for v in range(self.per):
            unit = p.dp * self.per + v
            i = unit // p.members
            m = (unit + (p.members // 2) * i) % p.members
            x = i * self.hp + p.me % p.members // self.gh
            away = (x != p.dp).astype(jnp.int32) + (m != p.m).astype(jnp.int32)

            @pl.when(away > 0)
            def _():
                frm = (x, p.seq_of(p.side, m))
                send(self.out.at[0], self.last.at[v], self.s2.at[0], self.r2.at[v], frm).wait_recv()

    def total(self, v):
        return self.last[v].astype(F32)

    def finish(self):
        for j in range(1, self.place.parts):
            for side in range(2):
                self.share(j, side).wait_send()
        self.cross().wait_send()
        for k in range(self.gh):
            self.deliver(k, lambda c: c.wait_send(), False)


def cols_scratch(parts, rows, width):
    return [
        VMEM((parts, 2, rows, width), BF16), VMEM((parts, 2, rows, width), BF16), VMEM((rows, width), BF16),
        DMA((parts, 2)), DMA((parts, 2)), DMA, DMA,
    ]


class Cols:
    def __init__(self, place, scratch):
        self.place = place
        self.buf, self.land, self.last, self.s1, self.r1, self.s2, self.r2 = scratch

    def put(self, i, val):
        p = self.place
        cols = val.shape[1] // p.parts
        val = val.astype(BF16)
        for x in range(p.parts):
            self.buf[x, i, : val.shape[0], :cols] = val[:, x * cols : (x + 1) * cols]

    def share(self, j, i):
        p = self.place
        x = (p.dp + j) % p.parts
        return send(self.buf.at[x, i], self.land.at[p.dp, i], self.s1.at[j, i], self.r1.at[p.dp, i], (x, p.me))

    def cross(self):
        p = self.place
        return send(self.buf.at[p.dp, 1 - p.side], self.last, self.s2, self.r2, p.partner)

    def first(self, i):
        for j in range(1, self.place.parts):
            self.share(j, i).start()

    def dp_sum(self, i):
        p = self.place
        val = self.buf[p.dp, i].astype(F32)
        for j in range(1, p.parts):
            x = (p.dp + j) % p.parts
            send(self.buf.at[x, i], self.land.at[x, i], self.s1.at[j, i], self.r1.at[x, i], (x, p.me)).wait_recv()
            val = val + self.land[x, i].astype(F32)
        return val

    def second(self):
        p = self.place
        self.buf[p.dp, 1 - p.side] = self.dp_sum(1 - p.side).astype(BF16)
        self.cross().start()

    def total(self):
        val = self.dp_sum(self.place.side)
        self.cross().wait_recv()
        return val + self.last[...].astype(F32)

    def finish(self):
        for j in range(1, self.place.parts):
            for i in range(2):
                self.share(j, i).wait_send()
        self.cross().wait_send()


def chip_rows(ref, chip, base=0):
    val = ref[pl.ds(base + 2 * chip, 2)]
    return val.reshape(-1, val.shape[-1])


def chip_put(ref, chip, val, base=0):
    ref[pl.ds(base + 2 * chip, 2)] = val.astype(ref.dtype).reshape((2,) + ref.shape[1:])


def ids_at(positions, ends):
    total = (positions >= ends[0]).astype(jnp.int32)
    for end in ends[1:]:
        total = total + (positions >= end).astype(jnp.int32)
    return total


def log2(n):
    assert n & (n - 1) == 0
    return n.bit_length() - 1


QB = 256
LANES = 128


def layer_kernel(
    shards, size, ff, parts,
    counts_ref, x_ref, ct_ref, gain_ref, nbias_ref, abias_ref, dbias_ref, bu_ref, wout_hbm, wu_hbm, wd_hbm, w_hbm,
    out_ref, sg_ref, qkv_ref, gout_ref, gab_ref, ggain_ref, gshift_ref, up_ref, gub_ref, gdown_ref, gdb_ref,
    pool, h_buf, m_buf, part2, x_buf, ct_buf, mid_buf, gmid_buf, qkv_buf, att_buf, att_b, att_land, lse_buf, mine_buf,
    act_buf, ghid_buf, gatt_buf, dk_acc, dv_acc, pre_buf, pre_land, wq_buf, wout_buf, wo_buf, wu_buf, wd_buf, row_buf,
    vec_buf, vec_land, bias_buf, bias_land, out_buf, out_land,
    ex_s, ex_r, att_s, att_r, pre_s, pre_r, vec_s, vec_r, bias_s, bias_r, loc, *rest,
):
    p = Place(shards, parts)
    me, dp, side, m = p.me, p.dp, p.side, p.m
    bar = pltpu.get_barrier_semaphore()
    for dev in p.others():
        pl.semaphore_signal(bar, inc=1, device_id=dev, device_id_type=MESH)
    rows, width = x_ref.shape[1:]
    members, half = p.members, p.half
    own = 2 * rows
    total = members * own
    sp = wo_buf.shape[0] // 2
    fp = wu_buf.shape[0] // 2
    units = [p.seq_of(i, m) for i in range(2)]

    span = (ff + 15) // 16 * 16 + 16
    windows = [u * ff // 16 * 16 - 16 * (u // (shards - 1)) for u in units]
    load_w0 = pltpu.make_async_copy(w_hbm, pool, loc.at[0])
    load_out = pltpu.make_async_copy(wout_hbm, wout_buf, loc.at[1])
    loads = [
        pltpu.make_async_copy(
            hbm.at[pl.ds(pl.multiple_of(windows[i], 16), span)], buf.at[pl.ds(i * fp, span)], loc.at[2 + 2 * i + j]
        )
        for j, (hbm, buf) in enumerate(((wu_hbm, wu_buf), (wd_hbm, wd_buf)))
        for i in range(2)
    ]
    load_w0.start()
    load_out.start()
    for c in loads:
        c.start()
    factor = 1.0 / math.sqrt(size)
    at_part, at_h2, at_gy = 0, members, 2 * members
    gat1 = Gather(p, h_buf, 0, rest[0:4])
    gaty = Gather(p, pool, at_gy, rest[4:8])
    gat = Gather(p, pool, at_h2, rest[8:12])
    gat2 = Gather(p, m_buf, 0, rest[12:16])
    sca = Scatter(p, pool, at_part, rest[16:22])
    sca2 = Scatter(p, part2, 0, rest[22:28])
    g_up = Rows(p, size, rest[28:39])
    g_qkv = Rows(p, size, rest[39:50])
    g_down = Cols(p, rest[50:57])
    g_out = Cols(p, rest[57:64])

    ends = [counts_ref[side, 0]]
    for i in range(1, counts_ref.shape[1]):
        ends.append(ends[-1] + counts_ref[side, i])

    def ids_of(t):
        mem = lax.shift_right_logical(t, log2(own))
        rho = lax.shift_right_logical(t, log2(rows)) & 1
        sig = rho + side - 2 * rho * side
        seq = sig * members + ((mem + (members // 2) * sig) & (members - 1))
        return ids_at(seq * rows + (t & (rows - 1)), ends)

    def iota(shape, dim):
        return lax.broadcasted_iota(jnp.int32, shape, dim)

    valid = (ids_of(iota((own, 1), 0) + m * own) < counts_ref.shape[1]).astype(F32)

    def swap(src, dst, i):
        return send(src, dst, ex_s.at[i], ex_r.at[i], p.partner)

    def norm_one(g):
        normed, _ = normalize(x_buf[g].astype(F32))
        h_buf[m, g] = (normed * gain_ref[0:1] + nbias_ref[0:1]).astype(BF16)

    x_buf[0] = x_ref[side]
    norm_one(0)
    pl.semaphore_wait(bar, len(p.others()))
    swap_x = swap(x_ref.at[1 - side], x_buf.at[1], 0)
    swap_ct = swap(ct_ref.at[1 - side], ct_buf, 1)
    swap_x.start()
    gat1.start(0)
    swap_ct.start()

    def iota2(shape):
        return iota(shape, 0), iota(shape, 1)

    def one_hot(hit, kind):
        return jnp.where(hit, 1.0, 0.0).astype(kind)

    at, lane = iota2((width, sp))
    pick = [jnp.logical_and(at == lane + u * size, lane < size) for u in units]
    exact = lax.dot_general(
        abias_ref[...], jnp.concatenate([one_hot(h, F32) for h in pick], axis=1), (((1,), (0,)), ((), ())),
        preferred_element_type=F32, precision=lax.Precision.HIGHEST,
    )
    row_buf[...] = jnp.zeros(row_buf.shape, F32)
    row_buf[0:1, : 2 * sp] = exact[0:1]
    row_buf[0:1, 4 * sp : 6 * sp] = exact[1:2]
    for i in range(2):
        row_buf[1:2, i * fp : i * fp + ff] = bu_ref[i]
    pick = jnp.concatenate([one_hot(h, BF16) for h in pick], axis=1)
    load_w0.wait()
    per_w = width // own
    for c in range(3):
        w = pool[c * per_w : (c + 1) * per_w].reshape(width, width)
        wq_buf[:, 2 * c * sp : 2 * (c + 1) * sp] = dot(w, pick).astype(BF16)
    swap_x.wait_recv()
    norm_one(1)
    gat1.start(1)
    pool[at_gy + m, 0] = (ct_ref[side].astype(F32) * valid[:rows]).astype(BF16)
    swap_ct.wait_recv()
    pool[at_gy + m, 1] = (ct_buf[...].astype(F32) * valid[rows:]).astype(BF16)
    load_out.wait()
    at, lane = iota2((sp, width))
    for i in range(2):
        hit = jnp.logical_and(lane == at + units[i] * size, at < size)
        wo_buf[i * sp : (i + 1) * sp] = dot(one_hot(hit, BF16), wout_buf[...]).astype(BF16)
    for c in loads:
        c.wait()
    at, lane = iota2((fp, span))
    for i in range(2):
        hit = jnp.logical_and(lane == at + (units[i] * ff - windows[i]), at < ff)
        for buf in (wu_buf, wd_buf):
            cut = dot(one_hot(hit, BF16), buf[i * fp : i * fp + span])
            buf[i * fp : (i + 1) * fp] = cut.astype(BF16)

    def project(chip):
        out = dot(chip_rows(h_buf, chip), wq_buf[...]) + row_buf[0:1, : 6 * sp]
        out = jnp.concatenate([out[:, : 2 * sp] * factor, out[:, 2 * sp :]], axis=1)
        chip_put(qkv_buf, chip, out)

    for k in range(1, half + 1):
        gat1.hop(k)
        gat1.ready(k - 1)
        if k == half - 1:
            gaty.start_both()
        for chip in gat1.blocks(k - 1):
            project(chip)
    gat1.ready(half)
    project(p.at(half, 0))

    qn = QB // own

    def att_copy(to):
        return send(att_b.at[to], att_land.at[m], att_s.at[to], att_r.at[m], p.dev(to))

    def lanes_of(part, i):
        return slice((2 * part + i) * sp, (2 * part + i + 1) * sp)

    row_ids = ids_of(iota((1, total), 1))

    def attend(b):
        query_ids = ids_of(iota((QB, 1), 0) + b * QB)
        same = query_ids == row_ids
        for i in range(2):
            query = qkv_buf[pl.ds(b * qn, qn), :, :, lanes_of(0, i)].reshape(QB, sp)
            keys = qkv_buf[:, :, :, lanes_of(1, i)].reshape(total, sp)
            values = qkv_buf[:, :, :, lanes_of(2, i)].reshape(total, sp)
            scores = jnp.where(same, dot(query, keys, 1, 1), NEG)
            high = jnp.max(scores, axis=-1, keepdims=True)
            weights = jnp.exp(scores - high)
            sums = jnp.sum(weights, axis=-1, keepdims=True)
            out = (dot(weights.astype(BF16), values) / sums).reshape(qn, 2, rows, sp)
            att_buf[pl.ds(b * qn, qn), :, :, i * sp : (i + 1) * sp] = out
            att_b[pl.ds(b * qn, qn), :, :, i * sp : (i + 1) * sp] = out.astype(BF16)
            lse = jnp.broadcast_to(high + jnp.log(sums), (QB, LANES))
            lse_buf[i, b] = jnp.transpose(lse)[0:8]
        for t in range(qn):
            to = b * qn + t

            @pl.when(to != m)
            def _():
                att_copy(to).start()

    blocks = total // QB
    pl.loop(0, blocks // 2)(attend)
    gaty.hop(1)
    pl.loop(blocks // 2, blocks)(attend)
    for k in range(2, half + 1):
        gaty.hop(k)
    att_land[m] = att_b[m]
    for j in range(1, members):
        frm = (m + members - j) % members
        send(att_b.at[frm], att_land.at[frm], att_s.at[frm], att_r.at[frm], p.dev(frm)).wait_recv()
    for j in range(members):
        for i in range(2):
            at = p.seq_of(i, j) * size
            mine_buf[:, at : at + size] = att_land[j].reshape(own, 2 * sp)[:, i * sp : i * sp + size]
    inputs = x_buf[...].reshape(own, width).astype(F32)
    mid = inputs + dot(mine_buf[:, :width], wout_buf[...]) + abias_ref[2:3]
    mid_buf[...] = mid
    normed, _ = normalize(mid)
    pool[at_h2 + m] = (normed * gain_ref[1:2] + nbias_ref[1:2]).astype(BF16).reshape(2, rows, width)
    gat.start_both()

    def forward(chip):
        hidden = dot(chip_rows(pool, chip, at_h2), wu_buf[...], 1, 1) + row_buf[1:2, : 2 * fp]
        act, slope = gelu_both(hidden)
        chip_put(act_buf, chip, act)
        ghid = (dot(chip_rows(pool, chip, at_gy), wd_buf[...], 1, 1) * slope).astype(BF16)
        chip_put(ghid_buf, chip, ghid)
        chip_put(pool, chip, dot(ghid, wu_buf[...]), at_part)

    for k in range(half + 1):
        if k < half:
            gat.hop(k + 1)
        gaty.ready(k)
        gat.ready(k)
        for d, chip in enumerate(gat.blocks(k)):
            forward(chip)
            sca.give(k, d)

    def flat(val):
        return val.reshape(total, val.shape[-1])

    for h in range(half):
        sca.hop(h)
        if h == 0:
            gdown = dot(flat(act_buf[...]), flat(pool[at_gy : at_gy + members]), 0, 0)
            for i in range(2):
                g_down.put(i, gdown[i * fp : i * fp + (ff + 15) // 16 * 16])
            g_down.first(1 - side)
    gup = dot(flat(ghid_buf[...]), flat(pool[at_h2 : at_h2 + members]), 0, 0)
    main, left = ff // LANES * LANES, ff % LANES
    low = (size + 15) // 16 * 16
    for i in range(2):
        turned = gup[i * fp + main : i * fp + main + (left + 15) // 16 * 16] if left else None
        g_up.fill(i, jnp.transpose(gup[i * fp : i * fp + main]), turned)
    g_up.first(1 - side)
    g_down.first(side)
    grad_h2 = sca.result()
    normed, scale = normalize(mid_buf[...])
    gy_own = pool[at_gy + m].reshape(own, width).astype(F32)
    gmid = gy_own + norm_back(grad_h2, normed, scale, gain_ref[1:2])
    gmid_buf[...] = gmid
    m_buf[m] = gmid.astype(BF16).reshape(2, rows, width)
    gat2.start_both()
    g_up.first(side)

    def over_rows(val):
        return jnp.sum(val, axis=0, keepdims=True)

    gain_two, shift_two, bias_out, bias_down = (
        over_rows(grad_h2 * normed), over_rows(grad_h2), over_rows(gmid), over_rows(gy_own)
    )
    bias_up = over_rows(flat(ghid_buf[...]).astype(F32))

    def down_part(chip):
        chip_put(part2, chip, dot(chip_rows(act_buf, chip), wd_buf[...]))

    def back(chip):
        block = chip_rows(m_buf, chip)
        chip_put(gatt_buf, chip, dot(block, wo_buf[...], 1, 1))
        return dot(chip_rows(att_b, chip), block, 0, 0)

    gout = None
    for k in range(half + 1):
        for d, chip in enumerate(gat.blocks(k)):
            down_part(chip)
            sca2.give(k, d)
        if k < half:
            gat2.hop(k + 1)
        if k == half - 1:
            g_down.second()
        gat2.ready(k)
        for chip in gat2.blocks(k):
            more = back(chip)
            gout = more if gout is None else gout + more
    for i in range(2):
        g_out.put(i, gout[i * sp : i * sp + low])
    for i in (1 - side, side):
        g_out.first(i)
    for x in (gat, gaty, sca):
        x.finish()
    load_w = pltpu.make_async_copy(w_hbm, pool, loc.at[0])
    load_w.start()
    sca2.hop(0)

    col_ids = ids_of(iota((total, 1), 0))

    def pre_copy(i, j):
        to = (m + j) % members
        return send(pre_buf.at[i, to], pre_land.at[i, m], pre_s.at[i, j], pre_r.at[i, m], p.dev(to))

    pre_buf[:, :, :, :, 3 * size :] = jnp.zeros(pre_buf.shape[:4] + (pre_buf.shape[4] - 3 * size,), BF16)
    bias_buf[...] = jnp.zeros(bias_buf.shape, F32)
    for i in range(2):
        for j in range(fp // LANES):
            bias_buf[i, 2 + j : 3 + j] = bias_up[:, i * fp + j * LANES : i * fp + (j + 1) * LANES]

    def lanes_at(k):
        return pl.ds(pl.multiple_of(k * sp, LANES), sp)

    mine_last = dp // g_qkv.hp
    for step in range(2):
        i = mine_last if step == 1 else 1 - mine_last
        dk_acc[...] = jnp.zeros(dk_acc.shape, F32)
        dv_acc[...] = jnp.zeros(dv_acc.shape, F32)

        def attend_back(b):
            blk = pl.ds(b * qn, qn)
            query = qkv_buf[blk, :, :, lanes_at(i)].reshape(QB, sp)
            keys = qkv_buf[:, :, :, lanes_at(2 + i)].reshape(total, sp)
            values = qkv_buf[:, :, :, lanes_at(4 + i)].reshape(total, sp)
            grad = gatt_buf[blk, :, :, lanes_at(i)].reshape(QB, sp)
            att = att_buf[blk, :, :, lanes_at(i)].reshape(QB, sp)
            delta = jnp.sum(grad.astype(F32) * att, axis=-1, keepdims=True)
            delta = jnp.transpose(jnp.broadcast_to(delta, (QB, LANES)))[0:1]
            same = col_ids == ids_of(iota((1, QB), 1) + b * QB)
            probs = jnp.exp(jnp.where(same, dot(keys, query, 1, 1), NEG) - lse_buf[i, b][0:1])
            grad_scores = (probs * (dot(values, grad, 1, 1) - delta)).astype(BF16)
            dv_acc[...] += dot(probs.astype(BF16), grad)
            dk_acc[...] += dot(grad_scores, query)
            dq = (dot(grad_scores, keys, 0, 0) * factor).astype(BF16)
            pre_buf[i, blk, :, :, :size] = dq[:, :size].reshape(qn, 2, rows, size)
            bias_buf[i, 0:1] += over_rows(dq.astype(F32))

        for b in range(blocks):
            attend_back(b)
            if step == 0 and b == 0:
                g_up.second()
        dk = dk_acc[...].astype(BF16)
        dv = dv_acc[...].astype(BF16)
        bias_buf[i, 1:2] = over_rows(dv.astype(F32))
        pre_buf[i, :, :, :, size : 2 * size] = dk[:, :size].reshape(members, 2, rows, size)
        pre_buf[i, :, :, :, 2 * size : 3 * size] = dv[:, :size].reshape(members, 2, rows, size)
        for j in range(1, members):
            pre_copy(i, j).start()
        grad = dot(pre_buf[i].reshape(total, pre_buf.shape[4]), flat(h_buf[...]), 0, 0)
        g_qkv.fill(i, jnp.transpose(grad))
        for owners in (1 - side, side):
            g_qkv.first(owners, i)
        if step == 0:
            for h in range(1, half):
                sca2.hop(h)
    def bias_copy(x, i):
        to = ((dp + x) % parts, p.seq_of(i, m))
        return send(
            bias_buf.at[i], bias_land.at[side * parts + dp], bias_s.at[x, i], bias_r.at[side * parts + dp], to
        )

    for x in range(parts):
        for i in range(2):
            if x > 0:
                bias_copy(x, i).start()
            else:

                @pl.when(side != i)
                def _():
                    bias_copy(0, i).start()

    down = sca2.result()
    out = ((mid_buf[...] + down + dbias_ref[...].reshape(1, width)) * valid).astype(BF16)
    out_ref[side] = out[:rows]
    out_buf[0] = out[rows:]
    g_qkv.second()
    g_out.second()
    swap_out = swap(out_buf.at[0], out_land.at[0], 2)
    swap_out.start()
    g_up.meet()
    load_w.wait()
    for i in range(2):
        for j in range(1, members):
            frm = (m + members - j) % members
            send(pre_buf.at[i, frm], pre_land.at[i, frm], pre_s.at[i, j], pre_r.at[i, frm], p.dev(frm)).wait_recv()
        pre_land[i, m] = pre_buf[i, m]
        for j in range(members):
            block = pre_land[i, j].reshape(own, pre_land.shape[4])
            for c in range(3):
                at = c * width + p.seq_of(i, j) * size
                mine_buf[:, at : at + size] = block[:, c * size : (c + 1) * size]
    grad_h1 = None
    for c in range(3):
        w = pool[c * per_w : (c + 1) * per_w].reshape(width, width)
        more = dot(mine_buf[:, c * width : (c + 1) * width], w, 1, 1)
        grad_h1 = more if grad_h1 is None else grad_h1 + more
    normed, scale = normalize(x_buf[...].reshape(own, width).astype(F32))
    sg = (gmid_buf[...] + norm_back(grad_h1, normed, scale, gain_ref[0:1])).astype(BF16)
    out_buf[1] = sg[rows:]
    swap_sg = swap(out_buf.at[1], out_land.at[1], 3)
    swap_sg.start()
    sg_ref[side] = sg[:rows]
    vecs = jnp.concatenate(
        [over_rows(grad_h1 * normed), gain_two, over_rows(grad_h1), shift_two, bias_out, bias_down, bias_out, bias_out],
        axis=0,
    )
    for s in range(shards):
        vec_buf[s, :, :size] = vecs[:, s * size : (s + 1) * size]
    per = shards // parts
    pairs = [(i, j) for i in range(parts) for j in range(shards) if i + j > 0]

    def vec_copy(i, j):
        to = (me + j) % shards
        slot = dp * shards + me
        return send(vec_buf.at[to], vec_land.at[slot], vec_s.at[i, j], vec_r.at[slot], ((dp + i) % parts, to))

    def vec_wait(i, j):
        frm = (me + j) % shards
        x = (dp + i) % parts
        slot = x * shards + frm
        send(vec_buf.at[0], vec_land.at[slot], vec_s.at[i, j], vec_r.at[slot], (x, frm)).wait_recv()

    for i, j in pairs:
        vec_copy(i, j).start()
    vec_land[dp * shards + me] = vec_buf[me]
    g_qkv.meet()

    cols = width // parts
    gdown_ref[...] = g_down.total()[:ff, :cols]
    gout_ref[...] = g_out.total()[:size, :cols]
    g_up.third()
    for v in range(per):
        acc = g_up.total(v)
        up_ref[:, v * ff : v * ff + main] = acc[:size, :main]
        if left:
            tail = jnp.transpose(acc[low:, :LANES])
            up_ref[:, v * ff + main : (v + 1) * ff] = tail[:size, :left]
    bias_land[side * parts + dp] = bias_buf[side]
    for s in range(2):
        for x in range(parts):
            slot = s * parts + x
            away = (side != s).astype(jnp.int32) + (dp != x).astype(jnp.int32)

            @pl.when(away > 0)
            def _():
                send(
                    bias_buf.at[0], bias_land.at[slot], bias_s.at[0, 0], bias_r.at[slot], (x, p.seq_of(s, m))
                ).wait_recv()

    acc = bias_land[0]
    for i in range(1, 2 * parts):
        acc = acc + bias_land[i]
    gab_ref[0:2] = acc[0:2, :size]
    for j in range(fp // LANES):
        n = min(LANES, ff - j * LANES)
        gub_ref[:, j * LANES : j * LANES + n] = acc[2 + j : 3 + j, :n]
    g_qkv.third()
    for v in range(per):
        acc = g_qkv.total(v)
        for c in range(3):
            qkv_ref[c, :, v * size : (v + 1) * size] = acc[:size, c * size : (c + 1) * size]
    swap_out.wait_recv()
    out_ref[1 - side] = out_land[0]
    swap_sg.wait_recv()
    sg_ref[1 - side] = out_land[1]
    for i, j in pairs:
        vec_wait(i, j)
    acc = vec_land[0]
    for i in range(1, shards * parts):
        acc = acc + vec_land[i]
    ggain_ref[...] = acc[0:2, :size]
    gshift_ref[...] = acc[2:4, :size]
    gab_ref[2:3] = acc[4:5, :size]
    gdb_ref[...] = acc[5:6, :size]

    for c in (swap_x, swap_ct, swap_out, swap_sg):
        c.wait_send()
    for j in range(1, members):
        att_copy((m + j) % members).wait_send()
        for i in range(2):
            pre_copy(i, j).wait_send()
    for x in range(parts):
        for i in range(2):
            if x > 0:
                bias_copy(x, i).wait_send()
            else:

                @pl.when(side != i)
                def _():
                    bias_copy(0, i).wait_send()

    for i, j in pairs:
        vec_copy(i, j).wait_send()
    for x in (gat1, gat2, sca2, g_up, g_qkv, g_down, g_out):
        x.finish()


def layer(shards, size, ff, parts, counts, states, cotangent, gains, nbias, abias, dbias, bu, w_out, w_up, w_down, w_qkv):
    rows, width = states.shape[1:]
    members = shards // 2
    n = members // 2
    sp, fp = up128(size), up128(ff)
    own = 2 * rows
    total = members * own
    per = shards // parts
    cols = width // parts
    r16 = lambda k: -(-k // 16) * 16
    sds = jax.ShapeDtypeStruct
    block = (members, 2, rows)
    wp = up128(3 * size)
    w4 = w_qkv.reshape(3 * width // own, 2, rows, width)
    return pl.pallas_call(
        functools.partial(layer_kernel, shards, size, ff, parts),
        out_shape=[
            sds((2, rows, width), BF16), sds((2, rows, width), BF16), sds((3, size, per * size), F32),
            sds((size, cols), F32), sds((3, size), F32), sds((2, size), F32), sds((2, size), F32),
            sds((size, per * ff), F32), sds((1, ff), F32), sds((ff, cols), F32), sds((1, size), F32),
        ],
        in_specs=[pl.BlockSpec(memory_space=pltpu.SMEM)]
        + [pl.BlockSpec(memory_space=VMEM)] * 7
        + [pl.BlockSpec(memory_space=pl.ANY)] * 4,
        out_specs=[pl.BlockSpec(memory_space=VMEM)] * 11,
        scratch_shapes=[
            VMEM(w4.shape, BF16), VMEM(block + (width,), BF16), VMEM(block + (width,), BF16), VMEM(block + (width,), BF16),
            VMEM((2, rows, width), BF16), VMEM((rows, width), BF16), VMEM((own, width), F32), VMEM((own, width), F32),
            VMEM(block + (6 * sp,), BF16), VMEM(block + (2 * sp,), F32), VMEM(block + (2 * sp,), BF16),
            VMEM(block + (2 * sp,), BF16), VMEM((2, total // QB, 8, QB), F32), VMEM((own, 3 * width), BF16),
            VMEM(block + (2 * fp,), BF16), VMEM(block + (2 * fp,), BF16), VMEM(block + (2 * sp,), BF16),
            VMEM((total, sp), F32), VMEM((total, sp), F32), VMEM((2,) + block + (wp,), BF16), VMEM((2,) + block + (wp,), BF16),
            VMEM((width, 6 * sp), BF16), VMEM(w_out.shape, BF16), VMEM((2 * sp, width), BF16), VMEM((2 * fp, width), BF16),
            VMEM((2 * fp, width), BF16),
            VMEM((2, max(6 * sp, 2 * fp)), F32),
            VMEM((shards, 8, LANES), F32), VMEM((shards * parts, 8, LANES), F32), VMEM((2, 8, LANES), F32),
            VMEM((2 * parts, 8, LANES), F32), VMEM((2, rows, width), BF16),
            VMEM((2, rows, width), BF16),
            DMA((4,)), DMA((4,)), DMA((members,)), DMA((members,)), DMA((2, members)), DMA((2, members)),
            DMA((parts, shards)), DMA((parts * shards,)), DMA((parts, 2)), DMA((2 * parts,)), DMA((6,)),
        ]
        + gather_sems(n) * 4
        + scatter_scratch(n, rows, width) * 2
        + rows_scratch(shards, parts, size, ff // LANES * LANES, ff % LANES)
        + rows_scratch(shards, parts, size, wp, 0)
        + cols_scratch(parts, r16(ff), up128(cols))
        + cols_scratch(parts, r16(size), up128(cols)),
        name="layer",
        compiler_params=pltpu.CompilerParams(
            collective_id=0, has_side_effects=True, vmem_limit_bytes=63 << 20
        ),
    )(counts, states, cotangent, gains, nbias, abias, dbias, bu, w_out, w_up, w_down, w4)


def deliver_kernel(*refs):
    count = len(refs) // 2
    for i in range(count):
        row = len(refs[count + i].shape) < len(refs[i].shape)
        refs[count + i][...] = refs[i][0] if row else refs[i][...]


def deliver(*arrays):
    return pl.pallas_call(
        deliver_kernel,
        out_shape=[jax.ShapeDtypeStruct(x.shape[1:] if x.shape[0] == 1 else x.shape, x.dtype) for x in arrays],
        in_specs=[pl.BlockSpec(memory_space=VMEM)] * len(arrays),
        out_specs=[pl.BlockSpec(memory_space=VMEM)] * len(arrays),
        name="deliver",
    )(*arrays)


def body(
    states, counts, cotangent, w_qkv, w_out, attn_bias, norm_gain, norm_bias,
    w_up, up_bias, w_down, down_bias,
):
    width = states.shape[2]
    shards = lax.axis_size("seq")
    parts = lax.axis_size("dp")
    size = width // HEADS
    ff = w_up.shape[1] // shards
    members = shards // 2
    me = lax.axis_index("seq")
    m = (me + (members // 2) * (me // members)) % members
    units = (m, members + (m + members // 2) % members)

    def mine(x, axis, count):
        return jnp.stack([lax.dynamic_slice_in_dim(x, u * count, count, axis) for u in units])

    layer_out, state_grad, g_qkv, g_out, g_ab, g_gain, g_shift, g_up, g_ub, g_down, g_db = deliver(
        *layer(
            shards, size, ff, parts, counts, states, cotangent, norm_gain, norm_bias, attn_bias, down_bias,
            mine(up_bias[None], 1, ff), w_out, w_up.T, w_down, w_qkv,
        )
    )
    return (
        layer_out, state_grad, g_qkv, g_out, g_ab, g_gain, g_shift, g_up,
        g_ub, g_down, g_db,
    )


def solution(mesh):
    placed = (P("dp", "seq", None), P("dp", None), P("dp", "seq", None)) + (P(),) * 9
    return jax.shard_map(
        body,
        mesh=mesh,
        in_specs=placed,
        out_specs=(
            P("dp", "seq", None), P("dp", "seq", None), P(None, "seq", "dp"), P("seq", "dp"),
            P(None, "seq"), P(None, "seq"), P(None, "seq"), P("seq", "dp"), P("seq"),
            P("seq", "dp"), P("seq"),
        ),
        check_vma=False,
    )
```

```python
import functools
import math

import jax
import jax.numpy as jnp
from jax import lax
from jax.experimental import pallas as pl
from jax.experimental.pallas import tpu as pltpu
from jax.sharding import PartitionSpec as P

HEADS = 16
EPS = 1e-06
NEG = -1e30
F32 = jnp.float32
BF16 = jnp.bfloat16
MESH = pl.DeviceIdType.MESH
VMEM = pltpu.VMEM
DMA = pltpu.SemaphoreType.DMA


def mm(spec, a, b):
    return jnp.einsum(spec, a, b, preferred_element_type=F32)


def dot(a, b, ca=1, cb=0):
    return lax.dot_general(a, b, (((ca,), (cb,)), ((), ())), preferred_element_type=F32)


def pad_to(x, axis, size):
    pads = [(0, 0)] * x.ndim
    pads[axis] = (0, size - x.shape[axis])
    return jnp.pad(x, pads)


def up128(n):
    return -(-n // 128) * 128


def normalize(values):
    mean = jnp.mean(values, axis=-1, keepdims=True)
    centred = values - mean
    scale = lax.rsqrt(jnp.mean(centred * centred, axis=-1, keepdims=True) + EPS)
    return (centred * scale, scale)


def norm_back(grad_norm, normed, scale, gain):
    scaled = grad_norm * gain
    return scale * (
        scaled
        - jnp.mean(scaled, axis=-1, keepdims=True)
        - normed * jnp.mean(scaled * normed, axis=-1, keepdims=True)
    )


def gelu_both(v):
    c, a = 0.7978845608028654, 0.044715
    sq = v * v
    t = jnp.tanh(c * (v + a * v * sq))
    half = 0.5 * (1.0 + t)
    return v * half, half + 0.5 * v * (1.0 - t * t) * (c * (1.0 + 3.0 * a * sq))


def send(src, dst, s, r, dev):
    return pltpu.make_async_remote_copy(
        src_ref=src, dst_ref=dst, send_sem=s, recv_sem=r, device_id=dev, device_id_type=MESH
    )


class Place:
    def __init__(self, shards, parts):
        self.shards, self.parts = shards, parts
        self.members = shards // 2
        self.n = self.members // 2
        self.half = self.n // 2
        self.me = lax.axis_index("seq")
        self.dp = lax.axis_index("dp")
        self.side = self.me // self.members
        self.m = (self.me + (self.members // 2) * self.side) % self.members
        self.chip = self.m // 2
        self.core = self.m % 2
        odd = self.chip % 2
        self.pos = (1 - odd) * (self.chip // 2) + odd * (self.n - 1 - self.chip // 2)
        self.to = (self.at(1, 1) * 2 + self.core, self.at(1, 0) * 2 + self.core)
        self.sib = self.chip * 2 + 1 - self.core
        self.partner = {"seq": self.seq_of(1 - self.side, self.m)}

    def seq_of(self, side, m):
        return side * self.members + (m + (self.members // 2) * side) % self.members

    def dev(self, m):
        return {"seq": self.seq_of(self.side, m)}

    def at(self, k, d):
        p = (self.pos + (self.n - k if d == 0 else k)) % self.n
        hi = p // self.half
        return (1 - hi) * 2 * p + hi * (2 * (self.n - 1 - p) + 1)

    def others(self):
        return [
            ((self.dp + i) % self.parts, (self.me + j) % self.shards)
            for i in range(self.parts) for j in range(self.shards) if i + j > 0
        ]


def gather_sems(n):
    return [DMA((2, n // 2 + 1, 2))] * 4


class Gather:
    def __init__(self, place, buf, base, sems):
        self.place, self.buf, self.base = place, buf, base
        self.ring_s, self.ring_r, self.sib_s, self.sib_r = sems
        self.sent = []

    def copy(self, k, d, g, to_sib):
        p = self.place
        block = self.buf.at[self.base + p.at(k, d) * 2 + p.core, g]
        s, r = (self.sib_s, self.sib_r) if to_sib else (self.ring_s, self.ring_r)
        return send(block, block, s.at[d, k, g], r.at[d, k, g], p.dev(p.sib if to_sib else p.to[d]))

    def go(self, *args):
        c = self.copy(*args)
        c.start()
        self.sent.append(c)

    def units(self, k):
        if k == self.place.half:
            return [(0, 0), (1, 1)]
        return [(0, 0), (1, 1), (0, 1), (1, 0)]

    def passes(self, k, d, g):
        return k < self.place.half - 1 or (k == self.place.half - 1 and g == d)

    def start(self, g):
        for d in (g, 1 - g):
            if self.passes(0, d, g):
                self.go(0, d, g, False)
        self.go(0, g, g, True)

    def start_both(self):
        for d, g in self.units(0):
            if self.passes(0, d, g):
                self.go(0, d, g, False)
        for g in range(2):
            self.go(0, g, g, True)

    def hop(self, k):
        for d, g in self.units(k):
            self.copy(k - 1, d, g, False).wait_recv()
            if self.passes(k, d, g):
                self.go(k, d, g, False)
            self.go(k, d, g, True)

    def ready(self, k):
        for d, g in self.units(k):
            if k > 0 or d == g:
                self.copy(k, d, g, True).wait_recv()

    def blocks(self, k):
        if k == 0 or k == self.place.half:
            return [self.place.at(k, 0)]
        return [self.place.at(k, 0), self.place.at(k, 1)]

    def finish(self):
        for c in self.sent:
            c.wait_send()


def scatter_scratch(n, rows, width):
    return [
        VMEM((n, 2, rows, width), BF16), VMEM((2, n // 2, 2, rows, width), BF16),
        DMA((n,)), DMA((n,)), DMA((2, n // 2, 2)), DMA((2, n // 2, 2)),
    ]


class Scatter:
    def __init__(self, place, part, base, scratch):
        self.place, self.part, self.base = place, part, base
        self.sib_land, self.land, self.sib_s, self.sib_r, self.ring_s, self.ring_r = scratch
        self.sent = []
        self.have = set()

    def slot(self, k, d):
        if k == 0:
            return 0
        return self.place.n - 1 if k == self.place.half else 2 * k - 1 + d

    def sib_copy(self, k, d):
        p, i = self.place, self.slot(k, d)
        src = self.part.at[self.base + p.at(k, d) * 2 + 1 - p.core]
        return send(src, self.sib_land.at[i], self.sib_s.at[i], self.sib_r.at[i], p.dev(p.sib))

    def give(self, k, d):
        c = self.sib_copy(k, d)
        c.start()
        self.sent.append(c)

    def from_sib(self, k, d):
        i = self.slot(k, d)
        if i not in self.have:
            self.have.add(i)
            self.sib_copy(k, d).wait_recv()
        return self.sib_land.at[i]

    def dist(self, h, d, g):
        return self.place.half - h if g == d else self.place.half - 1 - h

    def block(self, h, d, g):
        p = self.place
        return self.base + p.at(self.dist(h, d, g), 1 - d) * 2 + p.core

    def ring_copy(self, h, d, g):
        return send(
            self.part.at[self.block(h, d, g), g], self.land.at[d, h, g],
            self.ring_s.at[d, h, g], self.ring_r.at[d, h, g], self.place.dev(self.place.to[d]),
        )

    def hop(self, h):
        for d, g in [(0, 0), (1, 1), (0, 1), (1, 0)]:
            j = self.dist(h, d, g)
            if j == 0:
                continue
            own = self.block(h, d, g)
            val = self.part[own, g].astype(F32) + self.from_sib(j, 1 - d)[g].astype(F32)
            if h > 0:
                self.ring_copy(h - 1, d, g).wait_recv()
                val = val + self.land[d, h - 1, g].astype(F32)
            self.part[own, g] = val.astype(BF16)
            c = self.ring_copy(h, d, g)
            c.start()
            self.sent.append(c)

    def result(self):
        p = self.place
        out = []
        for g in range(2):
            val = self.part[self.base + p.m, g].astype(F32) + self.from_sib(0, 0)[g].astype(F32)
            for d in range(2):
                h = p.half - 1 if g == d else p.half - 2
                self.ring_copy(h, d, g).wait_recv()
                val = val + self.land[d, h, g].astype(F32)
            out.append(val)
        return jnp.concatenate(out, axis=0)

    def finish(self):
        for c in self.sent:
            c.wait_send()


def rows_scratch(shards, parts, size, width, left):
    gh, per = shards // parts, shards // parts
    r16 = lambda k: -(-k // 16) * 16
    packed = r16(gh * size) + r16(left) * -(-gh * size // width)
    rows = r16(size) + r16(left)
    return [
        VMEM((parts, 2, packed, width), BF16), VMEM((parts, 2, packed, width), BF16), VMEM((packed, width), BF16),
        VMEM((gh, rows, width), BF16), VMEM((per, rows, width), BF16),
        DMA((parts, 2)), DMA((parts, 2)), DMA((2,)), DMA((gh,)), DMA((per,)), DMA,
    ]


class Rows:
    def __init__(self, place, size, scratch):
        self.place, self.size = place, size
        self.buf, self.land, self.met, self.out, self.last = scratch[:5]
        self.s1, self.r1, self.sc, self.s2, self.r2, self.loc = scratch[5:]
        self.gh = self.out.shape[0]
        self.hp = place.parts // 2
        self.per = place.shards // place.parts
        self.below = (self.gh * size + 15) // 16 * 16
        self.low = (size + 15) // 16 * 16

    def fill(self, i, tall, turned=None):
        p, n, width = self.place, self.gh * self.size, self.buf.shape[3]
        for side in range(2):
            for q in range(self.hp):
                at = (side * p.members + q * self.gh) * self.size
                self.buf[i * self.hp + q, side, :n, : tall.shape[1]] = tall[at : at + n].astype(BF16)
                if turned is not None:
                    high = turned.shape[0]
                    for c in range(0, n, width):
                        to = self.below + c // width * high
                        cut = turned[:, at + c : at + min(c + width, n)].astype(BF16)
                        self.buf[i * self.hp + q, side, to : to + high, : cut.shape[1]] = cut

    def share(self, j, side):
        p = self.place
        x = (p.dp + j) % p.parts
        return send(
            self.buf.at[x, side], self.land.at[p.dp, side], self.s1.at[j, side], self.r1.at[p.dp, side], (x, p.me)
        )

    def first(self, side, unit=None):
        p = self.place
        for j in range(1, p.parts):
            if unit is None:
                self.share(j, side).start()
            else:

                @pl.when((p.dp + j) % p.parts // self.hp == unit)
                def _():
                    self.share(j, side).start()

    def shares(self, side):
        p = self.place
        for j in range(1, p.parts):
            x = (p.dp + j) % p.parts
            send(
                self.buf.at[x, side], self.land.at[x, side], self.s1.at[j, side], self.r1.at[x, side], (x, p.me)
            ).wait_recv()
        total = self.buf[p.dp, side].astype(F32)
        for j in range(1, p.parts):
            total = total + self.land[(p.dp + j) % p.parts, side].astype(F32)
        return total

    def cross(self):
        p = self.place
        return send(self.buf.at[p.dp, 1 - p.side], self.met, self.sc.at[0], self.sc.at[1], p.partner)

    def second(self):
        away = 1 - self.place.side
        self.buf[self.place.dp, away] = self.shares(away).astype(BF16)
        self.cross().start()

    def deliver(self, k, act, act_own):
        p = self.place
        unit = p.seq_of(p.dp // self.hp, p.m)
        keeper = unit // self.per
        owner = p.side * p.members + (p.dp % self.hp) * self.gh + k
        slot = unit % self.per
        away = (keeper != p.dp).astype(jnp.int32) + (owner != p.me).astype(jnp.int32)
        block = self.out.at[k]

        @pl.when(away > 0)
        def _():
            act(send(block, self.last.at[slot], self.s2.at[k], self.r2.at[slot], (keeper, owner)))

        if act_own:

            @pl.when(away == 0)
            def _():
                c = pltpu.make_async_copy(block, self.last.at[slot], self.loc)
                c.start()
                c.wait()

    def meet(self):
        total = self.shares(self.place.side)
        self.cross().wait_recv()
        total = total + self.met[...].astype(F32)
        size, high = self.size, self.out.shape[1] - self.low
        if high:
            parts = range(self.below, total.shape[0], high)
            turned = jnp.concatenate([total[at : at + high] for at in parts], axis=1)
        for k in range(self.gh):
            self.out[k, :size] = total[k * size : (k + 1) * size].astype(BF16)
            if high:
                self.out[k, self.low :, :size] = turned[:, k * size : (k + 1) * size].astype(BF16)
            self.deliver(k, lambda c: c.start(), True)

    def third(self):
        p = self.place
        for v in range(self.per):
            unit = p.dp * self.per + v
            i = unit // p.members
            m = (unit + (p.members // 2) * i) % p.members
            x = i * self.hp + p.me % p.members // self.gh
            away = (x != p.dp).astype(jnp.int32) + (m != p.m).astype(jnp.int32)

            @pl.when(away > 0)
            def _():
                frm = (x, p.seq_of(p.side, m))
                send(self.out.at[0], self.last.at[v], self.s2.at[0], self.r2.at[v], frm).wait_recv()

    def total(self, v):
        return self.last[v].astype(F32)

    def finish(self):
        for j in range(1, self.place.parts):
            for side in range(2):
                self.share(j, side).wait_send()
        self.cross().wait_send()
        for k in range(self.gh):
            self.deliver(k, lambda c: c.wait_send(), False)


def cols_scratch(parts, rows, width):
    return [
        VMEM((parts, 2, rows, width), BF16), VMEM((parts, 2, rows, width), BF16), VMEM((rows, width), BF16),
        DMA((parts, 2)), DMA((parts, 2)), DMA, DMA,
    ]


class Cols:
    def __init__(self, place, scratch):
        self.place = place
        self.buf, self.land, self.last, self.s1, self.r1, self.s2, self.r2 = scratch

    def put(self, i, val):
        p = self.place
        cols = val.shape[1] // p.parts
        val = val.astype(BF16)
        for x in range(p.parts):
            self.buf[x, i, : val.shape[0], :cols] = val[:, x * cols : (x + 1) * cols]

    def share(self, j, i):
        p = self.place
        x = (p.dp + j) % p.parts
        return send(self.buf.at[x, i], self.land.at[p.dp, i], self.s1.at[j, i], self.r1.at[p.dp, i], (x, p.me))

    def cross(self):
        p = self.place
        return send(self.buf.at[p.dp, 1 - p.side], self.last, self.s2, self.r2, p.partner)

    def first(self, i):
        for j in range(1, self.place.parts):
            self.share(j, i).start()

    def dp_sum(self, i):
        p = self.place
        val = self.buf[p.dp, i].astype(F32)
        for j in range(1, p.parts):
            x = (p.dp + j) % p.parts
            send(self.buf.at[x, i], self.land.at[x, i], self.s1.at[j, i], self.r1.at[x, i], (x, p.me)).wait_recv()
            val = val + self.land[x, i].astype(F32)
        return val

    def second(self):
        p = self.place
        self.buf[p.dp, 1 - p.side] = self.dp_sum(1 - p.side).astype(BF16)
        self.cross().start()

    def total(self):
        val = self.dp_sum(self.place.side)
        self.cross().wait_recv()
        return val + self.last[...].astype(F32)

    def finish(self):
        for j in range(1, self.place.parts):
            for i in range(2):
                self.share(j, i).wait_send()
        self.cross().wait_send()


def chip_rows(ref, chip, base=0):
    val = ref[pl.ds(base + 2 * chip, 2)]
    return val.reshape(-1, val.shape[-1])


def chip_put(ref, chip, val, base=0):
    ref[pl.ds(base + 2 * chip, 2)] = val.astype(ref.dtype).reshape((2,) + ref.shape[1:])


def ids_at(positions, ends):
    total = (positions >= ends[0]).astype(jnp.int32)
    for end in ends[1:]:
        total = total + (positions >= end).astype(jnp.int32)
    return total


def log2(n):
    assert n & (n - 1) == 0
    return n.bit_length() - 1


QB = 256
LANES = 128


def layer_kernel(
    shards, size, ff, parts,
    counts_ref, x_ref, ct_ref, gain_ref, nbias_ref, abias_ref, dbias_ref, bu_ref, wout_hbm, wu_hbm, wd_hbm, w_hbm,
    out_ref, sg_ref, qkv_ref, gout_ref, gab_ref, ggain_ref, gshift_ref, up_ref, gub_ref, gdown_ref, gdb_ref,
    pool, h_buf, m_buf, part2, x_buf, ct_buf, mid_buf, gmid_buf, qkv_buf, att_buf, att_b, att_land, lse_buf, mine_buf,
    act_buf, ghid_buf, gatt_buf, dk_acc, dv_acc, pre_buf, pre_land, wq_buf, wout_buf, wo_buf, wu_buf, wd_buf, row_buf,
    vec_buf, vec_land, bias_buf, bias_land, out_buf, out_land,
    ex_s, ex_r, att_s, att_r, pre_s, pre_r, vec_s, vec_r, bias_s, bias_r, loc, *rest,
):
    p = Place(shards, parts)
    me, dp, side, m = p.me, p.dp, p.side, p.m
    bar = pltpu.get_barrier_semaphore()
    for dev in p.others():
        pl.semaphore_signal(bar, inc=1, device_id=dev, device_id_type=MESH)
    rows, width = x_ref.shape[1:]
    members, half = p.members, p.half
    own = 2 * rows
    total = members * own
    sp = wo_buf.shape[0] // 2
    fp = wu_buf.shape[0] // 2
    units = [p.seq_of(i, m) for i in range(2)]

    span = (ff + 15) // 16 * 16 + 16
    windows = [u * ff // 16 * 16 - 16 * (u // (shards - 1)) for u in units]
    load_w0 = pltpu.make_async_copy(w_hbm, pool, loc.at[0])
    load_out = pltpu.make_async_copy(wout_hbm, wout_buf, loc.at[1])
    loads = [
        pltpu.make_async_copy(
            hbm.at[pl.ds(pl.multiple_of(windows[i], 16), span)], buf.at[pl.ds(i * fp, span)], loc.at[2 + 2 * i + j]
        )
        for j, (hbm, buf) in enumerate(((wu_hbm, wu_buf), (wd_hbm, wd_buf)))
        for i in range(2)
    ]
    load_w0.start()
    load_out.start()
    for c in loads:
        c.start()
    factor = 1.0 / math.sqrt(size)
    at_part, at_h2, at_gy = 0, members, 2 * members
    gat1 = Gather(p, h_buf, 0, rest[0:4])
    gaty = Gather(p, pool, at_gy, rest[4:8])
    gat = Gather(p, pool, at_h2, rest[8:12])
    gat2 = Gather(p, m_buf, 0, rest[12:16])
    sca = Scatter(p, pool, at_part, rest[16:22])
    sca2 = Scatter(p, part2, 0, rest[22:28])
    g_up = Rows(p, size, rest[28:39])
    g_qkv = Rows(p, size, rest[39:50])
    g_down = Cols(p, rest[50:57])
    g_out = Cols(p, rest[57:64])

    ends = [counts_ref[side, 0]]
    for i in range(1, counts_ref.shape[1]):
        ends.append(ends[-1] + counts_ref[side, i])

    def ids_of(t):
        mem = lax.shift_right_logical(t, log2(own))
        rho = lax.shift_right_logical(t, log2(rows)) & 1
        sig = rho + side - 2 * rho * side
        seq = sig * members + ((mem + (members // 2) * sig) & (members - 1))
        return ids_at(seq * rows + (t & (rows - 1)), ends)

    def iota(shape, dim):
        return lax.broadcasted_iota(jnp.int32, shape, dim)

    valid = (ids_of(iota((own, 1), 0) + m * own) < counts_ref.shape[1]).astype(F32)

    def swap(src, dst, i):
        return send(src, dst, ex_s.at[i], ex_r.at[i], p.partner)

    def norm_one(g):
        normed, _ = normalize(x_buf[g].astype(F32))
        h_buf[m, g] = (normed * gain_ref[0:1] + nbias_ref[0:1]).astype(BF16)

    x_buf[0] = x_ref[side]
    norm_one(0)
    pl.semaphore_wait(bar, len(p.others()))
    swap_x = swap(x_ref.at[1 - side], x_buf.at[1], 0)
    swap_ct = swap(ct_ref.at[1 - side], ct_buf, 1)
    swap_x.start()
    gat1.start(0)
    swap_ct.start()

    def iota2(shape):
        return iota(shape, 0), iota(shape, 1)

    def one_hot(hit, kind):
        return jnp.where(hit, 1.0, 0.0).astype(kind)

    at, lane = iota2((width, sp))
    pick = [jnp.logical_and(at == lane + u * size, lane < size) for u in units]
    exact = lax.dot_general(
        abias_ref[...], jnp.concatenate([one_hot(h, F32) for h in pick], axis=1), (((1,), (0,)), ((), ())),
        preferred_element_type=F32, precision=lax.Precision.HIGHEST,
    )
    row_buf[...] = jnp.zeros(row_buf.shape, F32)
    row_buf[0:1, : 2 * sp] = exact[0:1]
    row_buf[0:1, 4 * sp : 6 * sp] = exact[1:2]
    for i in range(2):
        row_buf[1:2, i * fp : i * fp + ff] = bu_ref[i]
    pick = jnp.concatenate([one_hot(h, BF16) for h in pick], axis=1)
    load_w0.wait()
    per_w = width // own
    for c in range(3):
        w = pool[c * per_w : (c + 1) * per_w].reshape(width, width)
        wq_buf[:, 2 * c * sp : 2 * (c + 1) * sp] = dot(w, pick).astype(BF16)
    swap_x.wait_recv()
    norm_one(1)
    gat1.start(1)
    pool[at_gy + m, 0] = (ct_ref[side].astype(F32) * valid[:rows]).astype(BF16)
    swap_ct.wait_recv()
    pool[at_gy + m, 1] = (ct_buf[...].astype(F32) * valid[rows:]).astype(BF16)

    def project(chip):
        out = dot(chip_rows(h_buf, chip), wq_buf[...]) + row_buf[0:1, : 6 * sp]
        out = jnp.concatenate([out[:, : 2 * sp] * factor, out[:, 2 * sp :]], axis=1)
        chip_put(qkv_buf, chip, out)

    for k in range(1, half + 1):
        gat1.hop(k)
        gat1.ready(k - 1)
        if k == half - 1:
            gaty.start_both()
        for chip in gat1.blocks(k - 1):
            project(chip)
    gat1.ready(half)
    project(p.at(half, 0))

    qn = QB // own

    def att_copy(to):
        return send(att_b.at[to], att_land.at[m], att_s.at[to], att_r.at[m], p.dev(to))

    def lanes_of(part, i):
        return slice((2 * part + i) * sp, (2 * part + i + 1) * sp)

    row_ids = ids_of(iota((1, total), 1))

    def attend(b):
        query_ids = ids_of(iota((QB, 1), 0) + b * QB)
        same = query_ids == row_ids
        for i in range(2):
            query = qkv_buf[pl.ds(b * qn, qn), :, :, lanes_of(0, i)].reshape(QB, sp)
            keys = qkv_buf[:, :, :, lanes_of(1, i)].reshape(total, sp)
            values = qkv_buf[:, :, :, lanes_of(2, i)].reshape(total, sp)
            scores = jnp.where(same, dot(query, keys, 1, 1), NEG)
            high = jnp.max(scores, axis=-1, keepdims=True)
            weights = jnp.exp(scores - high)
            sums = jnp.sum(weights, axis=-1, keepdims=True)
            out = (dot(weights.astype(BF16), values) / sums).reshape(qn, 2, rows, sp)
            att_buf[pl.ds(b * qn, qn), :, :, i * sp : (i + 1) * sp] = out
            att_b[pl.ds(b * qn, qn), :, :, i * sp : (i + 1) * sp] = out.astype(BF16)
            lse = jnp.broadcast_to(high + jnp.log(sums), (QB, LANES))
            lse_buf[i, b] = jnp.transpose(lse)[0:8]
        for t in range(qn):
            to = b * qn + t

            @pl.when(to != m)
            def _():
                att_copy(to).start()

    blocks = total // QB
    pl.loop(0, blocks // 2)(attend)
    gaty.hop(1)
    pl.loop(blocks // 2, blocks)(attend)
    for k in range(2, half + 1):
        gaty.hop(k)
    att_land[m] = att_b[m]
    for c in loads:
        c.wait()
    at, lane = iota2((fp, span))
    for i in range(2):
        hit = jnp.logical_and(lane == at + (units[i] * ff - windows[i]), at < ff)
        for buf in (wu_buf, wd_buf):
            cut = dot(one_hot(hit, BF16), buf[i * fp : i * fp + span])
            buf[i * fp : (i + 1) * fp] = cut.astype(BF16)
    load_out.wait()
    for j in range(1, members):
        frm = (m + members - j) % members
        send(att_b.at[frm], att_land.at[frm], att_s.at[frm], att_r.at[frm], p.dev(frm)).wait_recv()
    for j in range(members):
        for i in range(2):
            at = p.seq_of(i, j) * size
            mine_buf[:, at : at + size] = att_land[j].reshape(own, 2 * sp)[:, i * sp : i * sp + size]
    inputs = x_buf[...].reshape(own, width).astype(F32)
    mid = inputs + dot(mine_buf[:, :width], wout_buf[...]) + abias_ref[2:3]
    mid_buf[...] = mid
    normed, _ = normalize(mid)
    pool[at_h2 + m] = (normed * gain_ref[1:2] + nbias_ref[1:2]).astype(BF16).reshape(2, rows, width)
    gat.start_both()
    at, lane = iota2((sp, width))
    for i in range(2):
        hit = jnp.logical_and(lane == at + units[i] * size, at < size)
        wo_buf[i * sp : (i + 1) * sp] = dot(one_hot(hit, BF16), wout_buf[...]).astype(BF16)

    def forward(chip):
        hidden = dot(chip_rows(pool, chip, at_h2), wu_buf[...], 1, 1) + row_buf[1:2, : 2 * fp]
        act, slope = gelu_both(hidden)
        chip_put(act_buf, chip, act)
        ghid = (dot(chip_rows(pool, chip, at_gy), wd_buf[...], 1, 1) * slope).astype(BF16)
        chip_put(ghid_buf, chip, ghid)
        chip_put(pool, chip, dot(ghid, wu_buf[...]), at_part)

    for k in range(half + 1):
        if k < half:
            gat.hop(k + 1)
        gaty.ready(k)
        gat.ready(k)
        for d, chip in enumerate(gat.blocks(k)):
            forward(chip)
            sca.give(k, d)

    def flat(val):
        return val.reshape(total, val.shape[-1])

    for h in range(half):
        sca.hop(h)
        if h == 0:
            gdown = dot(flat(act_buf[...]), flat(pool[at_gy : at_gy + members]), 0, 0)
            for i in range(2):
                g_down.put(i, gdown[i * fp : i * fp + (ff + 15) // 16 * 16])
            g_down.first(1 - side)
    gup = dot(flat(ghid_buf[...]), flat(pool[at_h2 : at_h2 + members]), 0, 0)
    main, left = ff // LANES * LANES, ff % LANES
    low = (size + 15) // 16 * 16
    for i in range(2):
        turned = gup[i * fp + main : i * fp + main + (left + 15) // 16 * 16] if left else None
        g_up.fill(i, jnp.transpose(gup[i * fp : i * fp + main]), turned)
    g_up.first(1 - side)
    g_down.first(side)
    grad_h2 = sca.result()
    normed, scale = normalize(mid_buf[...])
    gy_own = pool[at_gy + m].reshape(own, width).astype(F32)
    gmid = gy_own + norm_back(grad_h2, normed, scale, gain_ref[1:2])
    gmid_buf[...] = gmid
    m_buf[m] = gmid.astype(BF16).reshape(2, rows, width)
    gat2.start_both()
    g_up.first(side)

    def over_rows(val):
        return jnp.sum(val, axis=0, keepdims=True)

    gain_two, shift_two, bias_out, bias_down = (
        over_rows(grad_h2 * normed), over_rows(grad_h2), over_rows(gmid), over_rows(gy_own)
    )
    bias_up = over_rows(flat(ghid_buf[...]).astype(F32))

    def down_part(chip):
        chip_put(part2, chip, dot(chip_rows(act_buf, chip), wd_buf[...]))

    def back(chip):
        block = chip_rows(m_buf, chip)
        chip_put(gatt_buf, chip, dot(block, wo_buf[...], 1, 1))
        return dot(chip_rows(att_b, chip), block, 0, 0)

    gout = None
    for k in range(half + 1):
        for d, chip in enumerate(gat.blocks(k)):
            down_part(chip)
            sca2.give(k, d)
        if k < half:
            gat2.hop(k + 1)
        if k == half - 1:
            g_down.second()
        gat2.ready(k)
        for chip in gat2.blocks(k):
            more = back(chip)
            gout = more if gout is None else gout + more
    for i in range(2):
        g_out.put(i, gout[i * sp : i * sp + low])
    for i in (1 - side, side):
        g_out.first(i)
    for x in (gat, gaty, sca):
        x.finish()
    load_w = pltpu.make_async_copy(w_hbm, pool, loc.at[0])
    load_w.start()
    sca2.hop(0)

    col_ids = ids_of(iota((total, 1), 0))

    def pre_copy(i, j):
        to = (m + j) % members
        return send(pre_buf.at[i, to], pre_land.at[i, m], pre_s.at[i, j], pre_r.at[i, m], p.dev(to))

    pre_buf[:, :, :, :, 3 * size :] = jnp.zeros(pre_buf.shape[:4] + (pre_buf.shape[4] - 3 * size,), BF16)
    bias_buf[...] = jnp.zeros(bias_buf.shape, F32)
    for i in range(2):
        for j in range(fp // LANES):
            bias_buf[i, 2 + j : 3 + j] = bias_up[:, i * fp + j * LANES : i * fp + (j + 1) * LANES]

    def lanes_at(k):
        return pl.ds(pl.multiple_of(k * sp, LANES), sp)

    mine_last = dp // g_qkv.hp
    for step in range(2):
        i = mine_last if step == 1 else 1 - mine_last
        dk_acc[...] = jnp.zeros(dk_acc.shape, F32)
        dv_acc[...] = jnp.zeros(dv_acc.shape, F32)

        def attend_back(b):
            blk = pl.ds(b * qn, qn)
            query = qkv_buf[blk, :, :, lanes_at(i)].reshape(QB, sp)
            keys = qkv_buf[:, :, :, lanes_at(2 + i)].reshape(total, sp)
            values = qkv_buf[:, :, :, lanes_at(4 + i)].reshape(total, sp)
            grad = gatt_buf[blk, :, :, lanes_at(i)].reshape(QB, sp)
            att = att_buf[blk, :, :, lanes_at(i)].reshape(QB, sp)
            delta = jnp.sum(grad.astype(F32) * att, axis=-1, keepdims=True)
            delta = jnp.transpose(jnp.broadcast_to(delta, (QB, LANES)))[0:1]
            same = col_ids == ids_of(iota((1, QB), 1) + b * QB)
            probs = jnp.exp(jnp.where(same, dot(keys, query, 1, 1), NEG) - lse_buf[i, b][0:1])
            grad_scores = (probs * (dot(values, grad, 1, 1) - delta)).astype(BF16)
            dv_acc[...] += dot(probs.astype(BF16), grad)
            dk_acc[...] += dot(grad_scores, query)
            dq = (dot(grad_scores, keys, 0, 0) * factor).astype(BF16)
            pre_buf[i, blk, :, :, :size] = dq[:, :size].reshape(qn, 2, rows, size)
            bias_buf[i, 0:1] += over_rows(dq.astype(F32))

        for b in range(blocks):
            attend_back(b)
            if step == 0 and b == 0:
                g_up.second()
        dk = dk_acc[...].astype(BF16)
        dv = dv_acc[...].astype(BF16)
        bias_buf[i, 1:2] = over_rows(dv.astype(F32))
        pre_buf[i, :, :, :, size : 2 * size] = dk[:, :size].reshape(members, 2, rows, size)
        pre_buf[i, :, :, :, 2 * size : 3 * size] = dv[:, :size].reshape(members, 2, rows, size)
        for j in range(1, members):
            pre_copy(i, j).start()
        grad = dot(pre_buf[i].reshape(total, pre_buf.shape[4]), flat(h_buf[...]), 0, 0)
        g_qkv.fill(i, jnp.transpose(grad))
        for owners in (1 - side, side):
            g_qkv.first(owners, i)
        if step == 0:
            for h in range(1, half):
                sca2.hop(h)
    def bias_copy(x, i):
        to = ((dp + x) % parts, p.seq_of(i, m))
        return send(
            bias_buf.at[i], bias_land.at[side * parts + dp], bias_s.at[x, i], bias_r.at[side * parts + dp], to
        )

    for x in range(parts):
        for i in range(2):
            if x > 0:
                bias_copy(x, i).start()
            else:

                @pl.when(side != i)
                def _():
                    bias_copy(0, i).start()

    down = sca2.result()
    out = ((mid_buf[...] + down + dbias_ref[...].reshape(1, width)) * valid).astype(BF16)
    out_ref[side] = out[:rows]
    out_buf[0] = out[rows:]
    g_qkv.second()
    g_out.second()
    swap_out = swap(out_buf.at[0], out_land.at[0], 2)
    load_w.wait()
    for i in range(2):
        for j in range(1, members):
            frm = (m + members - j) % members
            send(pre_buf.at[i, frm], pre_land.at[i, frm], pre_s.at[i, j], pre_r.at[i, frm], p.dev(frm)).wait_recv()
        pre_land[i, m] = pre_buf[i, m]
        for j in range(members):
            block = pre_land[i, j].reshape(own, pre_land.shape[4])
            for c in range(3):
                at = c * width + p.seq_of(i, j) * size
                mine_buf[:, at : at + size] = block[:, c * size : (c + 1) * size]
    grad_h1 = None
    for c in range(3):
        w = pool[c * per_w : (c + 1) * per_w].reshape(width, width)
        more = dot(mine_buf[:, c * width : (c + 1) * width], w, 1, 1)
        grad_h1 = more if grad_h1 is None else grad_h1 + more
    normed, scale = normalize(x_buf[...].reshape(own, width).astype(F32))
    sg = (gmid_buf[...] + norm_back(grad_h1, normed, scale, gain_ref[0:1])).astype(BF16)
    out_buf[1] = sg[rows:]
    swap_sg = swap(out_buf.at[1], out_land.at[1], 3)
    swap_sg.start()
    swap_out.start()
    sg_ref[side] = sg[:rows]
    vecs = jnp.concatenate(
        [over_rows(grad_h1 * normed), gain_two, over_rows(grad_h1), shift_two, bias_out, bias_down, bias_out, bias_out],
        axis=0,
    )
    for s in range(shards):
        vec_buf[s, :, :size] = vecs[:, s * size : (s + 1) * size]
    per = shards // parts
    pairs = [(i, j) for i in range(parts) for j in range(shards) if i + j > 0]

    def vec_copy(i, j):
        to = (me + j) % shards
        slot = dp * shards + me
        return send(vec_buf.at[to], vec_land.at[slot], vec_s.at[i, j], vec_r.at[slot], ((dp + i) % parts, to))

    def vec_wait(i, j):
        frm = (me + j) % shards
        x = (dp + i) % parts
        slot = x * shards + frm
        send(vec_buf.at[0], vec_land.at[slot], vec_s.at[i, j], vec_r.at[slot], (x, frm)).wait_recv()

    for i, j in pairs:
        vec_copy(i, j).start()
    vec_land[dp * shards + me] = vec_buf[me]
    g_up.meet()
    g_qkv.meet()

    cols = width // parts
    gdown_ref[...] = g_down.total()[:ff, :cols]
    gout_ref[...] = g_out.total()[:size, :cols]
    g_up.third()
    for v in range(per):
        acc = g_up.total(v)
        up_ref[:, v * ff : v * ff + main] = acc[:size, :main]
        if left:
            tail = jnp.transpose(acc[low:, :LANES])
            up_ref[:, v * ff + main : (v + 1) * ff] = tail[:size, :left]
    bias_land[side * parts + dp] = bias_buf[side]
    for s in range(2):
        for x in range(parts):
            slot = s * parts + x
            away = (side != s).astype(jnp.int32) + (dp != x).astype(jnp.int32)

            @pl.when(away > 0)
            def _():
                send(
                    bias_buf.at[0], bias_land.at[slot], bias_s.at[0, 0], bias_r.at[slot], (x, p.seq_of(s, m))
                ).wait_recv()

    acc = bias_land[0]
    for i in range(1, 2 * parts):
        acc = acc + bias_land[i]
    gab_ref[0:2] = acc[0:2, :size]
    for j in range(fp // LANES):
        n = min(LANES, ff - j * LANES)
        gub_ref[:, j * LANES : j * LANES + n] = acc[2 + j : 3 + j, :n]
    g_qkv.third()
    for v in range(per):
        acc = g_qkv.total(v)
        for c in range(3):
            qkv_ref[c, :, v * size : (v + 1) * size] = acc[:size, c * size : (c + 1) * size]
    swap_out.wait_recv()
    out_ref[1 - side] = out_land[0]
    swap_sg.wait_recv()
    sg_ref[1 - side] = out_land[1]
    for i, j in pairs:
        vec_wait(i, j)
    acc = vec_land[0]
    for i in range(1, shards * parts):
        acc = acc + vec_land[i]
    ggain_ref[...] = acc[0:2, :size]
    gshift_ref[...] = acc[2:4, :size]
    gab_ref[2:3] = acc[4:5, :size]
    gdb_ref[...] = acc[5:6, :size]

    for c in (swap_x, swap_ct, swap_out, swap_sg):
        c.wait_send()
    for j in range(1, members):
        att_copy((m + j) % members).wait_send()
        for i in range(2):
            pre_copy(i, j).wait_send()
    for x in range(parts):
        for i in range(2):
            if x > 0:
                bias_copy(x, i).wait_send()
            else:

                @pl.when(side != i)
                def _():
                    bias_copy(0, i).wait_send()

    for i, j in pairs:
        vec_copy(i, j).wait_send()
    for x in (gat1, gat2, sca2, g_up, g_qkv, g_down, g_out):
        x.finish()


def layer(shards, size, ff, parts, counts, states, cotangent, gains, nbias, abias, dbias, bu, w_out, w_up, w_down, w_qkv):
    rows, width = states.shape[1:]
    members = shards // 2
    n = members // 2
    sp, fp = up128(size), up128(ff)
    own = 2 * rows
    total = members * own
    per = shards // parts
    cols = width // parts
    r16 = lambda k: -(-k // 16) * 16
    sds = jax.ShapeDtypeStruct
    block = (members, 2, rows)
    wp = up128(3 * size)
    w4 = w_qkv.reshape(3 * width // own, 2, rows, width)
    return pl.pallas_call(
        functools.partial(layer_kernel, shards, size, ff, parts),
        out_shape=[
            sds((2, rows, width), BF16), sds((2, rows, width), BF16), sds((3, size, per * size), F32),
            sds((size, cols), F32), sds((3, size), F32), sds((2, size), F32), sds((2, size), F32),
            sds((size, per * ff), F32), sds((1, ff), F32), sds((ff, cols), F32), sds((1, size), F32),
        ],
        in_specs=[pl.BlockSpec(memory_space=pltpu.SMEM)]
        + [pl.BlockSpec(memory_space=VMEM)] * 7
        + [pl.BlockSpec(memory_space=pl.ANY)] * 4,
        out_specs=[pl.BlockSpec(memory_space=VMEM)] * 11,
        scratch_shapes=[
            VMEM(w4.shape, BF16), VMEM(block + (width,), BF16), VMEM(block + (width,), BF16), VMEM(block + (width,), BF16),
            VMEM((2, rows, width), BF16), VMEM((rows, width), BF16), VMEM((own, width), F32), VMEM((own, width), F32),
            VMEM(block + (6 * sp,), BF16), VMEM(block + (2 * sp,), F32), VMEM(block + (2 * sp,), BF16),
            VMEM(block + (2 * sp,), BF16), VMEM((2, total // QB, 8, QB), F32), VMEM((own, 3 * width), BF16),
            VMEM(block + (2 * fp,), BF16), VMEM(block + (2 * fp,), BF16), VMEM(block + (2 * sp,), BF16),
            VMEM((total, sp), F32), VMEM((total, sp), F32), VMEM((2,) + block + (wp,), BF16), VMEM((2,) + block + (wp,), BF16),
            VMEM((width, 6 * sp), BF16), VMEM(w_out.shape, BF16), VMEM((2 * sp, width), BF16), VMEM((2 * fp, width), BF16),
            VMEM((2 * fp, width), BF16),
            VMEM((2, max(6 * sp, 2 * fp)), F32),
            VMEM((shards, 8, LANES), F32), VMEM((shards * parts, 8, LANES), F32), VMEM((2, 8, LANES), F32),
            VMEM((2 * parts, 8, LANES), F32), VMEM((2, rows, width), BF16),
            VMEM((2, rows, width), BF16),
            DMA((4,)), DMA((4,)), DMA((members,)), DMA((members,)), DMA((2, members)), DMA((2, members)),
            DMA((parts, shards)), DMA((parts * shards,)), DMA((parts, 2)), DMA((2 * parts,)), DMA((6,)),
        ]
        + gather_sems(n) * 4
        + scatter_scratch(n, rows, width) * 2
        + rows_scratch(shards, parts, size, ff // LANES * LANES, ff % LANES)
        + rows_scratch(shards, parts, size, wp, 0)
        + cols_scratch(parts, r16(ff), up128(cols))
        + cols_scratch(parts, r16(size), up128(cols)),
        name="layer",
        compiler_params=pltpu.CompilerParams(
            collective_id=0, has_side_effects=True, vmem_limit_bytes=63 << 20
        ),
    )(counts, states, cotangent, gains, nbias, abias, dbias, bu, w_out, w_up, w_down, w4)


def deliver_kernel(*refs):
    count = len(refs) // 2
    for i in range(count):
        row = len(refs[count + i].shape) < len(refs[i].shape)
        refs[count + i][...] = refs[i][0] if row else refs[i][...]


def deliver(*arrays):
    return pl.pallas_call(
        deliver_kernel,
        out_shape=[jax.ShapeDtypeStruct(x.shape[1:] if x.shape[0] == 1 else x.shape, x.dtype) for x in arrays],
        in_specs=[pl.BlockSpec(memory_space=VMEM)] * len(arrays),
        out_specs=[pl.BlockSpec(memory_space=VMEM)] * len(arrays),
        name="deliver",
    )(*arrays)


def body(
    states, counts, cotangent, w_qkv, w_out, attn_bias, norm_gain, norm_bias,
    w_up, up_bias, w_down, down_bias,
):
    width = states.shape[2]
    shards = lax.axis_size("seq")
    parts = lax.axis_size("dp")
    size = width // HEADS
    ff = w_up.shape[1] // shards
    members = shards // 2
    me = lax.axis_index("seq")
    m = (me + (members // 2) * (me // members)) % members
    units = (m, members + (m + members // 2) % members)

    def mine(x, axis, count):
        return jnp.stack([lax.dynamic_slice_in_dim(x, u * count, count, axis) for u in units])

    layer_out, state_grad, g_qkv, g_out, g_ab, g_gain, g_shift, g_up, g_ub, g_down, g_db = deliver(
        *layer(
            shards, size, ff, parts, counts, states, cotangent, norm_gain, norm_bias, attn_bias, down_bias,
            mine(up_bias[None], 1, ff), w_out, w_up.T, w_down, w_qkv,
        )
    )
    return (
        layer_out, state_grad, g_qkv, g_out, g_ab, g_gain, g_shift, g_up,
        g_ub, g_down, g_db,
    )


def solution(mesh):
    placed = (P("dp", "seq", None), P("dp", None), P("dp", "seq", None)) + (P(),) * 9
    return jax.shard_map(
        body,
        mesh=mesh,
        in_specs=placed,
        out_specs=(
            P("dp", "seq", None), P("dp", "seq", None), P(None, "seq", "dp"), P("seq", "dp"),
            P(None, "seq"), P(None, "seq"), P(None, "seq"), P("seq", "dp"), P("seq"),
            P("seq", "dp"), P("seq"),
        ),
        check_vma=False,
    )
```
